512 devices in a mesh: gx: 32 (over z, x), gy: 16 (over y, core).
Axes of the slice: x: 4, y: 8, z: 8, core: 2. Of those that a mesh axis runs over, the one named last changes fastest.
Arguments:
- nest_state: float32 [4, 48, 192, 6144], P(None, None, 'gx', 'gy'), may hold values from -6 to 6
- stiffness: float32 [48, 192, 6144], P(None, 'gx', 'gy'), may hold values from 0.5 to 2
- parent: float32 [4, 48, 64, 2048], P(None, None, 'gx', 'gy'), may hold values from -6 to 6
- inverse_table: float32 [48, 48], replicated, may hold values from -0.12 to 0.52, as said below
- offsets: int32 [2], replicated, may hold values from -1 to 1
Outputs:
- new_state: float32 [4, 48, 192, 6144], P(None, None, 'gx', 'gy')
- parent_new: float32 [4, 48, 64, 2048], P(None, None, 'gx', 'gy')
The draws below stay inside these ranges and needn't reach their ends.
Inputs may be any that keep to these rules, and one draw needn't show every extreme that they name: `inverse_table`: close to 0.4 times the identity.
All inputs are finite; a program needn't handle non-finite values.
Results may differ from the reference program's by a relative error of at most 0.0001.
Values sent between devices are 32-bit elements; how exact they have to be, the bound alone decides.
No kernel may reach another device: no remote copies, remote signals or barrier semaphores. Data moves between devices by JAX's collectives and lax.ppermute only.
A program may use at most 128 MiB of HBM per device.

```python
import math
import jax
import jax.numpy as jnp
from jax import lax

LEVELS = 48
RATIO = 3
SUBSTEPS = 2
NX = 192
NY = 6144
NXP = 64
NYP = 2048


def draw_inverse_table(key, part):
    key = jax.random.fold_in(key, 7)
    identity = jnp.eye(LEVELS, dtype=jnp.float32)
    noise = jnp.clip(jax.random.normal(key, (LEVELS, LEVELS), jnp.float32), -4.0, 4.0)
    return 0.4 * (identity + 0.3 * noise / math.sqrt(LEVELS))


def level_of(key, shape, shards, smallest, top_value):
    gain, own = 1.0, jax.random.fold_in(key, 6)
    for axis_at, parts in shards:
        heights = jnp.exp(jax.random.uniform(jax.random.fold_in(own, axis_at), (parts,), jnp.float32, smallest / len(shards), top_value / len(shards)))
        gain = gain * jnp.repeat(heights, shape[axis_at] // parts).reshape([-1 if axis == axis_at else 1 for axis in range(len(shape))])
    return gain


def bell_draw(rng, extent, deviation, reach, split=(), held_as=jnp.bfloat16):
    entries = deviation * jax.random.normal(rng, extent, jnp.float32)
    if split:
        entries = entries * level_of(rng, extent, split, -0.22, 0.18)
    return jnp.clip(entries, -reach, reach).astype(held_as)


def setup_inputs(seed: int = 0) -> dict:
    keys = jax.random.split(jax.random.key(seed), 6)
    nest_state = bell_draw(keys[0], (4, LEVELS, NX, NY), 1.0, 6.0, ((2, 32), (3, 16)), jnp.float32)
    stiffness = jnp.clip(jnp.exp(math.log(2.0) - 1.3862944 * jax.random.uniform(keys[1], (LEVELS, NX, NY), jnp.float32) ** level_of(keys[1], (LEVELS, NX, NY), ((1, 32), (2, 16)), -0.2, 0.2)), 0.5, 2.0)
    parent = bell_draw(keys[2], (4, LEVELS, NXP, NYP), 1.0, 6.0, ((2, 32), (3, 16)), jnp.float32)
    inverse_table = draw_inverse_table(jax.random.fold_in(keys[5], 71), 0)
    offsets = jax.random.randint(keys[4], (2,), -1, 2).astype(jnp.int32)
    return {"nest_state": nest_state, "stiffness": stiffness, "parent": parent, "inverse_table": inverse_table, "offsets": offsets}


GRAD_COEF = 0.25
DIV_COEF = 0.25
COUPLE_COEF = 0.25
LIFT_COEF = 0.5


def level_up(field):
    return jnp.concatenate([field[1:], jnp.zeros_like(field[:1])], 0)


def level_down(field):
    return jnp.concatenate([jnp.zeros_like(field[:1]), field[:-1]], 0)


def vertical_solve(inverse, right_side, stiffness):
    flattened = right_side.reshape(right_side.shape[0], -1)
    first_sweep = jnp.dot(inverse, flattened, precision=lax.Precision.HIGHEST).reshape(right_side.shape)
    applied = (1.0 + stiffness) * first_sweep - 0.25 * (level_up(first_sweep) + level_down(first_sweep))
    leftover = (right_side - applied).reshape(flattened.shape)
    second_sweep = jnp.dot(inverse, leftover, precision=lax.Precision.HIGHEST).reshape(right_side.shape)
    return first_sweep + second_sweep


def smooth_pair(field):
    along_x = 0.25 * field[..., :-2, :] + 0.5 * field[..., 1:-1, :] + 0.25 * field[..., 2:, :]
    return 0.25 * along_x[..., :-2] + 0.5 * along_x[..., 1:-1] + 0.25 * along_x[..., 2:]


def substep_full(current, edge_zone, stiffness, inverse):
    u_wind, v_wind, w_wind, pressure = current[0], current[1], current[2], current[3]
    pres_pad = jnp.pad(pressure, ((0, 0), (1, 1), (1, 1)))
    u_next = jnp.where(edge_zone, u_wind, u_wind - GRAD_COEF * (pres_pad[:, 2:, 1:-1] - pres_pad[:, :-2, 1:-1]))
    v_next = jnp.where(edge_zone, v_wind, v_wind - GRAD_COEF * (pres_pad[:, 1:-1, 2:] - pres_pad[:, 1:-1, :-2]))
    u_pad = jnp.pad(u_next, ((0, 0), (1, 1), (0, 0)))
    v_pad = jnp.pad(v_next, ((0, 0), (0, 0), (1, 1)))
    divergence = (u_pad[:, 2:] - u_pad[:, :-2]) + (v_pad[:, :, 2:] - v_pad[:, :, :-2])
    right_side = pressure - DIV_COEF * divergence - COUPLE_COEF * (level_up(w_wind) - level_down(w_wind))
    solved = vertical_solve(inverse, right_side, stiffness)
    p_next = jnp.where(edge_zone, pressure, solved)
    w_next = jnp.where(edge_zone, w_wind, w_wind - LIFT_COEF * (level_up(p_next) - p_next))
    return jnp.stack([u_next, v_next, w_next, p_next])


def reference(nest_state, stiffness, parent, inverse_table, offsets):
    nest_x, nest_y = nest_state.shape[2], nest_state.shape[3]
    levels = nest_state.shape[1]
    move_x = RATIO * offsets[0]
    move_y = RATIO * offsets[1]
    row_index = jnp.arange(nest_x).astype(jnp.int32)
    col_index = jnp.arange(nest_y).astype(jnp.int32)
    edge_zone = ((row_index < RATIO) | (row_index >= nest_x - RATIO))[:, None] | ((col_index < RATIO) | (col_index >= nest_y - RATIO))[None, :]
    parent_x, parent_y = nest_x // RATIO, nest_y // RATIO
    source_x = jnp.clip(row_index // RATIO + offsets[0], 0, parent_x - 1).astype(jnp.int32)
    source_y = jnp.clip(col_index // RATIO + offsets[1], 0, parent_y - 1).astype(jnp.int32)
    boundary = jnp.take(jnp.take(parent, source_x, axis=2), source_y, axis=3)
    moved = jnp.roll(nest_state, (-move_x, -move_y), axis=(2, 3))
    current = jnp.where(edge_zone, boundary, moved)
    for substep in range(SUBSTEPS):
        current = substep_full(current, edge_zone, stiffness, inverse_table)
    blocks = current.reshape(4, levels, parent_x, RATIO, parent_y, RATIO).mean(axis=(3, 5))
    block_x = jnp.arange(parent_x).astype(jnp.int32)
    block_y = jnp.arange(parent_y).astype(jnp.int32)
    interior = (((block_x >= 1) & (block_x <= parent_x - 2))[:, None] & ((block_y >= 1) & (block_y <= parent_y - 2))[None, :]).astype(jnp.float32)
    weighted = blocks * interior
    weight_pad = jnp.pad(weighted, ((0, 0), (0, 0), (2, 2), (2, 2)))
    inner_pad = jnp.pad(interior, ((2, 2), (2, 2)))
    zero_start = jnp.zeros((), jnp.int32)
    start_x = (1 - offsets[0]).astype(jnp.int32)
    start_y = (1 - offsets[1]).astype(jnp.int32)
    weight_win = lax.dynamic_slice(weight_pad, (zero_start, zero_start, start_x, start_y), (4, levels, parent_x + 2, parent_y + 2))
    inner_win = lax.dynamic_slice(inner_pad, (start_x, start_y), (parent_x + 2, parent_y + 2))
    numerator = smooth_pair(weight_win)
    denominator = smooth_pair(inner_win)
    centre = inner_win[1:-1, 1:-1] > 0
    parent_new = jnp.where(centre, numerator / jnp.where(centre, denominator, 1.0), parent)
    return current, parent_new
```

```python
import functools

import jax
import jax.numpy as jnp
from jax import lax
from jax.experimental import pallas as pl
from jax.experimental.pallas import tpu as pltpu
from jax.sharding import PartitionSpec as P

RATIO = 3
GRAD = 0.25
DIV = 0.25
COUPLE = 0.25
LIFT = 0.5
F32 = jnp.float32
BF16 = jnp.bfloat16
VMEM_BYTES = 60 * 1024 * 1024

ROWS = 6
COLS = 384
LANES = 128
WIDE = COLS + LANES
SIDE = 8
PER_TILE = LANES // SIDE
P_DEEP, U_DEEP, V_DEEP, W_DEEP = 5, 4, 3, 3
KEEP = 3
WIN = ROWS + 2 * KEEP
P_AT = 0
U_AT = P_AT + P_DEEP
V_AT = U_AT + U_DEEP
W_AT = V_AT + V_DEEP
S_AT = W_AT + W_DEEP
PACK_AT = S_AT + ROWS
MESSAGE = PACK_AT + 2
S_GROUP = 4 * ROWS
EDGE_GROUP = S_GROUP + ROWS
GROUPS = EDGE_GROUP + 4
PACK = -(-GROUPS // PER_TILE) * LANES
U, V, W, PR = 0, 1, 2, 3


def lanes_of(shape):
    return lax.broadcasted_iota(jnp.int32, shape, len(shape) - 1)


def column_of_lane(shape):
    lane = lanes_of(shape)
    return jnp.where(lane < COLS + LANES // 2, lane, lane - WIDE)


def is_edge(index, count):
    return (index < RATIO) | (index >= count - RATIO)


def expand(coarse, first):
    lane = lanes_of(coarse.shape)
    return jnp.take_along_axis(coarse, (lane + first) // RATIO, axis=1)


def expand_all(coarse):
    parts = [expand(coarse, first) for first in range(0, COLS, LANES)]
    return jnp.concatenate(parts, axis=1)


def turn(x, amount):
    amount = amount % x.shape[1]
    return x if amount == 0 else pltpu.roll(x, amount, 1)


def next_col(x):
    return pltpu.roll(x, x.shape[1] - 1, 1)


def prev_col(x):
    return pltpu.roll(x, 1, 1)


def level_up(x):
    levels = x.shape[0]
    level = lax.broadcasted_iota(jnp.int32, x.shape, 0)
    return jnp.where(level < levels - 1, pltpu.roll(x, levels - 1, 0), 0.0)


def level_down(x):
    level = lax.broadcasted_iota(jnp.int32, x.shape, 0)
    return jnp.where(level > 0, pltpu.roll(x, 1, 0), 0.0)


def split_dot(table, x):
    high = x.astype(BF16)
    low = (x - high.astype(F32)).astype(BF16)
    stacked = jnp.concatenate([high, low, high], axis=0)
    return jnp.dot(table, stacked, preferred_element_type=F32)


def prepare_kernel(counts, off_ref, nest_ref, stiff_ref, parent_ref, cur_ref, left_ref, right_ref, edge_ref):
    nx, ny = counts
    gx, gy = lax.axis_index("gx"), lax.axis_index("gy")
    off_x, off_y = off_ref[0], off_ref[1]
    levels = nest_ref.shape[2]
    col = lanes_of((levels, COLS)) + (gy * COLS - RATIO * off_y)
    edge_col = is_edge(col, ny)
    place = lanes_of((levels, LANES)) // SIDE
    packs = {}

    def pack(row, group):
        tile, slot = group // PER_TILE, group % PER_TILE
        to_left = turn(row[:, :LANES], SIDE * slot)
        to_right = turn(row[:, COLS - LANES :], SIDE * (slot + 1) - LANES)
        if slot == 0:
            packs[tile] = (to_left, to_right)
        else:
            left, right = packs[tile]
            here = place == slot
            packs[tile] = (jnp.where(here, to_left, left), jnp.where(here, to_right, right))
        if slot == PER_TILE - 1 or group == GROUPS - 1:
            at = slice(LANES * tile, LANES * (tile + 1))
            left_ref[:, at] = packs[tile][0]
            right_ref[:, at] = packs[tile][1]

    rims = []
    for field in range(4):
        bounds = [expand_all(parent_ref[field, :, coarse, :]) for coarse in range(ROWS // RATIO)]
        for row in range(ROWS):
            i = gx * ROWS + row - RATIO * off_x
            held = is_edge(i, nx).astype(jnp.int32)
            value = jnp.where(edge_col | (held > 0), bounds[row // RATIO], nest_ref[field, row])
            cur_ref[field, row] = value
            pack(value, field * ROWS + row)
        rim = jnp.where(gx == 0, bounds[0], bounds[-1])
        edge_ref[field] = rim
        rims.append(rim)
    for row in range(ROWS):
        pack(stiff_ref[row], S_GROUP + row)
    for field in range(4):
        pack(rims[field], EDGE_GROUP + field)


def message_kernel(last_y, cur_ref, stiff_ref, parent_ref, left_ref, right_ref, up_ref, down_ref):
    gx, gy = lax.axis_index("gx"), lax.axis_index("gy")
    up_ref[PACK_AT] = left_ref[...]
    up_ref[PACK_AT + 1] = right_ref[...]
    levels = stiff_ref.shape[1]
    place = lanes_of((levels, LANES)) // SIDE

    def fill(slot_row, cell):
        for tile in range(PACK // LANES):
            at = slice(LANES * tile, LANES * (tile + 1))
            out = up_ref[slot_row, :, at]
            for slot in range(PER_TILE):
                group = tile * PER_TILE + slot
                if group < S_GROUP:
                    field, coarse = group // ROWS, (group % ROWS) // RATIO
                    value = parent_ref[field, :, coarse, cell : cell + 1]
                elif EDGE_GROUP <= group < GROUPS:
                    field = group - EDGE_GROUP
                    value = jnp.where(
                        gx == 0,
                        parent_ref[field, :, 0, cell : cell + 1],
                        parent_ref[field, :, ROWS // RATIO - 1, cell : cell + 1],
                    )
                else:
                    continue
                out = jnp.where(place == slot, value, out)
            up_ref[slot_row, :, at] = out

    @pl.when(gy == 0)
    def _():
        fill(PACK_AT, 0)

    @pl.when(gy == last_y)
    def _():
        fill(PACK_AT + 1, COLS // RATIO - 1)

    for pack in range(2):
        down_ref[PACK_AT + pack] = up_ref[PACK_AT + pack]
    for field, at, deep in ((PR, P_AT, P_DEEP), (U, U_AT, U_DEEP), (V, V_AT, V_DEEP), (W, W_AT, W_DEEP)):
        for row in range(deep):
            up_ref[at + row] = cur_ref[field, ROWS - deep + row]
            down_ref[at + row] = cur_ref[field, row]
    for row in range(ROWS):
        up_ref[S_AT + row] = stiff_ref[row]
        down_ref[S_AT + row] = stiff_ref[row]


def held_lanes(gy, off_y, ny, shape):
    j = column_of_lane(shape) + (gy * COLS - RATIO * off_y)
    return is_edge(j, ny).astype(jnp.int32)


def held_row(gx, row, off_x, nx):
    return is_edge(gx * ROWS + row - RATIO * off_x, nx).astype(jnp.int32)


def winds_x(held, gx, off_x, nx, p_ref, u_ref, out_ref):
    def body(at, carry):
        keep = (held + held_row(gx, at - U_DEEP, off_x, nx)) > 0
        wind = u_ref[at]
        out_ref[at] = jnp.where(keep, wind, wind - GRAD * (p_ref[at + 2] - p_ref[at]))
        return carry

    lax.fori_loop(0, ROWS + 2 * U_DEEP, body, 0)


def column_step(held, gx, off_x, nx, table, u_ref, p_ref, v_of, w_of, s_of, put):
    def body(at, carry):
        keep = (held + held_row(gx, at - KEEP, off_x, nx)) > 0
        pressure = p_ref[at + P_DEEP - KEEP]
        wind = v_of(at)
        wind = jnp.where(keep, wind, wind - GRAD * (next_col(pressure) - prev_col(pressure)))
        lift = w_of(at)
        divergence = (u_ref[at + 2] - u_ref[at]) + (next_col(wind) - prev_col(wind))
        right_side = pressure - DIV * divergence - COUPLE * (level_up(lift) - level_down(lift))
        levels = pressure.shape[0]
        both = split_dot(table, right_side)
        first, around = both[:levels], both[levels:]
        leftover = right_side - ((1.0 + s_of(at)) * first - 0.25 * around)
        solved = first + split_dot(table[:levels], leftover)
        p_next = jnp.where(keep, pressure, solved)
        w_next = jnp.where(keep, lift, lift - LIFT * (level_up(p_next) - p_next))
        put(at, wind, w_next, p_next)
        return carry

    lax.fori_loop(0, WIN, body, 0)


def first_kernel(
    counts, off_ref, cur_ref, stiff_ref, edge_ref, mine_ref, low_ref, high_ref, table_ref,
    u_out, v_out, w_out, p_out, s_out, up_out, down_out,
    p_win, u_win, v_win, w_win, s_win,
):
    nx, ny = counts
    gx, gy = lax.axis_index("gx"), lax.axis_index("gy")
    off_x, off_y = off_ref[0], off_ref[1]
    levels = stiff_ref.shape[1]
    lane = lanes_of((levels, LANES))

    def beside(source, group):
        tile, slot = group // PER_TILE, group % PER_TILE
        at = slice(LANES * tile, LANES * (tile + 1))
        left = turn(source[PACK_AT, :, at], LANES - SIDE * (slot + 1))
        right = turn(source[PACK_AT + 1, :, at], -SIDE * slot)
        return jnp.where(lane < LANES // 2, right, left)

    def place(window, at, main, ext):
        window[at, :, :COLS] = main
        window[at, :, COLS:] = ext

    for field, at, deep, window in (
        (PR, P_AT, P_DEEP, p_win),
        (U, U_AT, U_DEEP, u_win),
        (V, V_AT, V_DEEP, v_win),
        (W, W_AT, W_DEEP, w_win),
    ):
        for row in range(deep):
            place(window, row, low_ref[at + row], beside(low_ref, field * ROWS + ROWS - deep + row))
            place(window, deep + ROWS + row, high_ref[at + row], beside(high_ref, field * ROWS + row))
        for row in range(ROWS):
            place(window, deep + row, cur_ref[field, row], beside(mine_ref, field * ROWS + row))

        @pl.when(gx == 0)
        def _(field=field, deep=deep, window=window):
            for row in range(deep - KEEP, deep):
                place(window, row, edge_ref[field], beside(mine_ref, EDGE_GROUP + field))

        @pl.when(gx == nx // ROWS - 1)
        def _(field=field, deep=deep, window=window):
            for row in range(deep + ROWS, deep + ROWS + KEEP):
                place(window, row, edge_ref[field], beside(mine_ref, EDGE_GROUP + field))

    for row in range(ROWS):
        place(s_win, row, low_ref[S_AT + row], beside(low_ref, S_GROUP + row))
        place(s_win, ROWS + row, stiff_ref[row], beside(mine_ref, S_GROUP + row))
        place(s_win, 2 * ROWS + row, high_ref[S_AT + row], beside(high_ref, S_GROUP + row))

    held = held_lanes(gy, off_y, ny, (levels, WIDE))
    winds_x(held, gx, off_x, nx, p_win, u_win, u_out)
    move_y = lax.rem(RATIO * off_y + WIDE, WIDE)

    def stiffness(at):
        value = pltpu.roll(s_win[at + ROWS - KEEP - RATIO * off_x], move_y, 1)
        s_out[at] = value
        return value

    def put(at, v_next, w_next, p_next):
        v_out[at] = v_next
        w_out[at] = w_next
        p_out[at] = p_next

    column_step(
        held, gx, off_x, nx, table_ref[...], u_out, p_win,
        lambda at: v_win[at], lambda at: w_win[at], stiffness, put,
    )
    far = P_DEEP - KEEP
    for row in range(far):
        up_out[row] = p_out[KEEP + ROWS - P_DEEP + row]
        down_out[row] = p_out[KEEP + KEEP + row]


def second_kernel(
    counts, off_ref, u_ref, v_ref, w_ref, p_ref, s_ref, low_ref, high_ref, table_ref, parent_ref,
    new_ref, back_ref,
    p_win, u_win, v_win, w_win, q_win,
):
    nx, ny = counts
    gx, gy = lax.axis_index("gx"), lax.axis_index("gy")
    off_x, off_y = off_ref[0], off_ref[1]
    levels = u_ref.shape[1]
    far = P_DEEP - KEEP
    for row in range(far):
        p_win[row] = low_ref[row]
        p_win[far + WIN + row] = high_ref[row]
    for row in range(WIN):
        p_win[far + row] = p_ref[row]
    held = held_lanes(gy, off_y, ny, (levels, WIDE))
    winds_x(held, gx, off_x, nx, p_win, u_ref, u_win)

    def put(at, v_next, w_next, p_next):
        v_win[at] = v_next
        w_win[at] = w_next
        q_win[at] = p_next

    column_step(
        held, gx, off_x, nx, table_ref[...], u_win, p_win,
        lambda at: v_ref[at], lambda at: w_ref[at], lambda at: s_ref[at], put,
    )
    move_y = lax.rem(WIDE - RATIO * off_y, WIDE)
    windows = ((U, u_win, U_DEEP), (V, v_win, KEEP), (W, w_win, KEEP), (PR, q_win, KEEP))
    for field, window, deep in windows:
        for row in range(ROWS):
            moved = pltpu.roll(window[row + deep + RATIO * off_x], move_y, 1)
            new_ref[field, row] = moved[:, :COLS]

    cells_x, cells_y = nx // RATIO, ny // RATIO
    coarse_rows, coarse_cols = ROWS // RATIO, COLS // RATIO
    first_cell = gy * coarse_cols - off_y

    def inside(index, count):
        return (index >= 1) & (index <= count - 2)

    lane = lax.broadcasted_iota(jnp.int32, (WIDE, coarse_cols), 0)
    source = jnp.where(lane < COLS + LANES // 2, lane, lane - WIDE)
    apart = source - RATIO * lax.broadcasted_iota(jnp.int32, (WIDE, coarse_cols), 1)
    spread = jnp.where(
        (apart >= 0) & (apart < RATIO),
        0.5,
        jnp.where((apart >= -RATIO) & (apart < 2 * RATIO), 0.25, 0.0),
    ).astype(BF16)
    cell = lanes_of((levels, coarse_cols)) + first_cell
    weight_y = (
        0.25 * inside(cell - 1, cells_y).astype(F32)
        + 0.5 * inside(cell, cells_y).astype(F32)
        + 0.25 * inside(cell + 1, cells_y).astype(F32)
    )
    centre_y = inside(cell, cells_y).astype(jnp.int32)
    for coarse in range(coarse_rows):
        a = gx * coarse_rows + coarse - off_x
        inner = [inside(a + d, cells_x).astype(F32) for d in (-1, 0, 1)]
        weights = [s * m for s, m in zip((0.25, 0.5, 0.25), inner)]
        weight_x = weights[0] + weights[1] + weights[2]
        centre = (centre_y * inside(a, cells_x).astype(jnp.int32)) > 0
        scale = jnp.where(centre, 1.0 / jnp.where(centre, 9.0 * weight_x * weight_y, 1.0), 0.0)
        for field, window, deep in windows:
            start = deep - KEEP + RATIO * coarse
            total = None
            for d in range(3):
                part = window[start + 3 * d] + window[start + 3 * d + 1] + window[start + 3 * d + 2]
                part = jnp.where(inner[d] > 0, part * weights[d], 0.0)
                total = part if total is None else total + part
            total = jnp.where(held > 0, 0.0, total)
            high = total.astype(BF16)
            low = (total - high.astype(F32)).astype(BF16)
            summed = jnp.dot(high, spread, preferred_element_type=F32) + jnp.dot(
                low, spread, preferred_element_type=F32
            )
            back_ref[field, :, coarse, :] = jnp.where(centre, summed * scale, parent_ref[field, :, coarse, :])


def vmem_specs(count):
    return [pl.BlockSpec(memory_space=pltpu.VMEM)] * count


def call(body, ins, outs, scratch=()):
    smem = [pl.BlockSpec(memory_space=pltpu.SMEM) if x.dtype == jnp.int32 else pl.BlockSpec(memory_space=pltpu.VMEM) for x in ins]
    return pl.pallas_call(
        body,
        out_shape=[jax.ShapeDtypeStruct(shape, F32) for shape in outs],
        in_specs=smem,
        out_specs=vmem_specs(len(outs)),
        scratch_shapes=[pltpu.VMEM(shape, F32) for shape in scratch],
        compiler_params=pltpu.CompilerParams(vmem_limit_bytes=VMEM_BYTES),
    )(*ins)


def steps(axis, by):
    count = lax.axis_size(axis)
    return [(i, i + by) for i in range(count) if 0 <= i + by < count]


def per_device(nest_state, stiffness, parent, inverse_table, offsets):
    levels = nest_state.shape[1]
    nx = nest_state.shape[2] * lax.axis_size("gx")
    ny = nest_state.shape[3] * lax.axis_size("gy")
    counts = (nx, ny)
    nest = jnp.transpose(nest_state, (0, 2, 1, 3))
    stiff = jnp.transpose(stiffness, (1, 0, 2))

    shifted = jnp.concatenate([inverse_table[1:], jnp.zeros_like(inverse_table[:1])], 0) + jnp.concatenate(
        [jnp.zeros_like(inverse_table[:1]), inverse_table[:-1]], 0
    )
    stack = jnp.concatenate([inverse_table, shifted], 0)
    top = lax.reduce_precision(stack, 8, 7)
    table = jnp.concatenate([top, top, stack - top], 1).astype(BF16)

    cur, to_left, to_right, edge = call(
        functools.partial(prepare_kernel, counts),
        (offsets, nest, stiff, parent),
        [nest.shape, (levels, PACK), (levels, PACK), (4, levels, COLS)],
    )
    from_left = lax.ppermute(to_right, "gy", steps("gy", 1))
    from_right = lax.ppermute(to_left, "gy", steps("gy", -1))
    message = (MESSAGE, levels, COLS)
    up, down = call(
        functools.partial(message_kernel, lax.axis_size("gy") - 1),
        (cur, stiff, parent, from_left, from_right),
        [message, message],
    )
    low = lax.ppermute(up, "gx", steps("gx", 1))
    high = lax.ppermute(down, "gx", steps("gx", -1))
    win = (WIN, levels, WIDE)
    u_shape = (ROWS + 2 * U_DEEP, levels, WIDE)
    p_shape = (ROWS + 2 * P_DEEP, levels, WIDE)
    far = (P_DEEP - KEEP, levels, WIDE)
    u1, v1, w1, p1, s1, up, down = call(
        functools.partial(first_kernel, counts),
        (offsets, cur, stiff, edge, up, low, high, table),
        [u_shape, win, win, win, win, far, far],
        [p_shape, u_shape, win, win, (3 * ROWS, levels, WIDE)],
    )
    low = lax.ppermute(up, "gx", steps("gx", 1))
    high = lax.ppermute(down, "gx", steps("gx", -1))
    new, back = call(
        functools.partial(second_kernel, counts),
        (offsets, u1, v1, w1, p1, s1, low, high, table, parent),
        [nest.shape, parent.shape],
        [p_shape, u_shape, win, win, win],
    )
    return jnp.transpose(new, (0, 2, 1, 3)), back


def solution(mesh):
    return jax.shard_map(
        per_device,
        mesh=mesh,
        in_specs=(
            P(None, None, "gx", "gy"),
            P(None, "gx", "gy"),
            P(None, None, "gx", "gy"),
            P(),
            P(),
        ),
        out_specs=(P(None, None, "gx", "gy"), P(None, None, "gx", "gy")),
        check_vma=False,
    )
```

```python
import functools

import jax
import jax.numpy as jnp
from jax import lax
from jax.experimental import pallas as pl
from jax.experimental.pallas import tpu as pltpu
from jax.sharding import PartitionSpec as P

RATIO = 3
GRAD = 0.25
DIV = 0.25
COUPLE = 0.25
LIFT = 0.5
F32 = jnp.float32
BF16 = jnp.bfloat16
VMEM_BYTES = 32 * 1024 * 1024

ROWS = 6
COLS = 384
LANES = 128
WIDE = COLS + LANES
SIDE = 8
PER_TILE = LANES // SIDE
P_DEEP, U_DEEP, V_DEEP, W_DEEP = 5, 4, 3, 3
KEEP = 3
WIN = ROWS + 2 * KEEP
P_AT = 0
U_AT = P_AT + P_DEEP
V_AT = U_AT + U_DEEP
W_AT = V_AT + V_DEEP
S_AT = W_AT + W_DEEP
PACK_AT = S_AT + ROWS
MESSAGE = PACK_AT + 2
S_GROUP = 4 * ROWS
EDGE_GROUP = S_GROUP + ROWS
GROUPS = EDGE_GROUP + 4
PACK = -(-GROUPS // PER_TILE) * LANES
U, V, W, PR = 0, 1, 2, 3


def lanes_of(shape):
    return lax.broadcasted_iota(jnp.int32, shape, len(shape) - 1)


def column_of_lane(shape):
    lane = lanes_of(shape)
    return jnp.where(lane < COLS + LANES // 2, lane, lane - WIDE)


def is_edge(index, count):
    return (index < RATIO) | (index >= count - RATIO)


def expand(coarse, first):
    lane = lanes_of(coarse.shape)
    return jnp.take_along_axis(coarse, (lane + first) // RATIO, axis=1)


def expand_all(coarse):
    parts = [expand(coarse, first) for first in range(0, COLS, LANES)]
    return jnp.concatenate(parts, axis=1)


def turn(x, amount):
    amount = amount % x.shape[1]
    return x if amount == 0 else pltpu.roll(x, amount, 1)


def next_col(x):
    return pltpu.roll(x, x.shape[1] - 1, 1)


def prev_col(x):
    return pltpu.roll(x, 1, 1)


def level_up(x):
    levels = x.shape[0]
    level = lax.broadcasted_iota(jnp.int32, x.shape, 0)
    return jnp.where(level < levels - 1, pltpu.roll(x, levels - 1, 0), 0.0)


def level_down(x):
    level = lax.broadcasted_iota(jnp.int32, x.shape, 0)
    return jnp.where(level > 0, pltpu.roll(x, 1, 0), 0.0)


def split_dot(table, x):
    high = x.astype(BF16)
    low = (x - high.astype(F32)).astype(BF16)
    stacked = jnp.concatenate([high, low, high], axis=0)
    return jnp.dot(table, stacked, preferred_element_type=F32)


def prepare_kernel(counts, off_ref, nest_ref, stiff_ref, parent_ref, cur_ref, left_ref, right_ref, edge_ref):
    nx, ny = counts
    gx, gy = lax.axis_index("gx"), lax.axis_index("gy")
    off_x, off_y = off_ref[0], off_ref[1]
    levels = nest_ref.shape[2]
    col = lanes_of((levels, COLS)) + (gy * COLS - RATIO * off_y)
    edge_col = is_edge(col, ny)
    place = lanes_of((levels, LANES)) // SIDE
    packs = {}

    def pack(row, group):
        tile, slot = group // PER_TILE, group % PER_TILE
        to_left = turn(row[:, :LANES], SIDE * slot)
        to_right = turn(row[:, COLS - LANES :], SIDE * (slot + 1) - LANES)
        if slot == 0:
            packs[tile] = (to_left, to_right)
        else:
            left, right = packs[tile]
            here = place == slot
            packs[tile] = (jnp.where(here, to_left, left), jnp.where(here, to_right, right))
        if slot == PER_TILE - 1 or group == GROUPS - 1:
            at = slice(LANES * tile, LANES * (tile + 1))
            left_ref[:, at] = packs[tile][0]
            right_ref[:, at] = packs[tile][1]

    rims = []
    for field in range(4):
        bounds = [expand_all(parent_ref[field, :, coarse, :]) for coarse in range(ROWS // RATIO)]
        for row in range(ROWS):
            i = gx * ROWS + row - RATIO * off_x
            held = is_edge(i, nx).astype(jnp.int32)
            value = jnp.where(edge_col | (held > 0), bounds[row // RATIO], nest_ref[field, row])
            cur_ref[field, row] = value
            pack(value, field * ROWS + row)
        rim = jnp.where(gx == 0, bounds[0], bounds[-1])
        edge_ref[field] = rim
        rims.append(rim)
    for row in range(ROWS):
        pack(stiff_ref[row], S_GROUP + row)
    for field in range(4):
        pack(rims[field], EDGE_GROUP + field)


def message_kernel(last_y, cur_ref, stiff_ref, parent_ref, left_ref, right_ref, up_ref, down_ref):
    gx, gy = lax.axis_index("gx"), lax.axis_index("gy")
    up_ref[PACK_AT] = left_ref[...]
    up_ref[PACK_AT + 1] = right_ref[...]
    levels = stiff_ref.shape[1]
    place = lanes_of((levels, LANES)) // SIDE

    def fill(slot_row, cell):
        for tile in range(PACK // LANES):
            at = slice(LANES * tile, LANES * (tile + 1))
            out = up_ref[slot_row, :, at]
            for slot in range(PER_TILE):
                group = tile * PER_TILE + slot
                if group < S_GROUP:
                    field, coarse = group // ROWS, (group % ROWS) // RATIO
                    value = parent_ref[field, :, coarse, cell : cell + 1]
                elif EDGE_GROUP <= group < GROUPS:
                    field = group - EDGE_GROUP
                    value = jnp.where(
                        gx == 0,
                        parent_ref[field, :, 0, cell : cell + 1],
                        parent_ref[field, :, ROWS // RATIO - 1, cell : cell + 1],
                    )
                else:
                    continue
                out = jnp.where(place == slot, value, out)
            up_ref[slot_row, :, at] = out

    @pl.when(gy == 0)
    def _():
        fill(PACK_AT, 0)

    @pl.when(gy == last_y)
    def _():
        fill(PACK_AT + 1, COLS // RATIO - 1)

    for pack in range(2):
        down_ref[PACK_AT + pack] = up_ref[PACK_AT + pack]
    for field, at, deep in ((PR, P_AT, P_DEEP), (U, U_AT, U_DEEP), (V, V_AT, V_DEEP), (W, W_AT, W_DEEP)):
        for row in range(deep):
            up_ref[at + row] = cur_ref[field, ROWS - deep + row]
            down_ref[at + row] = cur_ref[field, row]
    for row in range(ROWS):
        up_ref[S_AT + row] = stiff_ref[row]
        down_ref[S_AT + row] = stiff_ref[row]


def held_lanes(gy, off_y, ny, shape):
    j = column_of_lane(shape) + (gy * COLS - RATIO * off_y)
    return is_edge(j, ny).astype(jnp.int32)


def held_row(gx, row, off_x, nx):
    return is_edge(gx * ROWS + row - RATIO * off_x, nx).astype(jnp.int32)


def winds_x(held, gx, off_x, nx, p_ref, u_ref, out_ref):
    def body(at, carry):
        keep = (held + held_row(gx, at - U_DEEP, off_x, nx)) > 0
        wind = u_ref[at]
        out_ref[at] = jnp.where(keep, wind, wind - GRAD * (p_ref[at + 2] - p_ref[at]))
        return carry

    lax.fori_loop(0, ROWS + 2 * U_DEEP, body, 0, unroll=2)


def column_step(held, gx, off_x, nx, table, u_ref, p_ref, v_of, w_of, s_of, put):
    def body(at, carry):
        keep = (held + held_row(gx, at - KEEP, off_x, nx)) > 0
        pressure = p_ref[at + P_DEEP - KEEP]
        wind = v_of(at)
        wind = jnp.where(keep, wind, wind - GRAD * (next_col(pressure) - prev_col(pressure)))
        lift = w_of(at)
        divergence = (u_ref[at + 2] - u_ref[at]) + (next_col(wind) - prev_col(wind))
        right_side = pressure - DIV * divergence - COUPLE * (level_up(lift) - level_down(lift))
        levels = pressure.shape[0]
        both = split_dot(table, right_side)
        first, around = both[:levels], both[levels:]
        leftover = right_side - ((1.0 + s_of(at)) * first - 0.25 * around)
        solved = first + split_dot(table[:levels], leftover)
        p_next = jnp.where(keep, pressure, solved)
        w_next = jnp.where(keep, lift, lift - LIFT * (level_up(p_next) - p_next))
        put(at, wind, w_next, p_next)
        return carry

    lax.fori_loop(0, WIN, body, 0, unroll=6)


def first_kernel(
    counts, off_ref, cur_ref, stiff_ref, edge_ref, mine_ref, low_ref, high_ref, table_ref,
    u_out, v_out, w_out, p_out, s_out, up_out, down_out,
    p_win, u_win, v_win, w_win, s_win,
):
    nx, ny = counts
    gx, gy = lax.axis_index("gx"), lax.axis_index("gy")
    off_x, off_y = off_ref[0], off_ref[1]
    levels = stiff_ref.shape[1]
    lane = lanes_of((levels, LANES))

    def beside(source, group):
        tile, slot = group // PER_TILE, group % PER_TILE
        at = slice(LANES * tile, LANES * (tile + 1))
        left = turn(source[PACK_AT, :, at], LANES - SIDE * (slot + 1))
        right = turn(source[PACK_AT + 1, :, at], -SIDE * slot)
        return jnp.where(lane < LANES // 2, right, left)

    def place(window, at, main, ext):
        window[at, :, :COLS] = main
        window[at, :, COLS:] = ext

    for field, at, deep, window in (
        (PR, P_AT, P_DEEP, p_win),
        (U, U_AT, U_DEEP, u_win),
        (V, V_AT, V_DEEP, v_win),
        (W, W_AT, W_DEEP, w_win),
    ):
        for row in range(deep):
            place(window, row, low_ref[at + row], beside(low_ref, field * ROWS + ROWS - deep + row))
            place(window, deep + ROWS + row, high_ref[at + row], beside(high_ref, field * ROWS + row))
        for row in range(ROWS):
            place(window, deep + row, cur_ref[field, row], beside(mine_ref, field * ROWS + row))

        @pl.when(gx == 0)
        def _(field=field, deep=deep, window=window):
            for row in range(deep - KEEP, deep):
                place(window, row, edge_ref[field], beside(mine_ref, EDGE_GROUP + field))

        @pl.when(gx == nx // ROWS - 1)
        def _(field=field, deep=deep, window=window):
            for row in range(deep + ROWS, deep + ROWS + KEEP):
                place(window, row, edge_ref[field], beside(mine_ref, EDGE_GROUP + field))

    for row in range(ROWS):
        place(s_win, row, low_ref[S_AT + row], beside(low_ref, S_GROUP + row))
        place(s_win, ROWS + row, stiff_ref[row], beside(mine_ref, S_GROUP + row))
        place(s_win, 2 * ROWS + row, high_ref[S_AT + row], beside(high_ref, S_GROUP + row))

    held = held_lanes(gy, off_y, ny, (levels, WIDE))
    winds_x(held, gx, off_x, nx, p_win, u_win, u_out)
    move_y = lax.rem(RATIO * off_y + WIDE, WIDE)

    def stiffness(at):
        value = pltpu.roll(s_win[at + ROWS - KEEP - RATIO * off_x], move_y, 1)
        s_out[at] = value
        return value

    def put(at, v_next, w_next, p_next):
        v_out[at] = v_next
        w_out[at] = w_next
        p_out[at] = p_next

    column_step(
        held, gx, off_x, nx, table_ref[...], u_out, p_win,
        lambda at: v_win[at], lambda at: w_win[at], stiffness, put,
    )
    far = P_DEEP - KEEP
    for row in range(far):
        up_out[row] = p_out[KEEP + ROWS - P_DEEP + row]
        down_out[row] = p_out[KEEP + KEEP + row]


def second_kernel(
    counts, off_ref, u_ref, v_ref, w_ref, p_ref, s_ref, low_ref, high_ref, table_ref, parent_ref,
    new_ref, back_ref,
    p_win, u_win, v_win, w_win, q_win,
):
    nx, ny = counts
    gx, gy = lax.axis_index("gx"), lax.axis_index("gy")
    off_x, off_y = off_ref[0], off_ref[1]
    levels = u_ref.shape[1]
    far = P_DEEP - KEEP
    for row in range(far):
        p_win[row] = low_ref[row]
        p_win[far + WIN + row] = high_ref[row]
    for row in range(WIN):
        p_win[far + row] = p_ref[row]
    held = held_lanes(gy, off_y, ny, (levels, WIDE))
    winds_x(held, gx, off_x, nx, p_win, u_ref, u_win)

    def put(at, v_next, w_next, p_next):
        v_win[at] = v_next
        w_win[at] = w_next
        q_win[at] = p_next

    column_step(
        held, gx, off_x, nx, table_ref[...], u_win, p_win,
        lambda at: v_ref[at], lambda at: w_ref[at], lambda at: s_ref[at], put,
    )
    move_y = lax.rem(WIDE - RATIO * off_y, WIDE)
    windows = ((U, u_win, U_DEEP), (V, v_win, KEEP), (W, w_win, KEEP), (PR, q_win, KEEP))
    for field, window, deep in windows:
        for row in range(ROWS):
            moved = pltpu.roll(window[row + deep + RATIO * off_x], move_y, 1)
            new_ref[field, row] = moved[:, :COLS]

    cells_x, cells_y = nx // RATIO, ny // RATIO
    coarse_rows, coarse_cols = ROWS // RATIO, COLS // RATIO
    first_cell = gy * coarse_cols - off_y

    def inside(index, count):
        return (index >= 1) & (index <= count - 2)

    lane = lax.broadcasted_iota(jnp.int32, (WIDE, coarse_cols), 0)
    source = jnp.where(lane < COLS + LANES // 2, lane, lane - WIDE)
    apart = source - RATIO * lax.broadcasted_iota(jnp.int32, (WIDE, coarse_cols), 1)
    spread = jnp.where(
        (apart >= 0) & (apart < RATIO),
        0.5,
        jnp.where((apart >= -RATIO) & (apart < 2 * RATIO), 0.25, 0.0),
    ).astype(BF16)
    cell = lanes_of((levels, coarse_cols)) + first_cell
    weight_y = (
        0.25 * inside(cell - 1, cells_y).astype(F32)
        + 0.5 * inside(cell, cells_y).astype(F32)
        + 0.25 * inside(cell + 1, cells_y).astype(F32)
    )
    centre_y = inside(cell, cells_y).astype(jnp.int32)
    for coarse in range(coarse_rows):
        a = gx * coarse_rows + coarse - off_x
        inner = [inside(a + d, cells_x).astype(F32) for d in (-1, 0, 1)]
        weights = [s * m for s, m in zip((0.25, 0.5, 0.25), inner)]
        weight_x = weights[0] + weights[1] + weights[2]
        centre = (centre_y * inside(a, cells_x).astype(jnp.int32)) > 0
        scale = jnp.where(centre, 1.0 / jnp.where(centre, 9.0 * weight_x * weight_y, 1.0), 0.0)
        for field, window, deep in windows:
            start = deep - KEEP + RATIO * coarse
            total = None
            for d in range(3):
                part = window[start + 3 * d] + window[start + 3 * d + 1] + window[start + 3 * d + 2]
                part = jnp.where(inner[d] > 0, part * weights[d], 0.0)
                total = part if total is None else total + part
            total = jnp.where(held > 0, 0.0, total)
            high = total.astype(BF16)
            low = (total - high.astype(F32)).astype(BF16)
            summed = jnp.dot(high, spread, preferred_element_type=F32) + jnp.dot(
                low, spread, preferred_element_type=F32
            )
            back_ref[field, :, coarse, :] = jnp.where(centre, summed * scale, parent_ref[field, :, coarse, :])


def vmem_specs(count):
    return [pl.BlockSpec(memory_space=pltpu.VMEM)] * count


def call(body, ins, outs, scratch=()):
    smem = [pl.BlockSpec(memory_space=pltpu.SMEM) if x.dtype == jnp.int32 else pl.BlockSpec(memory_space=pltpu.VMEM) for x in ins]
    return pl.pallas_call(
        body,
        out_shape=[jax.ShapeDtypeStruct(shape, F32) for shape in outs],
        in_specs=smem,
        out_specs=vmem_specs(len(outs)),
        scratch_shapes=[pltpu.VMEM(shape, F32) for shape in scratch],
        compiler_params=pltpu.CompilerParams(vmem_limit_bytes=VMEM_BYTES),
    )(*ins)


def steps(axis, by):
    count = lax.axis_size(axis)
    return [(i, i + by) for i in range(count) if 0 <= i + by < count]


def per_device(nest_state, stiffness, parent, inverse_table, offsets):
    levels = nest_state.shape[1]
    nx = nest_state.shape[2] * lax.axis_size("gx")
    ny = nest_state.shape[3] * lax.axis_size("gy")
    counts = (nx, ny)
    nest = jnp.transpose(nest_state, (0, 2, 1, 3))
    stiff = jnp.transpose(stiffness, (1, 0, 2))

    shifted = jnp.concatenate([inverse_table[1:], jnp.zeros_like(inverse_table[:1])], 0) + jnp.concatenate(
        [jnp.zeros_like(inverse_table[:1]), inverse_table[:-1]], 0
    )
    stack = jnp.concatenate([inverse_table, shifted], 0)
    top = lax.reduce_precision(stack, 8, 7)
    table = jnp.concatenate([top, top, stack - top], 1).astype(BF16)

    cur, to_left, to_right, edge = call(
        functools.partial(prepare_kernel, counts),
        (offsets, nest, stiff, parent),
        [nest.shape, (levels, PACK), (levels, PACK), (4, levels, COLS)],
    )
    from_left = lax.ppermute(to_right, "gy", steps("gy", 1))
    from_right = lax.ppermute(to_left, "gy", steps("gy", -1))
    message = (MESSAGE, levels, COLS)
    up, down = call(
        functools.partial(message_kernel, lax.axis_size("gy") - 1),
        (cur, stiff, parent, from_left, from_right),
        [message, message],
    )
    low = lax.ppermute(up, "gx", steps("gx", 1))
    high = lax.ppermute(down, "gx", steps("gx", -1))
    win = (WIN, levels, WIDE)
    u_shape = (ROWS + 2 * U_DEEP, levels, WIDE)
    p_shape = (ROWS + 2 * P_DEEP, levels, WIDE)
    far = (P_DEEP - KEEP, levels, WIDE)
    u1, v1, w1, p1, s1, up, down = call(
        functools.partial(first_kernel, counts),
        (offsets, cur, stiff, edge, up, low, high, table),
        [u_shape, win, win, win, win, far, far],
        [p_shape, u_shape, win, win, (3 * ROWS, levels, WIDE)],
    )
    low = lax.ppermute(up, "gx", steps("gx", 1))
    high = lax.ppermute(down, "gx", steps("gx", -1))
    new, back = call(
        functools.partial(second_kernel, counts),
        (offsets, u1, v1, w1, p1, s1, low, high, table, parent),
        [nest.shape, parent.shape],
        [p_shape, u_shape, win, win, win],
    )
    return jnp.transpose(new, (0, 2, 1, 3)), back


def solution(mesh):
    return jax.shard_map(
        per_device,
        mesh=mesh,
        in_specs=(
            P(None, None, "gx", "gy"),
            P(None, "gx", "gy"),
            P(None, None, "gx", "gy"),
            P(),
            P(),
        ),
        out_specs=(P(None, None, "gx", "gy"), P(None, None, "gx", "gy")),
        check_vma=False,
    )
```

```python
import functools

import jax
import jax.numpy as jnp
from jax import lax
from jax.experimental import pallas as pl
from jax.experimental.pallas import tpu as pltpu
from jax.sharding import PartitionSpec as P

RATIO = 3
GRAD = 0.25
DIV = 0.25
COUPLE = 0.25
LIFT = 0.5
F32 = jnp.float32
BF16 = jnp.bfloat16
VMEM_BYTES = 24 * 1024 * 1024

ROWS = 6
COLS = 384
LANES = 128
WIDE = COLS + LANES
SIDE = 8
SLOTS = LANES // SIDE
U, V, W, PR = 0, 1, 2, 3
DEEP = {PR: 5, U: 4, V: 3, W: 3}
NEAR = {PR: 2, U: 1}
KEEP = 3
S_GROUP = 4 * ROWS
EDGE_GROUP = S_GROUP + ROWS
GROUPS = EDGE_GROUP + 4
PACK = -(-GROUPS // SLOTS) * LANES
CHUNK_1 = ((V, 0, 3), (W, 0, 3), ("s", 0, 3))
CHUNK_2 = ((PR, 0, 2), (U, 0, 1), ("s", 3, 3))
CHUNK_3 = ((PR, 2, 3), (U, 1, 3))
SENT = [(PR, n) for n in range(5)] + [(U, n) for n in range(4)] + [(V, n) for n in range(3)]
SENT += [(W, n) for n in range(3)] + [("s", n) for n in range(6)]


def rows_of(chunk):
    return [(what, first + n) for what, first, count in chunk for n in range(count)]


def lanes_of(shape):
    return lax.broadcasted_iota(jnp.int32, shape, len(shape) - 1)


def column_of_lane(lane):
    return jnp.where(lane < COLS + LANES // 2, lane, lane - WIDE)


def is_edge(index, count):
    return (index < RATIO) | (index >= count - RATIO)


def expand_all(coarse):
    lane = lanes_of(coarse.shape)
    parts = [
        jnp.take_along_axis(coarse, (lane + first) // RATIO, axis=1) for first in range(0, COLS, LANES)
    ]
    return jnp.concatenate(parts, axis=1)


def turn(x, amount):
    amount = amount % x.shape[1]
    return x if amount == 0 else pltpu.roll(x, amount, 1)


def next_col(x):
    return pltpu.roll(x, x.shape[1] - 1, 1)


def prev_col(x):
    return pltpu.roll(x, 1, 1)


def level_up(x):
    levels = x.shape[0]
    level = lax.broadcasted_iota(jnp.int32, x.shape, 0)
    return jnp.where(level < levels - 1, pltpu.roll(x, levels - 1, 0), 0.0)


def level_down(x):
    level = lax.broadcasted_iota(jnp.int32, x.shape, 0)
    return jnp.where(level > 0, pltpu.roll(x, 1, 0), 0.0)


def split_dot(table, x):
    high = x.astype(BF16)
    low = (x - high.astype(F32)).astype(BF16)
    stacked = jnp.concatenate([high, low, high], axis=0)
    return jnp.dot(table, stacked, preferred_element_type=F32)


def own_row(near, side):
    return ROWS - 1 - near if side == 0 else near


def prepare_kernel(
    counts, off_ref, nest_ref, stiff_hbm, parent_hbm,
    cur_ref, stiff_ref, parent_ref, left_ref, right_ref, edge_ref, up_ref, down_ref,
    nest_win, parent_win, sems,
):
    nx, ny = counts
    copies = [pltpu.make_async_copy(parent_hbm, parent_win, sems.at[4])]
    copies += [pltpu.make_async_copy(nest_ref.at[f], nest_win.at[f], sems.at[f]) for f in (V, W, PR, U)]
    copies.append(pltpu.make_async_copy(stiff_hbm, stiff_ref, sems.at[5]))
    for copy in copies:
        copy.start()
    gx, gy = lax.axis_index("gx"), lax.axis_index("gy")
    off_x, off_y = off_ref[0], off_ref[1]
    levels = nest_win.shape[2]
    col = lanes_of((levels, COLS)) + (gy * COLS - RATIO * off_y)
    edge_col = is_edge(col, ny)
    place = lanes_of((levels, LANES)) // SIDE
    packs = [[None, None] for _ in range(PACK // LANES)]

    def pack(row, group):
        tile, slot = group // SLOTS, group % SLOTS
        sides = (
            turn(row[:, :LANES], SIDE * slot),
            turn(row[:, COLS - LANES :], SIDE * (slot + 1) - LANES),
        )
        for side, value in enumerate(sides):
            held = packs[tile][side]
            packs[tile][side] = value if held is None else jnp.where(place == slot, value, held)

    copies[0].wait()
    rims = []
    for at, field in enumerate((V, W, PR, U)):
        bounds = []
        for coarse in range(ROWS // RATIO):
            value = parent_win[field, :, coarse, :]
            parent_ref[field, coarse] = value
            bounds.append(expand_all(value))
        copies[1 + at].wait()
        for row in range(ROWS):
            i = gx * ROWS + row - RATIO * off_x
            held = is_edge(i, nx).astype(jnp.int32)
            value = jnp.where(edge_col | (held > 0), bounds[row // RATIO], nest_win[field, row])
            cur_ref[field, row] = value
            pack(value, field * ROWS + row)
        rim = jnp.where(gx == 0, bounds[0], bounds[-1])
        edge_ref[field] = rim
        pack(rim, EDGE_GROUP + field)
    copies[5].wait()
    for row in range(ROWS):
        pack(stiff_ref[row], S_GROUP + row)
    for tile, (left, right) in enumerate(packs):
        at = slice(LANES * tile, LANES * (tile + 1))
        left_ref[:, at] = left
        right_ref[:, at] = right
    fill_message(CHUNK_1, cur_ref, stiff_ref, up_ref, down_ref)


def fill_message(chunk, cur_ref, stiff_ref, up_ref, down_ref):
    for side, out in ((0, up_ref), (1, down_ref)):
        for at, (what, near) in enumerate(rows_of(chunk)):
            row = own_row(near, side)
            out[at] = stiff_ref[row] if what == "s" else cur_ref[what, row]


def group_of(what, row):
    return S_GROUP + row if what == "s" else what * ROWS + row


def near_kernel(last_y, cur_ref, stiff_ref, parent_ref, left_ref, right_ref, mine_ref, up_ref, down_ref):
    gx, gy = lax.axis_index("gx"), lax.axis_index("gy")
    levels = left_ref.shape[0]
    lane = lanes_of((levels, LANES))
    place = lane // SIDE
    mine_ref[0] = left_ref[...]
    mine_ref[1] = right_ref[...]

    def fill(side, cell):
        for tile in range(PACK // LANES):
            at = slice(LANES * tile, LANES * (tile + 1))
            out = mine_ref[side, :, at]
            for slot in range(SLOTS):
                group = tile * SLOTS + slot
                if group < S_GROUP:
                    value = parent_ref[group // ROWS, (group % ROWS) // RATIO, :, cell : cell + 1]
                elif EDGE_GROUP <= group < GROUPS:
                    field = group - EDGE_GROUP
                    value = jnp.where(
                        gx == 0,
                        parent_ref[field, 0, :, cell : cell + 1],
                        parent_ref[field, ROWS // RATIO - 1, :, cell : cell + 1],
                    )
                else:
                    continue
                out = jnp.where(place == slot, value, out)
            mine_ref[side, :, at] = out

    @pl.when(gy == 0)
    def _():
        fill(0, 0)

    @pl.when(gy == last_y)
    def _():
        fill(1, COLS // RATIO - 1)

    rows = rows_of(CHUNK_2)
    fill_message(CHUNK_2, cur_ref, stiff_ref, up_ref, down_ref)
    for side, out in ((0, up_ref), (1, down_ref)):
        tiles = [None] * (COLS // LANES)
        for hand in range(2):
            for at, (what, near) in enumerate(SENT):
                group = group_of(what, own_row(near, side))
                tile, slot = group // SLOTS, group % SLOTS
                target = hand * len(SENT) + at
                to_tile, to_slot = target // SLOTS, target % SLOTS
                value = turn(mine_ref[hand, :, LANES * tile : LANES * (tile + 1)], SIDE * (to_slot - slot))
                held = tiles[to_tile]
                tiles[to_tile] = value if held is None else jnp.where(place == to_slot, value, held)
        for tile, value in enumerate(tiles):
            out[len(rows), :, LANES * tile : LANES * (tile + 1)] = value


def beside(left, left_slot, right, right_slot):
    lane = lanes_of(left.shape)
    return jnp.where(
        lane < LANES // 2, turn(right, -SIDE * right_slot), turn(left, LANES - SIDE * (left_slot + 1))
    )


def mine_beside(mine_ref, group):
    tile, slot = group // SLOTS, group % SLOTS
    at = slice(LANES * tile, LANES * (tile + 1))
    return beside(mine_ref[0, :, at], slot, mine_ref[1, :, at], slot)


def sent_beside(near_ref, what, near):
    row = len(rows_of(CHUNK_2))
    index = SENT.index((what, near))
    tiles = []
    for target in (index, len(SENT) + index):
        tile = target // SLOTS
        tiles += [near_ref[row, :, LANES * tile : LANES * (tile + 1)], target % SLOTS]
    return beside(*tiles)


def far_kernel(
    cur_ref, stiff_ref, edge_ref, mine_ref, low1, high1, up_ref, down_ref, own_ref, own_s_ref, rim_ref
):
    del low1, high1
    fill_message(CHUNK_3, cur_ref, stiff_ref, up_ref, down_ref)
    for field in range(4):
        for row in range(ROWS):
            own_ref[field, row, :, :COLS] = cur_ref[field, row]
            own_ref[field, row, :, COLS:] = mine_beside(mine_ref, field * ROWS + row)
        rim_ref[field, :, :COLS] = edge_ref[field]
        rim_ref[field, :, COLS:] = mine_beside(mine_ref, EDGE_GROUP + field)
    for row in range(ROWS):
        own_s_ref[row, :, :COLS] = stiff_ref[row]
        own_s_ref[row, :, COLS:] = mine_beside(mine_ref, S_GROUP + row)


def received(refs, near_ref, what, near):
    for chunk, ref in zip((CHUNK_1, CHUNK_2, CHUNK_3), refs):
        rows = rows_of(chunk)
        if (what, near) in rows:
            main = ref[rows.index((what, near))]
    return jnp.concatenate([main, sent_beside(near_ref, what, near)], axis=1)


class Place:
    def __init__(self, counts, off_ref, levels):
        self.nx, self.ny = counts
        self.gx, self.gy = lax.axis_index("gx"), lax.axis_index("gy")
        self.off_x, self.off_y = off_ref[0], off_ref[1]
        j = column_of_lane(lanes_of((levels, WIDE))) + (self.gy * COLS - RATIO * self.off_y)
        self.held = is_edge(j, self.ny).astype(jnp.int32)

    def keep(self, row):
        i = self.gx * ROWS + row - RATIO * self.off_x
        return (self.held + is_edge(i, self.nx).astype(jnp.int32)) > 0

    def field_row(self, own, low, high, rim_ref, field, row):
        if 0 <= row < ROWS:
            return own[field, row]
        if row < 0:
            value = received(low, low[1], field, -1 - row)
            outer = self.gx == 0
        else:
            value = received(high, high[1], field, row - ROWS)
            outer = self.gx == self.nx // ROWS - 1
        return jnp.where(outer, rim_ref[field], value)


def wind_x(keep, wind, p_low, p_high):
    return jnp.where(keep, wind, wind - GRAD * (p_high - p_low))


def column_step(keep, table, pressure, u_low, u_high, wind, lift, stiffness):
    levels = pressure.shape[0]
    wind = jnp.where(keep, wind, wind - GRAD * (next_col(pressure) - prev_col(pressure)))
    divergence = (u_high - u_low) + (next_col(wind) - prev_col(wind))
    right_side = pressure - DIV * divergence - COUPLE * (level_up(lift) - level_down(lift))
    both = split_dot(table, right_side)
    first, around = both[:levels], both[levels:]
    leftover = right_side - ((1.0 + stiffness) * first - 0.25 * around)
    solved = first + split_dot(table[:levels], leftover)
    p_next = jnp.where(keep, pressure, solved)
    w_next = jnp.where(keep, lift, lift - LIFT * (level_up(p_next) - p_next))
    return wind, w_next, p_next


def own_kernel(
    counts, off_ref, own_ref, own_s_ref, rim_ref, low1, low2, high1, high2, table_ref,
    u_out, v_out, w_out, p_out, up_ref, down_ref,
    p_win, s_win,
):
    levels = own_ref.shape[2]
    at = Place(counts, off_ref, levels)
    low, high = (low1, low2, None), (high1, high2, None)
    deep = NEAR[PR]
    for row in range(-deep, ROWS + deep):
        p_win[row + deep] = at.field_row(own_ref, low, high, rim_ref, PR, row)
    for near in range(KEEP):
        s_win[KEEP - 1 - near] = received(low, low2, "s", near)
        s_win[KEEP + ROWS + near] = received(high, high2, "s", near)
    for row in range(ROWS):
        s_win[KEEP + row] = own_s_ref[row]
    for row in range(-1, ROWS + 1):
        wind = at.field_row(own_ref, low, high, rim_ref, U, row)
        u_out[row + 1] = wind_x(at.keep(row), wind, p_win[row + deep - 1], p_win[row + deep + 1])
    move_y = lax.rem(RATIO * at.off_y + WIDE, WIDE)
    table = table_ref[...]

    def body(row, carry):
        stiffness = pltpu.roll(s_win[row + KEEP - RATIO * at.off_x], move_y, 1)
        v_out[row], w_out[row], p_out[row] = column_step(
            at.keep(row), table, p_win[row + deep], u_out[row], u_out[row + 2],
            own_ref[V, row], own_ref[W, row], stiffness,
        )
        return carry

    lax.fori_loop(0, ROWS, body, 0, unroll=ROWS)
    for out, first in ((up_ref, 1), (down_ref, 3)):
        beyond = None
        for n in range(2):
            value = p_out[first + n]
            for tile in range(COLS // LANES):
                out[n * (COLS // LANES) + tile] = value[:, LANES * tile : LANES * (tile + 1)]
            ext = value[:, COLS:]
            beyond = ext if n == 0 else merge_ext(beyond, ext)
        out[2 * (COLS // LANES)] = beyond


def merge_ext(first, second):
    lane = lanes_of(first.shape)
    near = jnp.where(lane < LANES // 2, turn(second, SIDE), turn(second, -SIDE))
    return jnp.where((lane < SIDE) | (lane >= LANES - SIDE), first, near)


def split_ext(merged, n):
    if n == 0:
        return merged
    lane = lanes_of(merged.shape)
    return jnp.where(lane < LANES // 2, turn(merged, -SIDE), turn(merged, SIDE))


def halo_kernel(
    counts, off_ref, own_ref, own_s_ref, rim_ref, low1, low2, low3, high1, high2, high3, table_ref,
    u_own, v_own, w_own, p_own,
    u_rim, v_rim, w_rim, p_rim, s_rim, u_out, v_out, w_out, p_out,
    p_win, s_win, s_mid,
):
    levels = own_ref.shape[2]
    at = Place(counts, off_ref, levels)
    low, high = (low1, low2, low3), (high1, high2, high3)
    table = table_ref[...]
    deep = DEEP[PR]
    for n in range(deep + 1):
        p_win[n] = at.field_row(own_ref, low, high, rim_ref, PR, n - deep)
        p_win[deep + 1 + n] = at.field_row(own_ref, low, high, rim_ref, PR, ROWS - 1 + n)
    for near in range(ROWS):
        s_win[ROWS - 1 - near] = received(low, low2, "s", near)
        s_win[2 * ROWS + near] = received(high, high2, "s", near)
        s_win[ROWS + near] = own_s_ref[near]
    move_y = lax.rem(RATIO * at.off_y + WIDE, WIDE)

    def stiffness(row):
        return pltpu.roll(s_win[row + ROWS - RATIO * at.off_x], move_y, 1)

    def p_before(row):
        return p_win[row + deep] if row <= 0 else p_win[row - ROWS + 1 + deep + 1]

    def rim_of(depth, row):
        return row + depth if row < 0 else row - ROWS + depth

    for row in (-4, -3, -2, 7, 8, 9):
        wind = at.field_row(own_ref, low, high, rim_ref, U, row)
        u_rim[rim_of(4, row)] = wind_x(at.keep(row), wind, p_before(row - 1), p_before(row + 1))

    def u_after(row):
        return u_own[row + 1] if -1 <= row <= ROWS else u_rim[rim_of(4, row)]

    outer = (-3, -2, -1, 6, 7, 8)
    for row in outer:
        n = rim_of(KEEP, row)
        stiff = stiffness(row)
        if row in (-3, -2, 7, 8):
            s_rim[(-3, -2, 7, 8).index(row)] = stiff
        else:
            s_mid[0 if row < 0 else ROWS + 1] = stiff
        v_rim[n], w_rim[n], p_rim[n] = column_step(
            at.keep(row), table, p_before(row), u_after(row - 1), u_after(row + 1),
            at.field_row(own_ref, low, high, rim_ref, V, row),
            at.field_row(own_ref, low, high, rim_ref, W, row),
            stiff,
        )
    for row in range(ROWS):
        s_mid[row + 1] = stiffness(row)

    def pick(own, rim, row):
        return own[row] if 0 <= row < ROWS else rim[rim_of(KEEP, row)]

    for row in range(-2, ROWS + 2):
        u_out[row + 2] = wind_x(
            at.keep(row), u_after(row), pick(p_own, p_rim, row - 1), pick(p_own, p_rim, row + 1)
        )
    for row in range(-1, ROWS + 1):
        v_out[row + 1], w_out[row + 1], p_out[row + 1] = column_step(
            at.keep(row), table, pick(p_own, p_rim, row), u_out[row + 1], u_out[row + 3],
            pick(v_own, v_rim, row), pick(w_own, w_rim, row), s_mid[row + 1],
        )


def last_kernel(
    counts, off_ref, u_rim, v_rim, w_rim, p_rim, s_rim, u_mid, v_mid, w_mid, p_mid,
    low_ref, high_ref, table_ref, parent_ref,
    new_ref, back_ref,
    u_win, v_win, w_win, q_win,
):
    levels = u_rim.shape[1]
    at = Place(counts, off_ref, levels)
    table = table_ref[...]
    tiles = COLS // LANES

    def sent(ref, n):
        parts = [ref[n * tiles + tile] for tile in range(tiles)] + [split_ext(ref[2 * tiles], n)]
        return jnp.concatenate(parts, axis=1)

    for row in range(ROWS + 4):
        u_win[row + 2] = u_mid[row]
    for row in range(ROWS + 2):
        v_win[row + 2] = v_mid[row]
        w_win[row + 2] = w_mid[row]
        q_win[row + 2] = p_mid[row]
    low_p = [sent(low_ref, 0), sent(low_ref, 1), p_rim[0], p_rim[1]]
    high_p = [p_rim[4], p_rim[5], sent(high_ref, 0), sent(high_ref, 1)]
    for n, row in enumerate((-4, -3)):
        u_win[n] = wind_x(at.keep(row), u_rim[n], low_p[n], low_p[n + 2])
    for n, row in enumerate((8, 9)):
        u_win[12 + n] = wind_x(at.keep(row), u_rim[6 + n], high_p[n], high_p[n + 2])
    for n, row in enumerate((-3, -2, 7, 8)):
        rim = (0, 1, 4, 5)[n]
        v_win[row + KEEP], w_win[row + KEEP], q_win[row + KEEP] = column_step(
            at.keep(row), table, p_rim[rim], u_win[row + 3], u_win[row + 5],
            v_rim[rim], w_rim[rim], s_rim[n],
        )
    windows = ((U, u_win, 4), (V, v_win, KEEP), (W, w_win, KEEP), (PR, q_win, KEEP))
    finish(at, windows, parent_ref, new_ref, back_ref)


def finish(at, windows, parent_ref, new_ref, back_ref):
    levels = parent_ref.shape[2]
    move_y = lax.rem(WIDE - RATIO * at.off_y, WIDE)
    for field, window, deep in windows:
        for row in range(ROWS):
            moved = pltpu.roll(window[row + deep + RATIO * at.off_x], move_y, 1)
            new_ref[field, row] = moved[:, :COLS]

    cells_x, cells_y = at.nx // RATIO, at.ny // RATIO
    coarse_rows, coarse_cols = ROWS // RATIO, COLS // RATIO

    def inside(index, count):
        return (index >= 1) & (index <= count - 2)

    source = column_of_lane(lax.broadcasted_iota(jnp.int32, (WIDE, coarse_cols), 0))
    apart = source - RATIO * lax.broadcasted_iota(jnp.int32, (WIDE, coarse_cols), 1)
    spread = jnp.where(
        (apart >= 0) & (apart < RATIO),
        0.5,
        jnp.where((apart >= -RATIO) & (apart < 2 * RATIO), 0.25, 0.0),
    ).astype(BF16)
    cell = lanes_of((levels, coarse_cols)) + (at.gy * coarse_cols - at.off_y)
    weight_y = (
        0.25 * inside(cell - 1, cells_y).astype(F32)
        + 0.5 * inside(cell, cells_y).astype(F32)
        + 0.25 * inside(cell + 1, cells_y).astype(F32)
    )
    centre_y = inside(cell, cells_y).astype(jnp.int32)
    for coarse in range(coarse_rows):
        a = at.gx * coarse_rows + coarse - at.off_x
        inner = [inside(a + d, cells_x).astype(F32) for d in (-1, 0, 1)]
        weights = [s * m for s, m in zip((0.25, 0.5, 0.25), inner)]
        weight_x = weights[0] + weights[1] + weights[2]
        centre = (centre_y * inside(a, cells_x).astype(jnp.int32)) > 0
        scale = jnp.where(centre, 1.0 / jnp.where(centre, 9.0 * weight_x * weight_y, 1.0), 0.0)
        for field, window, deep in windows:
            start = deep - KEEP + RATIO * coarse
            total = None
            for d in range(3):
                part = window[start + 3 * d] + window[start + 3 * d + 1] + window[start + 3 * d + 2]
                part = jnp.where(inner[d] > 0, part * weights[d], 0.0)
                total = part if total is None else total + part
            total = jnp.where(at.held > 0, 0.0, total)
            high = total.astype(BF16)
            low = (total - high.astype(F32)).astype(BF16)
            summed = jnp.dot(high, spread, preferred_element_type=F32) + jnp.dot(
                low, spread, preferred_element_type=F32
            )
            back_ref[field, :, coarse, :] = jnp.where(centre, summed * scale, parent_ref[field, coarse])


def call(body, ins, outs, scratch=(), spaces=None):
    def space(x):
        if x.dtype == jnp.int32:
            return pltpu.SMEM
        return pltpu.VMEM

    spaces = spaces or [space(x) for x in ins]
    return pl.pallas_call(
        body,
        out_shape=[jax.ShapeDtypeStruct(shape, F32) for shape in outs],
        in_specs=[pl.BlockSpec(memory_space=s) for s in spaces],
        out_specs=[pl.BlockSpec(memory_space=pltpu.VMEM) for _ in outs],
        scratch_shapes=[s if not isinstance(s, tuple) else pltpu.VMEM(s, F32) for s in scratch],
        compiler_params=pltpu.CompilerParams(vmem_limit_bytes=VMEM_BYTES),
    )(*ins)


def exchange(up, down, axis):
    count = lax.axis_size(axis)
    forward = [(i, i + 1) for i in range(count - 1)]
    low = lax.ppermute(up, axis, forward)
    high = lax.ppermute(down, axis, [(target, source) for source, target in forward])
    return low, high


def per_device(nest_state, stiffness, parent, inverse_table, offsets):
    levels = nest_state.shape[1]
    nx = nest_state.shape[2] * lax.axis_size("gx")
    ny = nest_state.shape[3] * lax.axis_size("gy")
    counts = (nx, ny)
    nest = jnp.transpose(nest_state, (0, 2, 1, 3))
    stiff_in = jnp.transpose(stiffness, (1, 0, 2))

    nothing = jnp.zeros_like(inverse_table[:1])
    shifted = jnp.concatenate([inverse_table[1:], nothing], 0)
    shifted += jnp.concatenate([nothing, inverse_table[:-1]], 0)
    stack = jnp.concatenate([inverse_table, shifted], 0)
    top = lax.reduce_precision(stack, 8, 7)
    table = jnp.concatenate([top, top, stack - top], 1).astype(BF16)

    def rows(count, width=WIDE):
        return (count, levels, width)

    first, near, far = (len(rows_of(chunk)) for chunk in (CHUNK_1, CHUNK_2, CHUNK_3))
    cur, stiff, coarse, to_left, to_right, edge, up, down = call(
        functools.partial(prepare_kernel, counts),
        [pltpu.with_memory_space_constraint(x, pltpu.HBM) for x in (offsets, nest, stiff_in, parent)],
        [nest.shape, stiff_in.shape, (4, ROWS // RATIO, levels, LANES), (levels, PACK), (levels, PACK)]
        + [(4, levels, COLS), rows(first, COLS), rows(first, COLS)],
        [nest.shape, parent.shape, pltpu.SemaphoreType.DMA((6,))],
        [pltpu.SMEM, pltpu.HBM, pltpu.HBM, pltpu.HBM],
    )
    low1, high1 = exchange(up, down, "gx")
    from_left, from_right = exchange(to_right, to_left, "gy")
    mine, up, down = call(
        functools.partial(near_kernel, lax.axis_size("gy") - 1),
        (cur, stiff, coarse, from_left, from_right),
        [(2, levels, PACK), rows(near + 1, COLS), rows(near + 1, COLS)],
    )
    low2, high2 = exchange(up, down, "gx")
    up, down, own, own_s, rim = call(
        far_kernel,
        (cur, stiff, edge, mine, low1, high1),
        [rows(far, COLS), rows(far, COLS), (4, ROWS, levels, WIDE), rows(ROWS), rows(4)],
    )
    low3, high3 = exchange(up, down, "gx")
    message = (2 * (COLS // LANES) + 1, levels, LANES)
    u1, v1, w1, p1, up, down = call(
        functools.partial(own_kernel, counts),
        (offsets, own, own_s, rim, low1, low2, high1, high2, table),
        [rows(ROWS + 2), rows(ROWS), rows(ROWS), rows(ROWS), message, message],
        [rows(ROWS + 4), rows(2 * ROWS)],
    )
    low4, high4 = exchange(up, down, "gx")
    outer = call(
        functools.partial(halo_kernel, counts),
        (offsets, own, own_s, rim, low1, low2, low3, high1, high2, high3, table, u1, v1, w1, p1),
        [rows(8), rows(6), rows(6), rows(6), rows(4), rows(ROWS + 4), rows(ROWS + 2), rows(ROWS + 2), rows(ROWS + 2)],
        [rows(12), rows(3 * ROWS), rows(ROWS + 2)],
    )
    new, back = call(
        functools.partial(last_kernel, counts),
        (offsets, *outer, low4, high4, table, coarse),
        [nest.shape, parent.shape],
        [rows(ROWS + 8), rows(ROWS + 6), rows(ROWS + 6), rows(ROWS + 6)],
    )
    return jnp.transpose(new, (0, 2, 1, 3)), back


def solution(mesh):
    return jax.shard_map(
        per_device,
        mesh=mesh,
        in_specs=(
            P(None, None, "gx", "gy"),
            P(None, "gx", "gy"),
            P(None, None, "gx", "gy"),
            P(),
            P(),
        ),
        out_specs=(P(None, None, "gx", "gy"), P(None, None, "gx", "gy")),
        check_vma=False,
    )
```

```python
import functools

import jax
import jax.numpy as jnp
from jax import lax
from jax.experimental import pallas as pl
from jax.experimental.pallas import tpu as pltpu
from jax.sharding import PartitionSpec as P

RATIO = 3
GRAD = 0.25
DIV = 0.25
COUPLE = 0.25
LIFT = 0.5
F32 = jnp.float32
BF16 = jnp.bfloat16
VMEM_BYTES = 24 * 1024 * 1024

ROWS = 6
COLS = 384
LANES = 128
WIDE = COLS + LANES
SIDE = 8
SLOTS = LANES // SIDE
U, V, W, PR = 0, 1, 2, 3
NEAR = {PR: 2}
KEEP = 3
S_GROUP = 4 * ROWS
EDGE_GROUP = S_GROUP + ROWS
GROUPS = EDGE_GROUP + 4
PACK = -(-GROUPS // SLOTS) * LANES
CHUNK_1 = ((V, 0, 3), (W, 0, 3), ("s", 0, 3))
CHUNK_2 = ((PR, 0, 2), (U, 0, 1), ("s", 3, 1))
CHUNK_3 = ((PR, 2, 1), (U, 1, 3), ("s", 4, 2))
SENT = [(PR, n) for n in range(5)] + [(U, n) for n in range(4)] + [(V, n) for n in range(3)]
SENT += [(W, n) for n in range(3)] + [("s", n) for n in range(6)]


def rows_of(chunk):
    return [(what, first + n) for what, first, count in chunk for n in range(count)]


def lanes_of(shape):
    return lax.broadcasted_iota(jnp.int32, shape, len(shape) - 1)


def column_of_lane(lane):
    return jnp.where(lane < COLS + LANES // 2, lane, lane - WIDE)


def is_edge(index, count):
    return (index < RATIO) | (index >= count - RATIO)


def expand_all(coarse):
    lane = lanes_of(coarse.shape)
    parts = [
        jnp.take_along_axis(coarse, (lane + first) // RATIO, axis=1) for first in range(0, COLS, LANES)
    ]
    return jnp.concatenate(parts, axis=1)


def turn(x, amount):
    amount = amount % x.shape[1]
    return x if amount == 0 else pltpu.roll(x, amount, 1)


def next_col(x):
    return pltpu.roll(x, x.shape[1] - 1, 1)


def prev_col(x):
    return pltpu.roll(x, 1, 1)


def level_up(x):
    levels = x.shape[0]
    level = lax.broadcasted_iota(jnp.int32, x.shape, 0)
    return jnp.where(level < levels - 1, pltpu.roll(x, levels - 1, 0), 0.0)


def level_down(x):
    level = lax.broadcasted_iota(jnp.int32, x.shape, 0)
    return jnp.where(level > 0, pltpu.roll(x, 1, 0), 0.0)


def split_dot(table, x):
    high = x.astype(BF16)
    low = (x - high.astype(F32)).astype(BF16)
    stacked = jnp.concatenate([high, low, high], axis=0)
    return jnp.dot(table, stacked, preferred_element_type=F32)


def own_row(near, side):
    return ROWS - 1 - near if side == 0 else near


def is_odd(index):
    return lax.rem(index, 2) == 1


def by_pair(odd, up, down):
    return jnp.where(odd, up, down), jnp.where(odd, down, up)


class Received:
    def __init__(self, in_first, first, second):
        self.in_first, self.first, self.second = in_first, first, second

    def __getitem__(self, at):
        return jnp.where(self.in_first, self.first[at], self.second[at])


def low_high(odd, first, second):
    if first is None:
        return None, None
    return Received(jnp.logical_not(odd), first, second), Received(odd, first, second)


def prepare_kernel(
    counts, off_ref, nest_ref, stiff_hbm, parent_hbm,
    cur_ref, stiff_ref, parent_ref, left_ref, right_ref, edge_ref, up_ref, down_ref,
    nest_win, parent_win, sems,
):
    nx, ny = counts
    copies = [pltpu.make_async_copy(parent_hbm, parent_win, sems.at[4])]
    copies += [pltpu.make_async_copy(nest_ref.at[f], nest_win.at[f], sems.at[f]) for f in (V, W, PR, U)]
    copies.append(pltpu.make_async_copy(stiff_hbm, stiff_ref, sems.at[5]))
    for copy in copies:
        copy.start()
    gx, gy = lax.axis_index("gx"), lax.axis_index("gy")
    off_x, off_y = off_ref[0], off_ref[1]
    levels = nest_win.shape[2]
    col = lanes_of((levels, COLS)) + (gy * COLS - RATIO * off_y)
    edge_col = is_edge(col, ny)
    place = lanes_of((levels, LANES)) // SIDE
    packs = [[None, None] for _ in range(PACK // LANES)]

    def pack(row, group):
        tile, slot = group // SLOTS, group % SLOTS
        sides = (
            turn(row[:, :LANES], SIDE * slot),
            turn(row[:, COLS - LANES :], SIDE * (slot + 1) - LANES),
        )
        for side, value in enumerate(sides):
            held = packs[tile][side]
            packs[tile][side] = value if held is None else jnp.where(place == slot, value, held)

    copies[0].wait()
    rims = []
    for at, field in enumerate((V, W, PR, U)):
        bounds = []
        for coarse in range(ROWS // RATIO):
            value = parent_win[field, :, coarse, :]
            parent_ref[field, coarse] = value
            bounds.append(expand_all(value))
        copies[1 + at].wait()
        for row in range(ROWS):
            i = gx * ROWS + row - RATIO * off_x
            held = is_edge(i, nx).astype(jnp.int32)
            value = jnp.where(edge_col | (held > 0), bounds[row // RATIO], nest_win[field, row])
            cur_ref[field, row] = value
            pack(value, field * ROWS + row)
        rim = jnp.where(gx == 0, bounds[0], bounds[-1])
        edge_ref[field] = rim
        pack(rim, EDGE_GROUP + field)
    copies[5].wait()
    for row in range(ROWS):
        pack(stiff_ref[row], S_GROUP + row)
    for tile, (left, right) in enumerate(packs):
        at = slice(LANES * tile, LANES * (tile + 1))
        left_ref[:, at], right_ref[:, at] = by_pair(is_odd(gy), right, left)
    fill_message(CHUNK_1, cur_ref, stiff_ref, up_ref, down_ref)


def fill_message(chunk, cur_ref, stiff_ref, first_ref, second_ref):
    odd = is_odd(lax.axis_index("gx"))
    for at, (what, near) in enumerate(rows_of(chunk)):
        rows = by_pair(odd, own_row(near, 0), own_row(near, 1))
        for row, out in zip(rows, (first_ref, second_ref)):
            out[at] = stiff_ref[row] if what == "s" else cur_ref[what, row]


def group_of(what, row):
    return S_GROUP + row if what == "s" else what * ROWS + row


def near_kernel(last_y, cur_ref, stiff_ref, parent_ref, left_ref, right_ref, mine_ref, up_ref, down_ref):
    gx, gy = lax.axis_index("gx"), lax.axis_index("gy")
    levels = left_ref.shape[0]
    lane = lanes_of((levels, LANES))
    place = lane // SIDE
    from_left, from_right = low_high(is_odd(gy), left_ref, right_ref)
    mine_ref[0] = from_left[...]
    mine_ref[1] = from_right[...]

    def fill(side, cell):
        for tile in range(PACK // LANES):
            at = slice(LANES * tile, LANES * (tile + 1))
            out = mine_ref[side, :, at]
            for slot in range(SLOTS):
                group = tile * SLOTS + slot
                if group < S_GROUP:
                    value = parent_ref[group // ROWS, (group % ROWS) // RATIO, :, cell : cell + 1]
                elif EDGE_GROUP <= group < GROUPS:
                    field = group - EDGE_GROUP
                    value = jnp.where(
                        gx == 0,
                        parent_ref[field, 0, :, cell : cell + 1],
                        parent_ref[field, ROWS // RATIO - 1, :, cell : cell + 1],
                    )
                else:
                    continue
                out = jnp.where(place == slot, value, out)
            mine_ref[side, :, at] = out

    @pl.when(gy == 0)
    def _():
        fill(0, 0)

    @pl.when(gy == last_y)
    def _():
        fill(1, COLS // RATIO - 1)

    rows = rows_of(CHUNK_2)
    fill_message(CHUNK_2, cur_ref, stiff_ref, up_ref, down_ref)
    tight = []
    for side in range(2):
        tiles = [None] * (COLS // LANES)
        for hand in range(2):
            for at, (what, near) in enumerate(SENT):
                group = group_of(what, own_row(near, side))
                tile, slot = group // SLOTS, group % SLOTS
                target = hand * len(SENT) + at
                to_tile, to_slot = target // SLOTS, target % SLOTS
                value = turn(mine_ref[hand, :, LANES * tile : LANES * (tile + 1)], SIDE * (to_slot - slot))
                held = tiles[to_tile]
                tiles[to_tile] = value if held is None else jnp.where(place == to_slot, value, held)
        tight.append(jnp.concatenate(tiles, axis=1))
    up_ref[len(rows)], down_ref[len(rows)] = by_pair(is_odd(gx), *tight)


def beside(left, left_slot, right, right_slot):
    lane = lanes_of(left.shape)
    return jnp.where(
        lane < LANES // 2, turn(right, -SIDE * right_slot), turn(left, LANES - SIDE * (left_slot + 1))
    )


def mine_beside(mine_ref, group):
    tile, slot = group // SLOTS, group % SLOTS
    at = slice(LANES * tile, LANES * (tile + 1))
    return beside(mine_ref[0, :, at], slot, mine_ref[1, :, at], slot)


def sent_beside(near_ref, what, near):
    row = len(rows_of(CHUNK_2))
    index = SENT.index((what, near))
    tiles = []
    for target in (index, len(SENT) + index):
        tile = target // SLOTS
        tiles += [near_ref[row, :, LANES * tile : LANES * (tile + 1)], target % SLOTS]
    return beside(*tiles)


def far_kernel(
    counts, off_ref, cur_ref, stiff_ref, edge_ref, mine_ref, low1, high1, up_ref, down_ref, own_ref, own_s_ref, rim_ref
):
    del low1, high1
    at = Place(counts, off_ref, stiff_ref.shape[1])
    fill_message(CHUNK_3, cur_ref, stiff_ref, up_ref, down_ref)
    for n, (what, near) in enumerate(rows_of(CHUNK_3)):
        if what == U:
            rows = by_pair(is_odd(at.gx), own_row(near, 0), own_row(near, 1))
            for row, out in zip(rows, (up_ref, down_ref)):
                keep = at.keep(row)[:, :COLS]
                out[n] = wind_x(keep, cur_ref[U, row], cur_ref[PR, row - 1], cur_ref[PR, row + 1])
    for field in range(4):
        for row in range(ROWS):
            own_ref[field, row, :, :COLS] = cur_ref[field, row]
            own_ref[field, row, :, COLS:] = mine_beside(mine_ref, field * ROWS + row)
        rim_ref[field, :, :COLS] = edge_ref[field]
        rim_ref[field, :, COLS:] = mine_beside(mine_ref, EDGE_GROUP + field)
    for row in range(ROWS):
        own_s_ref[row, :, :COLS] = stiff_ref[row]
        own_s_ref[row, :, COLS:] = mine_beside(mine_ref, S_GROUP + row)


def received(refs, near_ref, what, near):
    for chunk, ref in zip((CHUNK_1, CHUNK_2, CHUNK_3), refs):
        rows = rows_of(chunk)
        if (what, near) in rows:
            main = ref[rows.index((what, near))]
    return jnp.concatenate([main, sent_beside(near_ref, what, near)], axis=1)


class Place:
    def __init__(self, counts, off_ref, levels):
        self.nx, self.ny = counts
        self.gx, self.gy = lax.axis_index("gx"), lax.axis_index("gy")
        self.last_x = self.nx // ROWS - 1
        self.off_x, self.off_y = off_ref[0], off_ref[1]
        j = column_of_lane(lanes_of((levels, WIDE))) + (self.gy * COLS - RATIO * self.off_y)
        self.held = is_edge(j, self.ny).astype(jnp.int32)

    def neighbours(self, *swaps):
        return zip(*[low_high(is_odd(self.gx), first, second) for first, second in swaps])

    def keep(self, row):
        i = self.gx * ROWS + row - RATIO * self.off_x
        return (self.held + is_edge(i, self.nx).astype(jnp.int32)) > 0

    def field_row(self, own, low, high, rim_ref, field, row):
        if 0 <= row < ROWS:
            return own[field, row]
        if row < 0:
            value = received(low, low[1], field, -1 - row)
            outer = self.gx == 0
        else:
            value = received(high, high[1], field, row - ROWS)
            outer = self.gx == self.last_x
        return jnp.where(outer, rim_ref[field], value)


def wind_x(keep, wind, p_low, p_high):
    return jnp.where(keep, wind, wind - GRAD * (p_high - p_low))


def column_step(keep, table, pressure, u_low, u_high, wind, lift, stiffness):
    levels = pressure.shape[0]
    wind = jnp.where(keep, wind, wind - GRAD * (next_col(pressure) - prev_col(pressure)))
    divergence = (u_high - u_low) + (next_col(wind) - prev_col(wind))
    right_side = pressure - DIV * divergence - COUPLE * (level_up(lift) - level_down(lift))
    both = split_dot(table, right_side)
    first, around = both[:levels], both[levels:]
    leftover = right_side - ((1.0 + stiffness) * first - 0.25 * around)
    solved = first + split_dot(table[:levels], leftover)
    p_next = jnp.where(keep, pressure, solved)
    w_next = jnp.where(keep, lift, lift - LIFT * (level_up(p_next) - p_next))
    return wind, w_next, p_next


def own_kernel(
    counts, off_ref, own_ref, own_s_ref, rim_ref, low1, low2, high1, high2, table_ref,
    u_out, v_out, w_out, p_out, up_ref, down_ref,
    p_win, s_win,
):
    levels = own_ref.shape[2]
    at = Place(counts, off_ref, levels)
    low, high = at.neighbours((low1, high1), (low2, high2), (None, None))
    deep = NEAR[PR]
    for row in range(-deep, ROWS + deep):
        p_win[row + deep] = at.field_row(own_ref, low, high, rim_ref, PR, row)
    for near in range(KEEP):
        s_win[KEEP - 1 - near] = received(low, low[1], "s", near)
        s_win[KEEP + ROWS + near] = received(high, high[1], "s", near)
    for row in range(ROWS):
        s_win[KEEP + row] = own_s_ref[row]
    for row in range(-1, ROWS + 1):
        wind = at.field_row(own_ref, low, high, rim_ref, U, row)
        u_out[row + 1] = wind_x(at.keep(row), wind, p_win[row + deep - 1], p_win[row + deep + 1])
    move_y = lax.rem(RATIO * at.off_y + WIDE, WIDE)
    table = table_ref[...]

    def body(row, carry):
        stiffness = pltpu.roll(s_win[row + KEEP - RATIO * at.off_x], move_y, 1)
        v_out[row], w_out[row], p_out[row] = column_step(
            at.keep(row), table, p_win[row + deep], u_out[row], u_out[row + 2],
            own_ref[V, row], own_ref[W, row], stiffness,
        )
        return carry

    lax.fori_loop(0, ROWS, body, 0, unroll=ROWS)
    starts = by_pair(is_odd(at.gx), 1, 3)
    for out, first in zip((up_ref, down_ref), starts):
        beyond = None
        for n in range(2):
            value = p_out[first + n]
            for tile in range(COLS // LANES):
                out[n * (COLS // LANES) + tile] = value[:, LANES * tile : LANES * (tile + 1)]
            ext = value[:, COLS:]
            beyond = ext if n == 0 else merge_ext(beyond, ext)
        out[2 * (COLS // LANES)] = beyond


def merge_ext(first, second):
    lane = lanes_of(first.shape)
    near = jnp.where(lane < LANES // 2, turn(second, SIDE), turn(second, -SIDE))
    return jnp.where((lane < SIDE) | (lane >= LANES - SIDE), first, near)


def split_ext(merged, n):
    if n == 0:
        return merged
    lane = lanes_of(merged.shape)
    return jnp.where(lane < LANES // 2, turn(merged, -SIDE), turn(merged, SIDE))


def halo_kernel(
    counts, off_ref, own_ref, own_s_ref, rim_ref, low1, low2, low3, high1, high2, high3, table_ref,
    u_own, v_own, w_own, p_own,
    u_rim, v_rim, w_rim, p_rim, s_rim, u_out, v_out, w_out, p_out,
    p_win, s_win, s_mid,
):
    levels = own_ref.shape[2]
    at = Place(counts, off_ref, levels)
    low, high = at.neighbours((low1, high1), (low2, high2), (low3, high3))
    table = table_ref[...]
    deep = KEEP
    for n in range(deep + 1):
        p_win[n] = at.field_row(own_ref, low, high, rim_ref, PR, n - deep)
        p_win[deep + 1 + n] = at.field_row(own_ref, low, high, rim_ref, PR, ROWS - 1 + n)
    for near in range(ROWS):
        s_win[ROWS - 1 - near] = received(low, low[1], "s", near)
        s_win[2 * ROWS + near] = received(high, high[1], "s", near)
        s_win[ROWS + near] = own_s_ref[near]
    move_y = lax.rem(RATIO * at.off_y + WIDE, WIDE)

    def stiffness(row):
        return pltpu.roll(s_win[row + ROWS - RATIO * at.off_x], move_y, 1)

    def p_before(row):
        return p_win[row + deep] if row <= 0 else p_win[row - ROWS + 1 + deep + 1]

    def rim_of(depth, row):
        return row + depth if row < 0 else row - ROWS + depth

    for row in (-4, -3, -2, 7, 8, 9):
        near = -1 - row if row < 0 else row - ROWS
        near_ref, outer = (low[1], at.gx == 0) if row < 0 else (high[1], at.gx == at.last_x)
        outward, inward = (sent_beside(near_ref, PR, near + by) for by in (1, -1))
        p_low, p_high = (outward, inward) if row < 0 else (inward, outward)
        main = received(low if row < 0 else high, near_ref, U, near)
        ext = wind_x(at.keep(row)[:, COLS:], main[:, COLS:], p_low, p_high)
        value = jnp.concatenate([main[:, :COLS], ext], axis=1)
        u_rim[rim_of(4, row)] = jnp.where(outer, rim_ref[U], value)

    def u_after(row):
        return u_own[row + 1] if -1 <= row <= ROWS else u_rim[rim_of(4, row)]

    outer = (-3, -2, -1, 6, 7, 8)
    for row in outer:
        n = rim_of(KEEP, row)
        stiff = stiffness(row)
        if row in (-3, -2, 7, 8):
            s_rim[(-3, -2, 7, 8).index(row)] = stiff
        else:
            s_mid[0 if row < 0 else ROWS + 1] = stiff
        v_rim[n], w_rim[n], p_rim[n] = column_step(
            at.keep(row), table, p_before(row), u_after(row - 1), u_after(row + 1),
            at.field_row(own_ref, low, high, rim_ref, V, row),
            at.field_row(own_ref, low, high, rim_ref, W, row),
            stiff,
        )
    for row in range(ROWS):
        s_mid[row + 1] = stiffness(row)

    def pick(own, rim, row):
        return own[row] if 0 <= row < ROWS else rim[rim_of(KEEP, row)]

    for row in range(-2, ROWS + 2):
        u_out[row + 2] = wind_x(
            at.keep(row), u_after(row), pick(p_own, p_rim, row - 1), pick(p_own, p_rim, row + 1)
        )
    for row in range(-1, ROWS + 1):
        v_out[row + 1], w_out[row + 1], p_out[row + 1] = column_step(
            at.keep(row), table, pick(p_own, p_rim, row), u_out[row + 1], u_out[row + 3],
            pick(v_own, v_rim, row), pick(w_own, w_rim, row), s_mid[row + 1],
        )


def last_kernel(
    counts, off_ref, u_rim, v_rim, w_rim, p_rim, s_rim, u_mid, v_mid, w_mid, p_mid,
    low_ref, high_ref, table_ref, parent_ref,
    new_ref, back_ref,
    u_win, v_win, w_win, q_win,
):
    levels = u_rim.shape[1]
    at = Place(counts, off_ref, levels)
    table = table_ref[...]
    tiles = COLS // LANES

    def sent(ref, n):
        parts = [ref[n * tiles + tile] for tile in range(tiles)] + [split_ext(ref[2 * tiles], n)]
        return jnp.concatenate(parts, axis=1)

    low_ref, high_ref = low_high(is_odd(at.gx), low_ref, high_ref)
    for row in range(ROWS + 4):
        u_win[row + 2] = u_mid[row]
    for row in range(ROWS + 2):
        v_win[row + 2] = v_mid[row]
        w_win[row + 2] = w_mid[row]
        q_win[row + 2] = p_mid[row]
    low_p = [sent(low_ref, 0), sent(low_ref, 1), p_rim[0], p_rim[1]]
    high_p = [p_rim[4], p_rim[5], sent(high_ref, 0), sent(high_ref, 1)]
    for n, row in enumerate((-4, -3)):
        u_win[n] = wind_x(at.keep(row), u_rim[n], low_p[n], low_p[n + 2])
    for n, row in enumerate((8, 9)):
        u_win[12 + n] = wind_x(at.keep(row), u_rim[6 + n], high_p[n], high_p[n + 2])
    for n, row in enumerate((-3, -2, 7, 8)):
        rim = (0, 1, 4, 5)[n]
        v_win[row + KEEP], w_win[row + KEEP], q_win[row + KEEP] = column_step(
            at.keep(row), table, p_rim[rim], u_win[row + 3], u_win[row + 5],
            v_rim[rim], w_rim[rim], s_rim[n],
        )
    windows = ((U, u_win, 4), (V, v_win, KEEP), (W, w_win, KEEP), (PR, q_win, KEEP))
    finish(at, windows, parent_ref, new_ref, back_ref)


def finish(at, windows, parent_ref, new_ref, back_ref):
    levels = parent_ref.shape[2]
    move_y = lax.rem(WIDE - RATIO * at.off_y, WIDE)
    for field, window, deep in windows:
        for row in range(ROWS):
            moved = pltpu.roll(window[row + deep + RATIO * at.off_x], move_y, 1)
            new_ref[field, row] = moved[:, :COLS]

    cells_x, cells_y = at.nx // RATIO, at.ny // RATIO
    coarse_rows, coarse_cols = ROWS // RATIO, COLS // RATIO

    def inside(index, count):
        return (index >= 1) & (index <= count - 2)

    source = column_of_lane(lax.broadcasted_iota(jnp.int32, (WIDE, coarse_cols), 0))
    apart = source - RATIO * lax.broadcasted_iota(jnp.int32, (WIDE, coarse_cols), 1)
    spread = jnp.where(
        (apart >= 0) & (apart < RATIO),
        0.5,
        jnp.where((apart >= -RATIO) & (apart < 2 * RATIO), 0.25, 0.0),
    ).astype(BF16)
    cell = lanes_of((levels, coarse_cols)) + (at.gy * coarse_cols - at.off_y)
    weight_y = (
        0.25 * inside(cell - 1, cells_y).astype(F32)
        + 0.5 * inside(cell, cells_y).astype(F32)
        + 0.25 * inside(cell + 1, cells_y).astype(F32)
    )
    centre_y = inside(cell, cells_y).astype(jnp.int32)
    for coarse in range(coarse_rows):
        a = at.gx * coarse_rows + coarse - at.off_x
        inner = [inside(a + d, cells_x).astype(F32) for d in (-1, 0, 1)]
        weights = [s * m for s, m in zip((0.25, 0.5, 0.25), inner)]
        weight_x = weights[0] + weights[1] + weights[2]
        centre = (centre_y * inside(a, cells_x).astype(jnp.int32)) > 0
        scale = jnp.where(centre, 1.0 / jnp.where(centre, 9.0 * weight_x * weight_y, 1.0), 0.0)
        for field, window, deep in windows:
            start = deep - KEEP + RATIO * coarse
            total = None
            for d in range(3):
                part = window[start + 3 * d] + window[start + 3 * d + 1] + window[start + 3 * d + 2]
                part = jnp.where(inner[d] > 0, part * weights[d], 0.0)
                total = part if total is None else total + part
            total = jnp.where(at.held > 0, 0.0, total)
            high = total.astype(BF16)
            low = (total - high.astype(F32)).astype(BF16)
            summed = jnp.dot(high, spread, preferred_element_type=F32) + jnp.dot(
                low, spread, preferred_element_type=F32
            )
            back_ref[field, :, coarse, :] = jnp.where(centre, summed * scale, parent_ref[field, coarse])


def call(body, ins, outs, scratch=(), spaces=None):
    def space(x):
        if x.dtype == jnp.int32:
            return pltpu.SMEM
        return pltpu.VMEM

    spaces = spaces or [space(x) for x in ins]
    return pl.pallas_call(
        body,
        out_shape=[jax.ShapeDtypeStruct(shape, F32) for shape in outs],
        in_specs=[pl.BlockSpec(memory_space=s) for s in spaces],
        out_specs=[pl.BlockSpec(memory_space=pltpu.VMEM) for _ in outs],
        scratch_shapes=[s if not isinstance(s, tuple) else pltpu.VMEM(s, F32) for s in scratch],
        compiler_params=pltpu.CompilerParams(vmem_limit_bytes=VMEM_BYTES),
    )(*ins)


def exchange(first, second, axis):
    def swap(x, start):
        pairs = [(i, i + 1) for i in range(start, lax.axis_size(axis) - 1, 2)]
        return lax.ppermute(x, axis, pairs + [(high, low) for low, high in pairs])

    return swap(first, 1), swap(second, 0)


def per_device(nest_state, stiffness, parent, inverse_table, offsets):
    levels = nest_state.shape[1]
    nx = nest_state.shape[2] * lax.axis_size("gx")
    ny = nest_state.shape[3] * lax.axis_size("gy")
    counts = (nx, ny)
    nest = jnp.transpose(nest_state, (0, 2, 1, 3))
    stiff_in = jnp.transpose(stiffness, (1, 0, 2))

    nothing = jnp.zeros_like(inverse_table[:1])
    shifted = jnp.concatenate([inverse_table[1:], nothing], 0)
    shifted += jnp.concatenate([nothing, inverse_table[:-1]], 0)
    stack = jnp.concatenate([inverse_table, shifted], 0)
    top = lax.reduce_precision(stack, 8, 7)
    table = jnp.concatenate([top, top, stack - top], 1).astype(BF16)

    def rows(count, width=WIDE):
        return (count, levels, width)

    first, near, far = (len(rows_of(chunk)) for chunk in (CHUNK_1, CHUNK_2, CHUNK_3))
    cur, stiff, coarse, to_left, to_right, edge, up, down = call(
        functools.partial(prepare_kernel, counts),
        [pltpu.with_memory_space_constraint(x, pltpu.HBM) for x in (offsets, nest, stiff_in, parent)],
        [nest.shape, stiff_in.shape, (4, ROWS // RATIO, levels, LANES), (levels, PACK), (levels, PACK)]
        + [(4, levels, COLS), rows(first, COLS), rows(first, COLS)],
        [nest.shape, parent.shape, pltpu.SemaphoreType.DMA((6,))],
        [pltpu.SMEM, pltpu.HBM, pltpu.HBM, pltpu.HBM],
    )
    low1, high1 = exchange(up, down, "gx")
    from_left, from_right = exchange(to_left, to_right, "gy")
    mine, up, down = call(
        functools.partial(near_kernel, lax.axis_size("gy") - 1),
        (cur, stiff, coarse, from_left, from_right),
        [(2, levels, PACK), rows(near + 1, COLS), rows(near + 1, COLS)],
    )
    low2, high2 = exchange(up, down, "gx")
    up, down, own, own_s, rim = call(
        functools.partial(far_kernel, counts),
        (offsets, cur, stiff, edge, mine, low1, high1),
        [rows(far, COLS), rows(far, COLS), (4, ROWS, levels, WIDE), rows(ROWS), rows(4)],
    )
    low3, high3 = exchange(up, down, "gx")
    message = (2 * (COLS // LANES) + 1, levels, LANES)
    u1, v1, w1, p1, up, down = call(
        functools.partial(own_kernel, counts),
        (offsets, own, own_s, rim, low1, low2, high1, high2, table),
        [rows(ROWS + 2), rows(ROWS), rows(ROWS), rows(ROWS), message, message],
        [rows(ROWS + 4), rows(2 * ROWS)],
    )
    low4, high4 = exchange(up, down, "gx")
    outer = call(
        functools.partial(halo_kernel, counts),
        (offsets, own, own_s, rim, low1, low2, low3, high1, high2, high3, table, u1, v1, w1, p1),
        [rows(8), rows(6), rows(6), rows(6), rows(4), rows(ROWS + 4), rows(ROWS + 2), rows(ROWS + 2), rows(ROWS + 2)],
        [rows(8), rows(3 * ROWS), rows(ROWS + 2)],
    )
    new, back = call(
        functools.partial(last_kernel, counts),
        (offsets, *outer, low4, high4, table, coarse),
        [nest.shape, parent.shape],
        [rows(ROWS + 8), rows(ROWS + 6), rows(ROWS + 6), rows(ROWS + 6)],
    )
    return jnp.transpose(new, (0, 2, 1, 3)), back


def solution(mesh):
    return jax.shard_map(
        per_device,
        mesh=mesh,
        in_specs=(
            P(None, None, "gx", "gy"),
            P(None, "gx", "gy"),
            P(None, None, "gx", "gy"),
            P(),
            P(),
        ),
        out_specs=(P(None, None, "gx", "gy"), P(None, None, "gx", "gy")),
        check_vma=False,
    )
```

```python
import functools

import jax
import jax.numpy as jnp
from jax import lax
from jax.experimental import pallas as pl
from jax.experimental.pallas import tpu as pltpu
from jax.sharding import PartitionSpec as P

RATIO = 3
GRAD = 0.25
DIV = 0.25
LIFT = 0.5
F32 = jnp.float32
BF16 = jnp.bfloat16
VMEM_BYTES = 24 * 1024 * 1024

ROWS = 6
COLS = 384
LANES = 128
WIDE = COLS + LANES
SIDE = 8
SLOTS = LANES // SIDE
U, V, W, PR = 0, 1, 2, 3
GROUP = 2
NEAR = {PR: 2}
KEEP = 3
S_GROUP = 4 * ROWS
EDGE_GROUP = S_GROUP + ROWS
GROUPS = EDGE_GROUP + 4
PACK = -(-GROUPS // SLOTS) * LANES
CHUNK_1 = ((V, 0, 3), (W, 0, 3), ("s", 0, 3))
CHUNK_2 = ((PR, 0, 2), (U, 0, 1), ("s", 3, 1))
CHUNK_3 = ((PR, 2, 1), (U, 1, 3), ("s", 4, 2))
SENT = [(PR, n) for n in range(5)] + [(U, n) for n in range(4)] + [(V, n) for n in range(3)]
SENT += [(W, n) for n in range(3)] + [("s", n) for n in range(6)]


def rows_of(chunk):
    return [(what, first + n) for what, first, count in chunk for n in range(count)]


def lanes_of(shape):
    return lax.broadcasted_iota(jnp.int32, shape, len(shape) - 1)


def column_of_lane(lane):
    return jnp.where(lane < COLS + LANES // 2, lane, lane - WIDE)


def is_edge(index, count):
    return (index < RATIO) | (index >= count - RATIO)


def expand_all(coarse):
    lane = lanes_of(coarse.shape)
    parts = [
        jnp.take_along_axis(coarse, (lane + first) // RATIO, axis=1) for first in range(0, COLS, LANES)
    ]
    return jnp.concatenate(parts, axis=1)


def turn(x, amount):
    amount = amount % x.shape[1]
    return x if amount == 0 else pltpu.roll(x, amount, 1)


def next_col(x):
    return pltpu.roll(x, x.shape[1] - 1, 1)


def prev_col(x):
    return pltpu.roll(x, 1, 1)


SUB = 8


def level_up(x):
    levels = x.shape[0]
    turned = pltpu.roll(x, levels - 1, 0)
    last = turned[levels - SUB :]
    level = lax.broadcasted_iota(jnp.int32, last.shape, 0)
    return jnp.concatenate([turned[: levels - SUB], jnp.where(level < SUB - 1, last, 0.0)], axis=0)


def level_down(x):
    turned = pltpu.roll(x, 1, 0)
    first = turned[:SUB]
    level = lax.broadcasted_iota(jnp.int32, first.shape, 0)
    return jnp.concatenate([jnp.where(level > 0, first, 0.0), turned[SUB:]], axis=0)


def split_dot(table, x):
    high = x.astype(BF16)
    low = (x - high.astype(F32)).astype(BF16)
    stacked = jnp.concatenate([high, low, high], axis=0)
    return jnp.dot(table, stacked, preferred_element_type=F32)


def own_row(near, side):
    return ROWS - 1 - near if side == 0 else near


def is_odd(index):
    return lax.rem(index, 2) == 1


def by_pair(odd, up, down):
    return jnp.where(odd, up, down), jnp.where(odd, down, up)


class Received:
    def __init__(self, in_first, first, second):
        self.in_first, self.first, self.second = in_first, first, second

    def __getitem__(self, at):
        return jnp.where(self.in_first, self.first[at], self.second[at])


def low_high(odd, first, second):
    if first is None:
        return None, None
    return Received(jnp.logical_not(odd), first, second), Received(odd, first, second)


def prepare_kernel(
    counts, off_ref, nest_ref, stiff_hbm, parent_hbm,
    cur_ref, stiff_ref, parent_ref, left_ref, right_ref, edge_ref, up_ref, down_ref,
    nest_win, parent_win, sems,
):
    nx, ny = counts
    copies = [pltpu.make_async_copy(parent_hbm, parent_win, sems.at[4])]
    copies += [pltpu.make_async_copy(nest_ref.at[f], nest_win.at[f], sems.at[f]) for f in (V, W, PR, U)]
    copies.append(pltpu.make_async_copy(stiff_hbm, stiff_ref, sems.at[5]))
    for copy in copies:
        copy.start()
    gx, gy = lax.axis_index("gx"), lax.axis_index("gy")
    off_x, off_y = off_ref[0], off_ref[1]
    levels = nest_win.shape[2]
    col = lanes_of((levels, COLS)) + (gy * COLS - RATIO * off_y)
    edge_col = is_edge(col, ny)
    place = lanes_of((levels, LANES)) // SIDE
    packs = [[None, None] for _ in range(PACK // LANES)]

    def pack(row, group):
        tile, slot = group // SLOTS, group % SLOTS
        sides = (
            turn(row[:, :LANES], SIDE * slot),
            turn(row[:, COLS - LANES :], SIDE * (slot + 1) - LANES),
        )
        for side, value in enumerate(sides):
            held = packs[tile][side]
            packs[tile][side] = value if held is None else jnp.where(place == slot, value, held)

    copies[0].wait()
    rims = []
    for at, field in enumerate((V, W, PR, U)):
        bounds = []
        for coarse in range(ROWS // RATIO):
            value = parent_win[field, :, coarse, :]
            parent_ref[field, coarse] = value
            bounds.append(expand_all(value))
        copies[1 + at].wait()
        for row in range(ROWS):
            i = gx * ROWS + row - RATIO * off_x
            held = is_edge(i, nx).astype(jnp.int32)
            value = jnp.where(edge_col | (held > 0), bounds[row // RATIO], nest_win[field, row])
            cur_ref[field, row] = value
            pack(value, field * ROWS + row)
        rim = jnp.where(gx == 0, bounds[0], bounds[-1])
        edge_ref[field] = rim
        pack(rim, EDGE_GROUP + field)
    copies[5].wait()
    for row in range(ROWS):
        pack(stiff_ref[row], S_GROUP + row)
    for tile, (left, right) in enumerate(packs):
        at = slice(LANES * tile, LANES * (tile + 1))
        left_ref[:, at], right_ref[:, at] = by_pair(is_odd(gy), right, left)
    fill_message(CHUNK_1, cur_ref, stiff_ref, up_ref, down_ref)


def fill_message(chunk, cur_ref, stiff_ref, first_ref, second_ref):
    odd = is_odd(lax.axis_index("gx"))
    for at, (what, near) in enumerate(rows_of(chunk)):
        rows = by_pair(odd, own_row(near, 0), own_row(near, 1))
        for row, out in zip(rows, (first_ref, second_ref)):
            out[at] = stiff_ref[row] if what == "s" else cur_ref[what, row]


def group_of(what, row):
    return S_GROUP + row if what == "s" else what * ROWS + row


def near_kernel(last_y, cur_ref, stiff_ref, parent_ref, left_ref, right_ref, mine_ref, up_ref, down_ref):
    gx, gy = lax.axis_index("gx"), lax.axis_index("gy")
    levels = left_ref.shape[0]
    lane = lanes_of((levels, LANES))
    place = lane // SIDE
    from_left, from_right = low_high(is_odd(gy), left_ref, right_ref)
    mine_ref[0] = from_left[...]
    mine_ref[1] = from_right[...]

    def fill(side, cell):
        for tile in range(PACK // LANES):
            at = slice(LANES * tile, LANES * (tile + 1))
            out = mine_ref[side, :, at]
            for slot in range(SLOTS):
                group = tile * SLOTS + slot
                if group < S_GROUP:
                    value = parent_ref[group // ROWS, (group % ROWS) // RATIO, :, cell : cell + 1]
                elif EDGE_GROUP <= group < GROUPS:
                    field = group - EDGE_GROUP
                    value = jnp.where(
                        gx == 0,
                        parent_ref[field, 0, :, cell : cell + 1],
                        parent_ref[field, ROWS // RATIO - 1, :, cell : cell + 1],
                    )
                else:
                    continue
                out = jnp.where(place == slot, value, out)
            mine_ref[side, :, at] = out

    @pl.when(gy == 0)
    def _():
        fill(0, 0)

    @pl.when(gy == last_y)
    def _():
        fill(1, COLS // RATIO - 1)

    rows = rows_of(CHUNK_2)
    fill_message(CHUNK_2, cur_ref, stiff_ref, up_ref, down_ref)
    tight = []
    for side in range(2):
        tiles = [None] * (COLS // LANES)
        for hand in range(2):
            for at, (what, near) in enumerate(SENT):
                group = group_of(what, own_row(near, side))
                tile, slot = group // SLOTS, group % SLOTS
                target = hand * len(SENT) + at
                to_tile, to_slot = target // SLOTS, target % SLOTS
                value = turn(mine_ref[hand, :, LANES * tile : LANES * (tile + 1)], SIDE * (to_slot - slot))
                held = tiles[to_tile]
                tiles[to_tile] = value if held is None else jnp.where(place == to_slot, value, held)
        tight.append(jnp.concatenate(tiles, axis=1))
    up_ref[len(rows)], down_ref[len(rows)] = by_pair(is_odd(gx), *tight)


def beside(left, left_slot, right, right_slot):
    lane = lanes_of(left.shape)
    return jnp.where(
        lane < LANES // 2, turn(right, -SIDE * right_slot), turn(left, LANES - SIDE * (left_slot + 1))
    )


def mine_beside(mine_ref, group):
    tile, slot = group // SLOTS, group % SLOTS
    at = slice(LANES * tile, LANES * (tile + 1))
    return beside(mine_ref[0, :, at], slot, mine_ref[1, :, at], slot)


def sent_beside(near_ref, what, near):
    row = len(rows_of(CHUNK_2))
    index = SENT.index((what, near))
    tiles = []
    for target in (index, len(SENT) + index):
        tile = target // SLOTS
        tiles += [near_ref[row, :, LANES * tile : LANES * (tile + 1)], target % SLOTS]
    return beside(*tiles)


def far_kernel(
    counts, off_ref, cur_ref, stiff_ref, edge_ref, mine_ref, low1, high1, up_ref, down_ref, own_ref, own_s_ref, rim_ref
):
    del low1, high1
    at = Place(counts, off_ref, stiff_ref.shape[1])
    fill_message(CHUNK_3, cur_ref, stiff_ref, up_ref, down_ref)
    for n, (what, near) in enumerate(rows_of(CHUNK_3)):
        if what == U:
            rows = by_pair(is_odd(at.gx), own_row(near, 0), own_row(near, 1))
            for row, out in zip(rows, (up_ref, down_ref)):
                keep = at.keep(row)[:, :COLS]
                out[n] = wind_x(keep, cur_ref[U, row], cur_ref[PR, row - 1], cur_ref[PR, row + 1])
    for field in range(4):
        for row in range(ROWS):
            own_ref[field, row, :, :COLS] = cur_ref[field, row]
            own_ref[field, row, :, COLS:] = mine_beside(mine_ref, field * ROWS + row)
        rim_ref[field, :, :COLS] = edge_ref[field]
        rim_ref[field, :, COLS:] = mine_beside(mine_ref, EDGE_GROUP + field)
    for row in range(ROWS):
        own_s_ref[row, :, :COLS] = stiff_ref[row]
        own_s_ref[row, :, COLS:] = mine_beside(mine_ref, S_GROUP + row)


def received(refs, near_ref, what, near):
    for chunk, ref in zip((CHUNK_1, CHUNK_2, CHUNK_3), refs):
        rows = rows_of(chunk)
        if (what, near) in rows:
            main = ref[rows.index((what, near))]
    return jnp.concatenate([main, sent_beside(near_ref, what, near)], axis=1)


class Place:
    def __init__(self, counts, off_ref, levels):
        self.nx, self.ny = counts
        self.gx, self.gy = lax.axis_index("gx"), lax.axis_index("gy")
        self.last_x = self.nx // ROWS - 1
        self.off_x, self.off_y = off_ref[0], off_ref[1]
        j = column_of_lane(lanes_of((SUB, WIDE))) + (self.gy * COLS - RATIO * self.off_y)
        self.copies = levels // SUB
        self.held_once = is_edge(j, self.ny).astype(jnp.int32)
        self.held = self.over_levels(self.held_once)

    def neighbours(self, *swaps):
        return zip(*[low_high(is_odd(self.gx), first, second) for first, second in swaps])

    def keep(self, row):
        i = self.gx * ROWS + row - RATIO * self.off_x
        return self.over_levels(self.held_once + is_edge(i, self.nx).astype(jnp.int32)) > 0

    def over_levels(self, tile):
        return jnp.concatenate([tile] * self.copies, axis=0)

    def field_row(self, own, low, high, rim_ref, field, row):
        if 0 <= row < ROWS:
            return own[field, row]
        if row < 0:
            value = received(low, low[1], field, -1 - row)
            outer = self.gx == 0
        else:
            value = received(high, high[1], field, row - ROWS)
            outer = self.gx == self.last_x
        return jnp.where(outer, rim_ref[field], value)


def wind_x(keep, wind, p_low, p_high):
    return jnp.where(keep, wind, wind - GRAD * (p_high - p_low))


def in_groups(rows):
    rows = list(rows)
    return [rows[first : first + GROUP] for first in range(0, len(rows), GROUP)]


def side_by_side(rows):
    return rows[0] if len(rows) == 1 else jnp.concatenate(rows, axis=1)


def apart(x, count):
    return [x[:, WIDE * n : WIDE * (n + 1)] for n in range(count)]


def column_steps(table, rows):
    levels = table.shape[0] // 2
    winds, right_sides = [], []
    for keep, pressure, u_low, u_high, wind, lift, stiffness in rows:
        wind = jnp.where(keep, wind, wind - GRAD * (next_col(pressure) - prev_col(pressure)))
        change = (u_high - u_low) + (next_col(wind) - prev_col(wind)) + (level_up(lift) - level_down(lift))
        winds.append(wind)
        right_sides.append(pressure - DIV * change)
    both = split_dot(table, side_by_side(right_sides))
    firsts, arounds = apart(both[:levels], len(rows)), apart(both[levels:], len(rows))
    leftovers = [
        (right_side - first) - row[6] * first + around
        for row, right_side, first, around in zip(rows, right_sides, firsts, arounds)
    ]
    seconds = apart(split_dot(table[:levels], side_by_side(leftovers)), len(rows))
    results = []
    for (keep, pressure, _, _, _, lift, _), wind, first, second in zip(rows, winds, firsts, seconds):
        p_next = jnp.where(keep, pressure, first + second)
        w_next = jnp.where(keep, lift, lift - LIFT * (level_up(p_next) - p_next))
        results.append((wind, w_next, p_next))
    return results


def own_kernel(
    counts, off_ref, own_ref, own_s_ref, rim_ref, low1, low2, high1, high2, table_ref,
    u_out, v_out, w_out, p_out, up_ref, down_ref,
    p_win, s_win,
):
    levels = own_ref.shape[2]
    at = Place(counts, off_ref, levels)
    low, high = at.neighbours((low1, high1), (low2, high2), (None, None))
    deep = NEAR[PR]
    for row in range(-deep, ROWS + deep):
        p_win[row + deep] = at.field_row(own_ref, low, high, rim_ref, PR, row)
    for near in range(KEEP):
        s_win[KEEP - 1 - near] = received(low, low[1], "s", near)
        s_win[KEEP + ROWS + near] = received(high, high[1], "s", near)
    for row in range(ROWS):
        s_win[KEEP + row] = own_s_ref[row]
    for row in range(-1, ROWS + 1):
        wind = at.field_row(own_ref, low, high, rim_ref, U, row)
        u_out[row + 1] = wind_x(at.keep(row), wind, p_win[row + deep - 1], p_win[row + deep + 1])
    move_y = lax.rem(RATIO * at.off_y + WIDE, WIDE)
    table = table_ref[...]

    for rows in in_groups(range(ROWS)):
        results = column_steps(
            table,
            [
                (
                    at.keep(row), p_win[row + deep], u_out[row], u_out[row + 2],
                    own_ref[V, row], own_ref[W, row],
                    pltpu.roll(s_win[row + KEEP - RATIO * at.off_x], move_y, 1),
                )
                for row in rows
            ],
        )
        for row, result in zip(rows, results):
            v_out[row], w_out[row], p_out[row] = result
    starts = by_pair(is_odd(at.gx), 1, 3)
    for out, first in zip((up_ref, down_ref), starts):
        beyond = None
        for n in range(2):
            value = p_out[first + n]
            for tile in range(COLS // LANES):
                out[n * (COLS // LANES) + tile] = value[:, LANES * tile : LANES * (tile + 1)]
            ext = value[:, COLS:]
            beyond = ext if n == 0 else merge_ext(beyond, ext)
        out[2 * (COLS // LANES)] = beyond


def merge_ext(first, second):
    lane = lanes_of(first.shape)
    near = jnp.where(lane < LANES // 2, turn(second, SIDE), turn(second, -SIDE))
    return jnp.where((lane < SIDE) | (lane >= LANES - SIDE), first, near)


def split_ext(merged, n):
    if n == 0:
        return merged
    lane = lanes_of(merged.shape)
    return jnp.where(lane < LANES // 2, turn(merged, -SIDE), turn(merged, SIDE))


def halo_kernel(
    counts, off_ref, own_ref, own_s_ref, rim_ref, low1, low2, low3, high1, high2, high3, table_ref,
    u_own, v_own, w_own, p_own,
    u_rim, v_rim, w_rim, p_rim, s_rim, u_out, v_out, w_out, p_out,
    p_win, s_win, s_mid,
):
    levels = own_ref.shape[2]
    at = Place(counts, off_ref, levels)
    low, high = at.neighbours((low1, high1), (low2, high2), (low3, high3))
    table = table_ref[...]
    deep = KEEP
    for n in range(deep + 1):
        p_win[n] = at.field_row(own_ref, low, high, rim_ref, PR, n - deep)
        p_win[deep + 1 + n] = at.field_row(own_ref, low, high, rim_ref, PR, ROWS - 1 + n)
    for near in range(ROWS):
        s_win[ROWS - 1 - near] = received(low, low[1], "s", near)
        s_win[2 * ROWS + near] = received(high, high[1], "s", near)
        s_win[ROWS + near] = own_s_ref[near]
    move_y = lax.rem(RATIO * at.off_y + WIDE, WIDE)

    def stiffness(row):
        return pltpu.roll(s_win[row + ROWS - RATIO * at.off_x], move_y, 1)

    def p_before(row):
        return p_win[row + deep] if row <= 0 else p_win[row - ROWS + 1 + deep + 1]

    def rim_of(depth, row):
        return row + depth if row < 0 else row - ROWS + depth

    for row in (-4, -3, -2, 7, 8, 9):
        near = -1 - row if row < 0 else row - ROWS
        near_ref, outer = (low[1], at.gx == 0) if row < 0 else (high[1], at.gx == at.last_x)
        outward, inward = (sent_beside(near_ref, PR, near + by) for by in (1, -1))
        p_low, p_high = (outward, inward) if row < 0 else (inward, outward)
        main = received(low if row < 0 else high, near_ref, U, near)
        ext = wind_x(at.keep(row)[:, COLS:], main[:, COLS:], p_low, p_high)
        value = jnp.concatenate([main[:, :COLS], ext], axis=1)
        u_rim[rim_of(4, row)] = jnp.where(outer, rim_ref[U], value)

    def u_after(row):
        return u_own[row + 1] if -1 <= row <= ROWS else u_rim[rim_of(4, row)]

    for n, row in enumerate((-3, -2, 7, 8)):
        s_rim[n] = stiffness(row)
    for row in range(-1, ROWS + 1):
        s_mid[row + 1] = stiffness(row)
    for rows in in_groups((-3, -2, -1, 6, 7, 8)):
        results = column_steps(
            table,
            [
                (
                    at.keep(row), p_before(row), u_after(row - 1), u_after(row + 1),
                    at.field_row(own_ref, low, high, rim_ref, V, row),
                    at.field_row(own_ref, low, high, rim_ref, W, row),
                    s_rim[(-3, -2, 7, 8).index(row)] if row in (-3, -2, 7, 8) else s_mid[row + 1],
                )
                for row in rows
            ],
        )
        for row, result in zip(rows, results):
            n = rim_of(KEEP, row)
            v_rim[n], w_rim[n], p_rim[n] = result

    def pick(own, rim, row):
        return own[row] if 0 <= row < ROWS else rim[rim_of(KEEP, row)]

    for row in range(-2, ROWS + 2):
        u_out[row + 2] = wind_x(
            at.keep(row), u_after(row), pick(p_own, p_rim, row - 1), pick(p_own, p_rim, row + 1)
        )
    for rows in in_groups(range(-1, ROWS + 1)):
        results = column_steps(
            table,
            [
                (
                    at.keep(row), pick(p_own, p_rim, row), u_out[row + 1], u_out[row + 3],
                    pick(v_own, v_rim, row), pick(w_own, w_rim, row), s_mid[row + 1],
                )
                for row in rows
            ],
        )
        for row, result in zip(rows, results):
            v_out[row + 1], w_out[row + 1], p_out[row + 1] = result


def last_kernel(
    counts, off_ref, u_rim, v_rim, w_rim, p_rim, s_rim, u_mid, v_mid, w_mid, p_mid,
    low_ref, high_ref, table_ref, parent_ref,
    new_hbm, back_hbm,
    u_win, v_win, w_win, q_win, new_win, back_win, sems,
):
    levels = u_rim.shape[1]
    at = Place(counts, off_ref, levels)
    table = table_ref[...]
    tiles = COLS // LANES

    def sent(ref, n):
        parts = [ref[n * tiles + tile] for tile in range(tiles)] + [split_ext(ref[2 * tiles], n)]
        return jnp.concatenate(parts, axis=1)

    low_ref, high_ref = low_high(is_odd(at.gx), low_ref, high_ref)
    for row in range(ROWS + 4):
        u_win[row + 2] = u_mid[row]
    for row in range(ROWS + 2):
        v_win[row + 2] = v_mid[row]
        w_win[row + 2] = w_mid[row]
        q_win[row + 2] = p_mid[row]
    windows = ((U, u_win, 4), (V, v_win, KEEP), (W, w_win, KEEP), (PR, q_win, KEEP))
    send_out(True, at, windows, new_win, new_hbm, sems)
    low_p = [sent(low_ref, 0), sent(low_ref, 1), p_rim[0], p_rim[1]]
    high_p = [p_rim[4], p_rim[5], sent(high_ref, 0), sent(high_ref, 1)]
    for n, row in enumerate((-4, -3)):
        u_win[n] = wind_x(at.keep(row), u_rim[n], low_p[n], low_p[n + 2])
    for n, row in enumerate((8, 9)):
        u_win[12 + n] = wind_x(at.keep(row), u_rim[6 + n], high_p[n], high_p[n + 2])
    for rows in in_groups(enumerate((-3, -2, 7, 8))):
        rims = [(0, 1, 4, 5)[n] for n, _ in rows]
        results = column_steps(
            table,
            [
                (
                    at.keep(row), p_rim[rim], u_win[row + 3], u_win[row + 5],
                    v_rim[rim], w_rim[rim], s_rim[n],
                )
                for (n, row), rim in zip(rows, rims)
            ],
        )
        for (_, row), result in zip(rows, results):
            v_win[row + KEEP], w_win[row + KEEP], q_win[row + KEEP] = result
    send_out(False, at, windows, new_win, new_hbm, sems)
    feed_back(at, windows, parent_ref, back_win, back_hbm, sems)
    for ready in (True, False):
        send_out(ready, at, windows, new_win, new_hbm, sems, wait=True)


def send_out(ready, at, windows, new_win, new_hbm, sems, wait=False):
    move_y = lax.rem(WIDE - RATIO * at.off_y, WIDE)
    for step in (-1, 0, 1):
        kept = [row for row in range(ROWS) if (-1 <= row + RATIO * step <= ROWS) == ready]
        if not kept:
            continue

        @pl.when(at.off_x == step)
        def _(step=step, kept=kept):
            for field, window, deep in windows:
                if not wait:
                    for row in kept:
                        moved = pltpu.roll(window[row + deep + RATIO * step], move_y, 1)
                        new_win[field, row] = moved[:, :COLS]
                part = pl.ds(kept[0], len(kept))
                copy = pltpu.make_async_copy(
                    new_win.at[field, part], new_hbm.at[field, part], sems.at[field + (0 if ready else 4)]
                )
                if wait:
                    copy.wait()
                else:
                    copy.start()


def feed_back(at, windows, parent_ref, back_win, back_hbm, sems):
    levels = parent_ref.shape[2]
    cells_x, cells_y = at.nx // RATIO, at.ny // RATIO
    coarse_rows, coarse_cols = ROWS // RATIO, COLS // RATIO

    def inside(index, count):
        return (index >= 1) & (index <= count - 2)

    source = column_of_lane(lax.broadcasted_iota(jnp.int32, (WIDE, coarse_cols), 0))
    apart = source - RATIO * lax.broadcasted_iota(jnp.int32, (WIDE, coarse_cols), 1)
    spread = jnp.where(
        (apart >= 0) & (apart < RATIO),
        0.5,
        jnp.where((apart >= -RATIO) & (apart < 2 * RATIO), 0.25, 0.0),
    ).astype(BF16)
    cell = lanes_of((levels, coarse_cols)) + (at.gy * coarse_cols - at.off_y)
    weight_y = (
        0.25 * inside(cell - 1, cells_y).astype(F32)
        + 0.5 * inside(cell, cells_y).astype(F32)
        + 0.25 * inside(cell + 1, cells_y).astype(F32)
    )
    centre_y = inside(cell, cells_y).astype(jnp.int32)
    smooth = []
    for coarse in range(coarse_rows):
        a = at.gx * coarse_rows + coarse - at.off_x
        inner = [inside(a + d, cells_x).astype(F32) for d in (-1, 0, 1)]
        weights = [s * m for s, m in zip((0.25, 0.5, 0.25), inner)]
        weight_x = weights[0] + weights[1] + weights[2]
        centre = (centre_y * inside(a, cells_x).astype(jnp.int32)) > 0
        scale = jnp.where(centre, 1.0 / jnp.where(centre, 9.0 * weight_x * weight_y, 1.0), 0.0)
        smooth.append((inner, weights, centre, scale))
    copies = []
    for field, window, deep in windows:
        for coarse, (inner, weights, centre, scale) in enumerate(smooth):
            start = deep - KEEP + RATIO * coarse
            total = None
            for d in range(3):
                part = window[start + 3 * d] + window[start + 3 * d + 1] + window[start + 3 * d + 2]
                part = jnp.where(inner[d] > 0, part * weights[d], 0.0)
                total = part if total is None else total + part
            total = jnp.where(at.held > 0, 0.0, total)
            high = total.astype(BF16)
            low = (total - high.astype(F32)).astype(BF16)
            summed = jnp.dot(high, spread, preferred_element_type=F32) + jnp.dot(
                low, spread, preferred_element_type=F32
            )
            back_win[field, :, coarse, :] = jnp.where(centre, summed * scale, parent_ref[field, coarse])
        copies.append(pltpu.make_async_copy(back_win.at[field], back_hbm.at[field], sems.at[8 + field]))
        copies[-1].start()
    for copy in copies:
        copy.wait()


def call(body, ins, outs, scratch=(), spaces=None, out_spaces=None):
    def space(x):
        if x.dtype == jnp.int32:
            return pltpu.SMEM
        return pltpu.VMEM

    spaces = spaces or [space(x) for x in ins]
    return pl.pallas_call(
        body,
        out_shape=[jax.ShapeDtypeStruct(shape, F32) for shape in outs],
        in_specs=[pl.BlockSpec(memory_space=s) for s in spaces],
        out_specs=[pl.BlockSpec(memory_space=s) for s in out_spaces or [pltpu.VMEM] * len(outs)],
        scratch_shapes=[s if not isinstance(s, tuple) else pltpu.VMEM(s, F32) for s in scratch],
        compiler_params=pltpu.CompilerParams(vmem_limit_bytes=VMEM_BYTES),
    )(*ins)


def exchange(first, second, axis):
    def swap(x, start):
        pairs = [(i, i + 1) for i in range(start, lax.axis_size(axis) - 1, 2)]
        return lax.ppermute(x, axis, pairs + [(high, low) for low, high in pairs])

    return swap(first, 1), swap(second, 0)


def per_device(nest_state, stiffness, parent, inverse_table, offsets):
    levels = nest_state.shape[1]
    nx = nest_state.shape[2] * lax.axis_size("gx")
    ny = nest_state.shape[3] * lax.axis_size("gy")
    counts = (nx, ny)
    nest = jnp.transpose(nest_state, (0, 2, 1, 3))
    stiff_in = jnp.transpose(stiffness, (1, 0, 2))

    nothing = jnp.zeros_like(inverse_table[:1])
    shifted = jnp.concatenate([inverse_table[1:], nothing], 0)
    shifted += jnp.concatenate([nothing, inverse_table[:-1]], 0)
    stack = jnp.concatenate([inverse_table, 0.25 * shifted], 0)
    top = lax.reduce_precision(stack, 8, 7)
    table = jnp.concatenate([top, top, stack - top], 1).astype(BF16)

    def rows(count, width=WIDE):
        return (count, levels, width)

    first, near, far = (len(rows_of(chunk)) for chunk in (CHUNK_1, CHUNK_2, CHUNK_3))
    cur, stiff, coarse, to_left, to_right, edge, up, down = call(
        functools.partial(prepare_kernel, counts),
        [pltpu.with_memory_space_constraint(x, pltpu.HBM) for x in (offsets, nest, stiff_in, parent)],
        [nest.shape, stiff_in.shape, (4, ROWS // RATIO, levels, LANES), (levels, PACK), (levels, PACK)]
        + [(4, levels, COLS), rows(first, COLS), rows(first, COLS)],
        [nest.shape, parent.shape, pltpu.SemaphoreType.DMA((6,))],
        [pltpu.SMEM, pltpu.HBM, pltpu.HBM, pltpu.HBM],
    )
    low1, high1 = exchange(up, down, "gx")
    from_left, from_right = exchange(to_left, to_right, "gy")
    mine, up, down = call(
        functools.partial(near_kernel, lax.axis_size("gy") - 1),
        (cur, stiff, coarse, from_left, from_right),
        [(2, levels, PACK), rows(near + 1, COLS), rows(near + 1, COLS)],
    )
    low2, high2 = exchange(up, down, "gx")
    up, down, own, own_s, rim = call(
        functools.partial(far_kernel, counts),
        (offsets, cur, stiff, edge, mine, low1, high1),
        [rows(far, COLS), rows(far, COLS), (4, ROWS, levels, WIDE), rows(ROWS), rows(4)],
    )
    low3, high3 = exchange(up, down, "gx")
    message = (2 * (COLS // LANES) + 1, levels, LANES)
    u1, v1, w1, p1, up, down = call(
        functools.partial(own_kernel, counts),
        (offsets, own, own_s, rim, low1, low2, high1, high2, table),
        [rows(ROWS + 2), rows(ROWS), rows(ROWS), rows(ROWS), message, message],
        [rows(ROWS + 4), rows(2 * ROWS)],
    )
    low4, high4 = exchange(up, down, "gx")
    outer = call(
        functools.partial(halo_kernel, counts),
        (offsets, own, own_s, rim, low1, low2, low3, high1, high2, high3, table, u1, v1, w1, p1),
        [rows(8), rows(6), rows(6), rows(6), rows(4), rows(ROWS + 4), rows(ROWS + 2), rows(ROWS + 2), rows(ROWS + 2)],
        [rows(8), rows(3 * ROWS), rows(ROWS + 2)],
    )
    new, back = call(
        functools.partial(last_kernel, counts),
        (offsets, *outer, low4, high4, table, coarse),
        [nest.shape, parent.shape],
        [rows(ROWS + 8), rows(ROWS + 6), rows(ROWS + 6), rows(ROWS + 6)]
        + [nest.shape, parent.shape, pltpu.SemaphoreType.DMA((12,))],
        out_spaces=[pl.ANY, pl.ANY],
    )
    return jnp.transpose(new, (0, 2, 1, 3)), back


def solution(mesh):
    return jax.shard_map(
        per_device,
        mesh=mesh,
        in_specs=(
            P(None, None, "gx", "gy"),
            P(None, "gx", "gy"),
            P(None, None, "gx", "gy"),
            P(),
            P(),
        ),
        out_specs=(P(None, None, "gx", "gy"), P(None, None, "gx", "gy")),
        check_vma=False,
    )
```

```python
import functools

import jax
import jax.numpy as jnp
from jax import lax
from jax.experimental import pallas as pl
from jax.experimental.pallas import tpu as pltpu
from jax.sharding import PartitionSpec as P

RATIO = 3
GRAD = 0.25
DIV = 0.25
LIFT = 0.5
F32 = jnp.float32
BF16 = jnp.bfloat16
VMEM_BYTES = 24 * 1024 * 1024

ROWS = 6
COLS = 384
LANES = 128
WIDE = COLS + LANES
SIDE = 8
SLOTS = LANES // SIDE
U, V, W, PR = 0, 1, 2, 3
GROUP = 2
NEAR = {PR: 2}
KEEP = 3
S_GROUP = 4 * ROWS
EDGE_GROUP = S_GROUP + ROWS
GROUPS = EDGE_GROUP + 4
PACK = -(-GROUPS // SLOTS) * LANES
CHUNK_1 = ((V, 0, 3), (W, 0, 3), ("s", 0, 3))
CHUNK_2 = ((PR, 0, 2), (U, 0, 1), ("s", 3, 1))
CHUNK_3 = ((PR, 2, 1), (U, 1, 3), ("s", 4, 2))
SENT = [(PR, n) for n in range(5)] + [(U, n) for n in range(4)] + [(V, n) for n in range(3)]
SENT += [(W, n) for n in range(3)] + [("s", n) for n in range(6)]


def rows_of(chunk):
    return [(what, first + n) for what, first, count in chunk for n in range(count)]


def lanes_of(shape):
    return lax.broadcasted_iota(jnp.int32, shape, len(shape) - 1)


def column_of_lane(lane):
    return jnp.where(lane < COLS + LANES // 2, lane, lane - WIDE)


def is_edge(index, count):
    return (index < RATIO) | (index >= count - RATIO)


def expand_all(coarse):
    lane = lanes_of(coarse.shape)
    parts = [
        jnp.take_along_axis(coarse, (lane + first) // RATIO, axis=1) for first in range(0, COLS, LANES)
    ]
    return jnp.concatenate(parts, axis=1)


def turn(x, amount):
    amount = amount % x.shape[1]
    return x if amount == 0 else pltpu.roll(x, amount, 1)


def next_col(x):
    return pltpu.roll(x, x.shape[1] - 1, 1)


def prev_col(x):
    return pltpu.roll(x, 1, 1)


SUB = 8


def level_up(x):
    levels = x.shape[0]
    turned = pltpu.roll(x, levels - 1, 0)
    last = turned[levels - SUB :]
    level = lax.broadcasted_iota(jnp.int32, last.shape, 0)
    return jnp.concatenate([turned[: levels - SUB], jnp.where(level < SUB - 1, last, 0.0)], axis=0)


def level_down(x):
    turned = pltpu.roll(x, 1, 0)
    first = turned[:SUB]
    level = lax.broadcasted_iota(jnp.int32, first.shape, 0)
    return jnp.concatenate([jnp.where(level > 0, first, 0.0), turned[SUB:]], axis=0)


def split_dot(table, x):
    high = x.astype(BF16)
    low = (x - high.astype(F32)).astype(BF16)
    stacked = jnp.concatenate([high, low, high], axis=0)
    return jnp.dot(table, stacked, preferred_element_type=F32)


def own_row(near, side):
    return ROWS - 1 - near if side == 0 else near


def is_odd(index):
    return lax.rem(index, 2) == 1


def by_pair(odd, up, down):
    return jnp.where(odd, up, down), jnp.where(odd, down, up)


class Received:
    def __init__(self, in_first, first, second):
        self.in_first, self.first, self.second = in_first, first, second

    def __getitem__(self, at):
        return jnp.where(self.in_first, self.first[at], self.second[at])


def low_high(odd, first, second):
    if first is None:
        return None, None
    return Received(jnp.logical_not(odd), first, second), Received(odd, first, second)


def prepare_kernel(
    counts, off_ref, nest_ref, stiff_hbm, parent_hbm,
    cur_ref, stiff_ref, parent_ref, left_ref, right_ref, edge_ref, up_ref, down_ref,
    nest_win, parent_win, sems,
):
    nx, ny = counts
    copies = [pltpu.make_async_copy(parent_hbm, parent_win, sems.at[4])]
    copies += [pltpu.make_async_copy(nest_ref.at[f], nest_win.at[f], sems.at[f]) for f in (V, W, PR, U)]
    copies.append(pltpu.make_async_copy(stiff_hbm, stiff_ref, sems.at[5]))
    for copy in copies:
        copy.start()
    gx, gy = lax.axis_index("gx"), lax.axis_index("gy")
    off_x, off_y = off_ref[0], off_ref[1]
    levels = nest_win.shape[2]
    col = lanes_of((levels, COLS)) + (gy * COLS - RATIO * off_y)
    edge_col = is_edge(col, ny)
    place = lanes_of((levels, LANES)) // SIDE

    def pack(packs, row, group):
        tile, slot = group // SLOTS, group % SLOTS
        sides = (
            turn(row[:, :LANES], SIDE * slot),
            turn(row[:, COLS - LANES :], SIDE * (slot + 1) - LANES),
        )
        for side, value in enumerate(sides):
            held = packs[tile][side]
            packs[tile][side] = value if held is None else jnp.where(place == slot, value, held)

    def fill(on_rim):
        packs = [[None, None] for _ in range(PACK // LANES)]
        if on_rim:
            copies[0].wait()
        for at, field in enumerate((V, W, PR, U)):
            if on_rim:
                bounds = [expand_all(parent_win[field, :, coarse, :]) for coarse in range(ROWS // RATIO)]
            copies[1 + at].wait()
            for row in range(ROWS):
                value = nest_win[field, row]
                if on_rim:
                    i = gx * ROWS + row - RATIO * off_x
                    held = is_edge(i, nx).astype(jnp.int32)
                    value = jnp.where(edge_col | (held > 0), bounds[row // RATIO], value)
                cur_ref[field, row] = value
                pack(packs, value, field * ROWS + row)
            rim = jnp.where(gx == 0, bounds[0], bounds[-1]) if on_rim else jnp.zeros((levels, COLS), F32)
            edge_ref[field] = rim
            if on_rim:
                pack(packs, rim, EDGE_GROUP + field)
        copies[5].wait()
        for row in range(ROWS):
            pack(packs, stiff_ref[row], S_GROUP + row)
        for tile, (left, right) in enumerate(packs):
            at = slice(LANES * tile, LANES * (tile + 1))
            if left is None:
                left = right = jnp.zeros((levels, LANES), F32)
            left_ref[:, at], right_ref[:, at] = by_pair(is_odd(gy), right, left)
        if not on_rim:
            copies[0].wait()
        for field in range(4):
            for coarse in range(ROWS // RATIO):
                parent_ref[field, coarse] = parent_win[field, :, coarse, :]

    rim_x = (gx == 0) | (gx == nx // ROWS - 1)
    rim_y = (gy == 0) | (gy == ny // COLS - 1)
    pl.when(rim_x | rim_y)(lambda: fill(True))
    pl.when(jnp.logical_not(rim_x | rim_y))(lambda: fill(False))
    fill_message(CHUNK_1, cur_ref, stiff_ref, up_ref, down_ref)


def fill_message(chunk, cur_ref, stiff_ref, first_ref, second_ref):
    odd = is_odd(lax.axis_index("gx"))
    for at, (what, near) in enumerate(rows_of(chunk)):
        rows = by_pair(odd, own_row(near, 0), own_row(near, 1))
        for row, out in zip(rows, (first_ref, second_ref)):
            out[at] = stiff_ref[row] if what == "s" else cur_ref[what, row]


def group_of(what, row):
    return S_GROUP + row if what == "s" else what * ROWS + row


def near_kernel(last_y, cur_ref, stiff_ref, parent_ref, left_ref, right_ref, mine_ref, up_ref, down_ref):
    gx, gy = lax.axis_index("gx"), lax.axis_index("gy")
    levels = left_ref.shape[0]
    lane = lanes_of((levels, LANES))
    place = lane // SIDE
    from_left, from_right = low_high(is_odd(gy), left_ref, right_ref)
    mine_ref[0] = from_left[...]
    mine_ref[1] = from_right[...]

    def fill(side, cell):
        for tile in range(PACK // LANES):
            at = slice(LANES * tile, LANES * (tile + 1))
            out = mine_ref[side, :, at]
            for slot in range(SLOTS):
                group = tile * SLOTS + slot
                if group < S_GROUP:
                    value = parent_ref[group // ROWS, (group % ROWS) // RATIO, :, cell : cell + 1]
                elif EDGE_GROUP <= group < GROUPS:
                    field = group - EDGE_GROUP
                    value = jnp.where(
                        gx == 0,
                        parent_ref[field, 0, :, cell : cell + 1],
                        parent_ref[field, ROWS // RATIO - 1, :, cell : cell + 1],
                    )
                else:
                    continue
                out = jnp.where(place == slot, value, out)
            mine_ref[side, :, at] = out

    @pl.when(gy == 0)
    def _():
        fill(0, 0)

    @pl.when(gy == last_y)
    def _():
        fill(1, COLS // RATIO - 1)

    rows = rows_of(CHUNK_2)
    fill_message(CHUNK_2, cur_ref, stiff_ref, up_ref, down_ref)
    tight = []
    for side in range(2):
        tiles = [None] * (COLS // LANES)
        for hand in range(2):
            for at, (what, near) in enumerate(SENT):
                group = group_of(what, own_row(near, side))
                tile, slot = group // SLOTS, group % SLOTS
                target = hand * len(SENT) + at
                to_tile, to_slot = target // SLOTS, target % SLOTS
                value = turn(mine_ref[hand, :, LANES * tile : LANES * (tile + 1)], SIDE * (to_slot - slot))
                held = tiles[to_tile]
                tiles[to_tile] = value if held is None else jnp.where(place == to_slot, value, held)
        tight.append(jnp.concatenate(tiles, axis=1))
    up_ref[len(rows)], down_ref[len(rows)] = by_pair(is_odd(gx), *tight)


def beside(left, left_slot, right, right_slot):
    lane = lanes_of(left.shape)
    return jnp.where(
        lane < LANES // 2, turn(right, -SIDE * right_slot), turn(left, LANES - SIDE * (left_slot + 1))
    )


def mine_beside(mine_ref, group):
    tile, slot = group // SLOTS, group % SLOTS
    at = slice(LANES * tile, LANES * (tile + 1))
    return beside(mine_ref[0, :, at], slot, mine_ref[1, :, at], slot)


def sent_beside(near_ref, what, near):
    row = len(rows_of(CHUNK_2))
    index = SENT.index((what, near))
    tiles = []
    for target in (index, len(SENT) + index):
        tile = target // SLOTS
        tiles += [near_ref[row, :, LANES * tile : LANES * (tile + 1)], target % SLOTS]
    return beside(*tiles)


def far_kernel(
    counts, off_ref, cur_ref, stiff_ref, edge_ref, mine_ref, low1, high1, up_ref, down_ref, own_ref, own_s_ref, rim_ref
):
    del low1, high1
    at = Place(counts, off_ref, stiff_ref.shape[1])
    fill_message(CHUNK_3, cur_ref, stiff_ref, up_ref, down_ref)
    for n, (what, near) in enumerate(rows_of(CHUNK_3)):
        if what == U:
            rows = by_pair(is_odd(at.gx), own_row(near, 0), own_row(near, 1))
            for row, out in zip(rows, (up_ref, down_ref)):
                keep = at.keep(row)[:, :COLS]
                out[n] = wind_x(keep, cur_ref[U, row], cur_ref[PR, row - 1], cur_ref[PR, row + 1])
    for field in range(4):
        for row in range(ROWS):
            own_ref[field, row, :, :COLS] = cur_ref[field, row]
            own_ref[field, row, :, COLS:] = mine_beside(mine_ref, field * ROWS + row)
        rim_ref[field, :, :COLS] = edge_ref[field]
        rim_ref[field, :, COLS:] = mine_beside(mine_ref, EDGE_GROUP + field)
    for row in range(ROWS):
        own_s_ref[row, :, :COLS] = stiff_ref[row]
        own_s_ref[row, :, COLS:] = mine_beside(mine_ref, S_GROUP + row)


def received(refs, near_ref, what, near):
    for chunk, ref in zip((CHUNK_1, CHUNK_2, CHUNK_3), refs):
        rows = rows_of(chunk)
        if (what, near) in rows:
            main = ref[rows.index((what, near))]
    return jnp.concatenate([main, sent_beside(near_ref, what, near)], axis=1)


class Place:
    def __init__(self, counts, off_ref, levels):
        self.nx, self.ny = counts
        self.gx, self.gy = lax.axis_index("gx"), lax.axis_index("gy")
        self.last_x = self.nx // ROWS - 1
        self.off_x, self.off_y = off_ref[0], off_ref[1]
        j = column_of_lane(lanes_of((SUB, WIDE))) + (self.gy * COLS - RATIO * self.off_y)
        self.copies = levels // SUB
        self.held_once = is_edge(j, self.ny).astype(jnp.int32)
        self.held = self.over_levels(self.held_once)

    def neighbours(self, *swaps):
        return zip(*[low_high(is_odd(self.gx), first, second) for first, second in swaps])

    def keep(self, row):
        i = self.gx * ROWS + row - RATIO * self.off_x
        return self.over_levels(self.held_once + is_edge(i, self.nx).astype(jnp.int32)) > 0

    def over_levels(self, tile):
        return jnp.concatenate([tile] * self.copies, axis=0)

    def field_row(self, own, low, high, rim_ref, field, row):
        if 0 <= row < ROWS:
            return own[field, row]
        if row < 0:
            value = received(low, low[1], field, -1 - row)
            outer = self.gx == 0
        else:
            value = received(high, high[1], field, row - ROWS)
            outer = self.gx == self.last_x
        return jnp.where(outer, rim_ref[field], value)


def wind_x(keep, wind, p_low, p_high):
    return jnp.where(keep, wind, wind - GRAD * (p_high - p_low))


def in_groups(rows):
    rows = list(rows)
    return [rows[first : first + GROUP] for first in range(0, len(rows), GROUP)]


def side_by_side(rows):
    return rows[0] if len(rows) == 1 else jnp.concatenate(rows, axis=1)


def apart(x, count):
    return [x[:, WIDE * n : WIDE * (n + 1)] for n in range(count)]


def column_steps(table, rows):
    levels = table.shape[0] // 2
    winds, right_sides = [], []
    for keep, pressure, u_low, u_high, wind, lift, stiffness in rows:
        wind = jnp.where(keep, wind, wind - GRAD * (next_col(pressure) - prev_col(pressure)))
        change = (u_high - u_low) + (next_col(wind) - prev_col(wind)) + (level_up(lift) - level_down(lift))
        winds.append(wind)
        right_sides.append(pressure - DIV * change)
    both = split_dot(table, side_by_side(right_sides))
    firsts, arounds = apart(both[:levels], len(rows)), apart(both[levels:], len(rows))
    leftovers = [
        (right_side - first) - row[6] * first + around
        for row, right_side, first, around in zip(rows, right_sides, firsts, arounds)
    ]
    seconds = apart(split_dot(table[:levels], side_by_side(leftovers)), len(rows))
    results = []
    for (keep, pressure, _, _, _, lift, _), wind, first, second in zip(rows, winds, firsts, seconds):
        p_next = jnp.where(keep, pressure, first + second)
        w_next = jnp.where(keep, lift, lift - LIFT * (level_up(p_next) - p_next))
        results.append((wind, w_next, p_next))
    return results


def own_kernel(
    counts, off_ref, own_ref, own_s_ref, rim_ref, low1, low2, high1, high2, table_ref,
    u_out, v_out, w_out, p_out, up_ref, down_ref,
    p_win, s_win,
):
    levels = own_ref.shape[2]
    at = Place(counts, off_ref, levels)
    low, high = at.neighbours((low1, high1), (low2, high2), (None, None))
    deep = NEAR[PR]
    for row in range(-deep, ROWS + deep):
        p_win[row + deep] = at.field_row(own_ref, low, high, rim_ref, PR, row)
    for near in range(KEEP):
        s_win[KEEP - 1 - near] = received(low, low[1], "s", near)
        s_win[KEEP + ROWS + near] = received(high, high[1], "s", near)
    for row in range(ROWS):
        s_win[KEEP + row] = own_s_ref[row]
    for row in range(-1, ROWS + 1):
        wind = at.field_row(own_ref, low, high, rim_ref, U, row)
        u_out[row + 1] = wind_x(at.keep(row), wind, p_win[row + deep - 1], p_win[row + deep + 1])
    move_y = lax.rem(RATIO * at.off_y + WIDE, WIDE)
    table = table_ref[...]

    for rows in in_groups(range(ROWS)):
        results = column_steps(
            table,
            [
                (
                    at.keep(row), p_win[row + deep], u_out[row], u_out[row + 2],
                    own_ref[V, row], own_ref[W, row],
                    pltpu.roll(s_win[row + KEEP - RATIO * at.off_x], move_y, 1),
                )
                for row in rows
            ],
        )
        for row, result in zip(rows, results):
            v_out[row], w_out[row], p_out[row] = result
    starts = by_pair(is_odd(at.gx), 1, 3)
    for out, first in zip((up_ref, down_ref), starts):
        beyond = None
        for n in range(2):
            value = p_out[first + n]
            for tile in range(COLS // LANES):
                out[n * (COLS // LANES) + tile] = value[:, LANES * tile : LANES * (tile + 1)]
            ext = value[:, COLS:]
            beyond = ext if n == 0 else merge_ext(beyond, ext)
        out[2 * (COLS // LANES)] = beyond


def merge_ext(first, second):
    lane = lanes_of(first.shape)
    near = jnp.where(lane < LANES // 2, turn(second, SIDE), turn(second, -SIDE))
    return jnp.where((lane < SIDE) | (lane >= LANES - SIDE), first, near)


def split_ext(merged, n):
    if n == 0:
        return merged
    lane = lanes_of(merged.shape)
    return jnp.where(lane < LANES // 2, turn(merged, -SIDE), turn(merged, SIDE))


def halo_kernel(
    counts, off_ref, own_ref, own_s_ref, rim_ref, low1, low2, low3, high1, high2, high3, table_ref,
    u_own, v_own, w_own, p_own,
    u_rim, v_rim, w_rim, p_rim, s_rim, u_out, v_out, w_out, p_out,
    p_win, s_win, s_mid,
):
    levels = own_ref.shape[2]
    at = Place(counts, off_ref, levels)
    low, high = at.neighbours((low1, high1), (low2, high2), (low3, high3))
    table = table_ref[...]
    deep = KEEP
    for n in range(deep + 1):
        p_win[n] = at.field_row(own_ref, low, high, rim_ref, PR, n - deep)
        p_win[deep + 1 + n] = at.field_row(own_ref, low, high, rim_ref, PR, ROWS - 1 + n)
    for near in range(ROWS):
        s_win[ROWS - 1 - near] = received(low, low[1], "s", near)
        s_win[2 * ROWS + near] = received(high, high[1], "s", near)
        s_win[ROWS + near] = own_s_ref[near]
    move_y = lax.rem(RATIO * at.off_y + WIDE, WIDE)

    def stiffness(row):
        return pltpu.roll(s_win[row + ROWS - RATIO * at.off_x], move_y, 1)

    def p_before(row):
        return p_win[row + deep] if row <= 0 else p_win[row - ROWS + 1 + deep + 1]

    def rim_of(depth, row):
        return row + depth if row < 0 else row - ROWS + depth

    for row in (-4, -3, -2, 7, 8, 9):
        near = -1 - row if row < 0 else row - ROWS
        near_ref, outer = (low[1], at.gx == 0) if row < 0 else (high[1], at.gx == at.last_x)
        outward, inward = (sent_beside(near_ref, PR, near + by) for by in (1, -1))
        p_low, p_high = (outward, inward) if row < 0 else (inward, outward)
        main = received(low if row < 0 else high, near_ref, U, near)
        ext = wind_x(at.keep(row)[:, COLS:], main[:, COLS:], p_low, p_high)
        value = jnp.concatenate([main[:, :COLS], ext], axis=1)
        u_rim[rim_of(4, row)] = jnp.where(outer, rim_ref[U], value)

    def u_after(row):
        return u_own[row + 1] if -1 <= row <= ROWS else u_rim[rim_of(4, row)]

    for n, row in enumerate((-3, -2, 7, 8)):
        s_rim[n] = stiffness(row)
    for row in range(-1, ROWS + 1):
        s_mid[row + 1] = stiffness(row)
    for rows in in_groups((-3, -2, -1, 6, 7, 8)):
        results = column_steps(
            table,
            [
                (
                    at.keep(row), p_before(row), u_after(row - 1), u_after(row + 1),
                    at.field_row(own_ref, low, high, rim_ref, V, row),
                    at.field_row(own_ref, low, high, rim_ref, W, row),
                    s_rim[(-3, -2, 7, 8).index(row)] if row in (-3, -2, 7, 8) else s_mid[row + 1],
                )
                for row in rows
            ],
        )
        for row, result in zip(rows, results):
            n = rim_of(KEEP, row)
            v_rim[n], w_rim[n], p_rim[n] = result

    def pick(own, rim, row):
        return own[row] if 0 <= row < ROWS else rim[rim_of(KEEP, row)]

    for row in range(-2, ROWS + 2):
        u_out[row + 2] = wind_x(
            at.keep(row), u_after(row), pick(p_own, p_rim, row - 1), pick(p_own, p_rim, row + 1)
        )
    for rows in in_groups(range(-1, ROWS + 1)):
        results = column_steps(
            table,
            [
                (
                    at.keep(row), pick(p_own, p_rim, row), u_out[row + 1], u_out[row + 3],
                    pick(v_own, v_rim, row), pick(w_own, w_rim, row), s_mid[row + 1],
                )
                for row in rows
            ],
        )
        for row, result in zip(rows, results):
            v_out[row + 1], w_out[row + 1], p_out[row + 1] = result


def last_kernel(
    counts, off_ref, u_rim, v_rim, w_rim, p_rim, s_rim, u_mid, v_mid, w_mid, p_mid,
    low_ref, high_ref, table_ref, parent_ref,
    new_hbm, back_hbm,
    u_win, v_win, w_win, q_win, new_win, back_win, sems,
):
    levels = u_rim.shape[1]
    at = Place(counts, off_ref, levels)
    table = table_ref[...]
    tiles = COLS // LANES

    def sent(ref, n):
        parts = [ref[n * tiles + tile] for tile in range(tiles)] + [split_ext(ref[2 * tiles], n)]
        return jnp.concatenate(parts, axis=1)

    low_ref, high_ref = low_high(is_odd(at.gx), low_ref, high_ref)
    for row in range(ROWS + 4):
        u_win[row + 2] = u_mid[row]
    for row in range(ROWS + 2):
        v_win[row + 2] = v_mid[row]
        w_win[row + 2] = w_mid[row]
        q_win[row + 2] = p_mid[row]
    windows = ((U, u_win, 4), (V, v_win, KEEP), (W, w_win, KEEP), (PR, q_win, KEEP))
    send_out(True, at, windows, new_win, new_hbm, sems)
    low_p = [sent(low_ref, 0), sent(low_ref, 1), p_rim[0], p_rim[1]]
    high_p = [p_rim[4], p_rim[5], sent(high_ref, 0), sent(high_ref, 1)]
    for n, row in enumerate((-4, -3)):
        u_win[n] = wind_x(at.keep(row), u_rim[n], low_p[n], low_p[n + 2])
    for n, row in enumerate((8, 9)):
        u_win[12 + n] = wind_x(at.keep(row), u_rim[6 + n], high_p[n], high_p[n + 2])
    for rows in in_groups(enumerate((-3, -2, 7, 8))):
        rims = [(0, 1, 4, 5)[n] for n, _ in rows]
        results = column_steps(
            table,
            [
                (
                    at.keep(row), p_rim[rim], u_win[row + 3], u_win[row + 5],
                    v_rim[rim], w_rim[rim], s_rim[n],
                )
                for (n, row), rim in zip(rows, rims)
            ],
        )
        for (_, row), result in zip(rows, results):
            v_win[row + KEEP], w_win[row + KEEP], q_win[row + KEEP] = result
    send_out(False, at, windows, new_win, new_hbm, sems)
    feed_back(at, windows, parent_ref, back_win, back_hbm, sems)
    for ready in (True, False):
        send_out(ready, at, windows, new_win, new_hbm, sems, wait=True)


def send_out(ready, at, windows, new_win, new_hbm, sems, wait=False):
    move_y = lax.rem(WIDE - RATIO * at.off_y, WIDE)
    for step in (-1, 0, 1):
        kept = [row for row in range(ROWS) if (-1 <= row + RATIO * step <= ROWS) == ready]
        if not kept:
            continue

        @pl.when(at.off_x == step)
        def _(step=step, kept=kept):
            for field, window, deep in windows:
                if not wait:
                    for row in kept:
                        moved = pltpu.roll(window[row + deep + RATIO * step], move_y, 1)
                        new_win[field, row] = moved[:, :COLS]
                part = pl.ds(kept[0], len(kept))
                copy = pltpu.make_async_copy(
                    new_win.at[field, part], new_hbm.at[field, part], sems.at[field + (0 if ready else 4)]
                )
                if wait:
                    copy.wait()
                else:
                    copy.start()


def feed_back(at, windows, parent_ref, back_win, back_hbm, sems):
    levels = parent_ref.shape[2]
    cells_x, cells_y = at.nx // RATIO, at.ny // RATIO
    coarse_rows, coarse_cols = ROWS // RATIO, COLS // RATIO

    def inside(index, count):
        return (index >= 1) & (index <= count - 2)

    source = column_of_lane(lax.broadcasted_iota(jnp.int32, (WIDE, coarse_cols), 0))
    apart = source - RATIO * lax.broadcasted_iota(jnp.int32, (WIDE, coarse_cols), 1)
    spread = jnp.where(
        (apart >= 0) & (apart < RATIO),
        0.5,
        jnp.where((apart >= -RATIO) & (apart < 2 * RATIO), 0.25, 0.0),
    ).astype(BF16)
    cell = lanes_of((levels, coarse_cols)) + (at.gy * coarse_cols - at.off_y)
    weight_y = (
        0.25 * inside(cell - 1, cells_y).astype(F32)
        + 0.5 * inside(cell, cells_y).astype(F32)
        + 0.25 * inside(cell + 1, cells_y).astype(F32)
    )
    centre_y = inside(cell, cells_y).astype(jnp.int32)
    smooth = []
    for coarse in range(coarse_rows):
        a = at.gx * coarse_rows + coarse - at.off_x
        inner = [inside(a + d, cells_x).astype(F32) for d in (-1, 0, 1)]
        weights = [s * m for s, m in zip((0.25, 0.5, 0.25), inner)]
        weight_x = weights[0] + weights[1] + weights[2]
        centre = (centre_y * inside(a, cells_x).astype(jnp.int32)) > 0
        scale = jnp.where(centre, 1.0 / jnp.where(centre, 9.0 * weight_x * weight_y, 1.0), 0.0)
        smooth.append((inner, weights, centre, scale))
    copies = []
    for field, window, deep in windows:
        for coarse, (inner, weights, centre, scale) in enumerate(smooth):
            start = deep - KEEP + RATIO * coarse
            total = None
            for d in range(3):
                part = window[start + 3 * d] + window[start + 3 * d + 1] + window[start + 3 * d + 2]
                part = jnp.where(inner[d] > 0, part * weights[d], 0.0)
                total = part if total is None else total + part
            total = jnp.where(at.held > 0, 0.0, total)
            high = total.astype(BF16)
            low = (total - high.astype(F32)).astype(BF16)
            summed = jnp.dot(high, spread, preferred_element_type=F32) + jnp.dot(
                low, spread, preferred_element_type=F32
            )
            back_win[field, :, coarse, :] = jnp.where(centre, summed * scale, parent_ref[field, coarse])
        copies.append(pltpu.make_async_copy(back_win.at[field], back_hbm.at[field], sems.at[8 + field]))
        copies[-1].start()
    for copy in copies:
        copy.wait()


def call(body, ins, outs, scratch=(), spaces=None, out_spaces=None):
    def space(x):
        if x.dtype == jnp.int32:
            return pltpu.SMEM
        return pltpu.VMEM

    spaces = spaces or [space(x) for x in ins]
    return pl.pallas_call(
        body,
        out_shape=[jax.ShapeDtypeStruct(shape, F32) for shape in outs],
        in_specs=[pl.BlockSpec(memory_space=s) for s in spaces],
        out_specs=[pl.BlockSpec(memory_space=s) for s in out_spaces or [pltpu.VMEM] * len(outs)],
        scratch_shapes=[s if not isinstance(s, tuple) else pltpu.VMEM(s, F32) for s in scratch],
        compiler_params=pltpu.CompilerParams(vmem_limit_bytes=VMEM_BYTES),
    )(*ins)


def exchange(first, second, axis):
    def swap(x, start):
        pairs = [(i, i + 1) for i in range(start, lax.axis_size(axis) - 1, 2)]
        return lax.ppermute(x, axis, pairs + [(high, low) for low, high in pairs])

    return swap(first, 1), swap(second, 0)


def per_device(nest_state, stiffness, parent, inverse_table, offsets):
    levels = nest_state.shape[1]
    nx = nest_state.shape[2] * lax.axis_size("gx")
    ny = nest_state.shape[3] * lax.axis_size("gy")
    counts = (nx, ny)
    nest = jnp.transpose(nest_state, (0, 2, 1, 3))
    stiff_in = jnp.transpose(stiffness, (1, 0, 2))

    nothing = jnp.zeros_like(inverse_table[:1])
    shifted = jnp.concatenate([inverse_table[1:], nothing], 0)
    shifted += jnp.concatenate([nothing, inverse_table[:-1]], 0)
    stack = jnp.concatenate([inverse_table, 0.25 * shifted], 0)
    top = lax.reduce_precision(stack, 8, 7)
    table = jnp.concatenate([top, top, stack - top], 1).astype(BF16)

    def rows(count, width=WIDE):
        return (count, levels, width)

    first, near, far = (len(rows_of(chunk)) for chunk in (CHUNK_1, CHUNK_2, CHUNK_3))
    cur, stiff, coarse, to_left, to_right, edge, up, down = call(
        functools.partial(prepare_kernel, counts),
        [pltpu.with_memory_space_constraint(x, pltpu.HBM) for x in (offsets, nest, stiff_in, parent)],
        [nest.shape, stiff_in.shape, (4, ROWS // RATIO, levels, LANES), (levels, PACK), (levels, PACK)]
        + [(4, levels, COLS), rows(first, COLS), rows(first, COLS)],
        [nest.shape, parent.shape, pltpu.SemaphoreType.DMA((6,))],
        [pltpu.SMEM, pltpu.HBM, pltpu.HBM, pltpu.HBM],
    )
    low1, high1 = exchange(up, down, "gx")
    from_left, from_right = exchange(to_left, to_right, "gy")
    mine, up, down = call(
        functools.partial(near_kernel, lax.axis_size("gy") - 1),
        (cur, stiff, coarse, from_left, from_right),
        [(2, levels, PACK), rows(near + 1, COLS), rows(near + 1, COLS)],
    )
    low2, high2 = exchange(up, down, "gx")
    up, down, own, own_s, rim = call(
        functools.partial(far_kernel, counts),
        (offsets, cur, stiff, edge, mine, low1, high1),
        [rows(far, COLS), rows(far, COLS), (4, ROWS, levels, WIDE), rows(ROWS), rows(4)],
    )
    low3, high3 = exchange(up, down, "gx")
    message = (2 * (COLS // LANES) + 1, levels, LANES)
    u1, v1, w1, p1, up, down = call(
        functools.partial(own_kernel, counts),
        (offsets, own, own_s, rim, low1, low2, high1, high2, table),
        [rows(ROWS + 2), rows(ROWS), rows(ROWS), rows(ROWS), message, message],
        [rows(ROWS + 4), rows(2 * ROWS)],
    )
    low4, high4 = exchange(up, down, "gx")
    outer = call(
        functools.partial(halo_kernel, counts),
        (offsets, own, own_s, rim, low1, low2, low3, high1, high2, high3, table, u1, v1, w1, p1),
        [rows(8), rows(6), rows(6), rows(6), rows(4), rows(ROWS + 4), rows(ROWS + 2), rows(ROWS + 2), rows(ROWS + 2)],
        [rows(8), rows(3 * ROWS), rows(ROWS + 2)],
    )
    new, back = call(
        functools.partial(last_kernel, counts),
        (offsets, *outer, low4, high4, table, coarse),
        [nest.shape, parent.shape],
        [rows(ROWS + 8), rows(ROWS + 6), rows(ROWS + 6), rows(ROWS + 6)]
        + [nest.shape, parent.shape, pltpu.SemaphoreType.DMA((12,))],
        out_spaces=[pl.ANY, pl.ANY],
    )
    return jnp.transpose(new, (0, 2, 1, 3)), back


def solution(mesh):
    return jax.shard_map(
        per_device,
        mesh=mesh,
        in_specs=(
            P(None, None, "gx", "gy"),
            P(None, "gx", "gy"),
            P(None, None, "gx", "gy"),
            P(),
            P(),
        ),
        out_specs=(P(None, None, "gx", "gy"), P(None, None, "gx", "gy")),
        check_vma=False,
    )
```

```python
import functools

import jax
import jax.numpy as jnp
from jax import lax
from jax.experimental import pallas as pl
from jax.experimental.pallas import tpu as pltpu
from jax.sharding import PartitionSpec as P

RATIO = 3
GRAD = 0.25
DIV = 0.25
LIFT = 0.5
F32 = jnp.float32
BF16 = jnp.bfloat16
VMEM_BYTES = 24 * 1024 * 1024

ROWS = 6
COLS = 384
LANES = 128
WIDE = COLS + LANES
SIDE = 8
SLOTS = LANES // SIDE
U, V, W, PR = 0, 1, 2, 3
GROUP = 2
NEAR = {PR: 2}
KEEP = 3
S_GROUP = 4 * ROWS
EDGE_GROUP = S_GROUP + ROWS
GROUPS = EDGE_GROUP + 4
PACK = -(-GROUPS // SLOTS) * LANES
CHUNK_1 = ((V, 0, 3), (W, 0, 3), ("s", 0, 3))
CHUNK_2 = ((PR, 0, 2), (U, 0, 1), ("s", 3, 1))
CHUNK_3 = ((PR, 2, 1), (U, 1, 3), ("s", 4, 2))
SENT = [(PR, n) for n in range(5)] + [(U, n) for n in range(4)] + [(V, n) for n in range(3)]
SENT += [(W, n) for n in range(3)] + [("s", n) for n in range(6)]


def rows_of(chunk):
    return [(what, first + n) for what, first, count in chunk for n in range(count)]


def lanes_of(shape):
    return lax.broadcasted_iota(jnp.int32, shape, len(shape) - 1)


def column_of_lane(lane):
    return jnp.where(lane < COLS + LANES // 2, lane, lane - WIDE)


def is_edge(index, count):
    return (index < RATIO) | (index >= count - RATIO)


def expand_all(coarse):
    lane = lanes_of(coarse.shape)
    parts = [
        jnp.take_along_axis(coarse, (lane + first) // RATIO, axis=1) for first in range(0, COLS, LANES)
    ]
    return jnp.concatenate(parts, axis=1)


def turn(x, amount):
    amount = amount % x.shape[1]
    return x if amount == 0 else pltpu.roll(x, amount, 1)


def next_col(x):
    return pltpu.roll(x, x.shape[1] - 1, 1)


def prev_col(x):
    return pltpu.roll(x, 1, 1)


SUB = 8


def level_up(x):
    levels = x.shape[0]
    turned = pltpu.roll(x, levels - 1, 0)
    last = turned[levels - SUB :]
    level = lax.broadcasted_iota(jnp.int32, last.shape, 0)
    return jnp.concatenate([turned[: levels - SUB], jnp.where(level < SUB - 1, last, 0.0)], axis=0)


def level_down(x):
    turned = pltpu.roll(x, 1, 0)
    first = turned[:SUB]
    level = lax.broadcasted_iota(jnp.int32, first.shape, 0)
    return jnp.concatenate([jnp.where(level > 0, first, 0.0), turned[SUB:]], axis=0)


def split_dot(table, x):
    high = x.astype(BF16)
    low = (x - high.astype(F32)).astype(BF16)
    stacked = jnp.concatenate([high, low, high], axis=0)
    return jnp.dot(table, stacked, preferred_element_type=F32)


def own_row(near, side):
    return ROWS - 1 - near if side == 0 else near


def is_odd(index):
    return lax.rem(index, 2) == 1


def by_pair(odd, up, down):
    return jnp.where(odd, up, down), jnp.where(odd, down, up)


class Received:
    def __init__(self, in_first, first, second):
        self.in_first, self.first, self.second = in_first, first, second

    def __getitem__(self, at):
        return jnp.where(self.in_first, self.first[at], self.second[at])


def low_high(odd, first, second):
    if first is None:
        return None, None
    return Received(jnp.logical_not(odd), first, second), Received(odd, first, second)


def prepare_kernel(
    counts, off_ref, nest_ref, stiff_hbm, parent_hbm,
    cur_ref, stiff_ref, parent_ref, left_ref, right_ref, edge_ref, up_ref, down_ref,
    nest_win, parent_win, sems,
):
    nx, ny = counts
    copies = [pltpu.make_async_copy(parent_hbm, parent_win, sems.at[4])]
    copies += [pltpu.make_async_copy(nest_ref.at[f], nest_win.at[f], sems.at[f]) for f in (V, W, PR, U)]
    copies.append(pltpu.make_async_copy(stiff_hbm, stiff_ref, sems.at[5]))
    for copy in copies:
        copy.start()
    gx, gy = lax.axis_index("gx"), lax.axis_index("gy")
    off_x, off_y = off_ref[0], off_ref[1]
    levels = nest_win.shape[2]
    col = lanes_of((levels, COLS)) + (gy * COLS - RATIO * off_y)
    edge_col = is_edge(col, ny)
    place = lanes_of((levels, LANES)) // SIDE

    def pack(packs, row, group):
        tile, slot = group // SLOTS, group % SLOTS
        sides = (
            turn(row[:, :LANES], SIDE * slot),
            turn(row[:, COLS - LANES :], SIDE * (slot + 1) - LANES),
        )
        for side, value in enumerate(sides):
            held = packs[tile][side]
            packs[tile][side] = value if held is None else jnp.where(place == slot, value, held)

    def fill(on_rim):
        packs = [[None, None] for _ in range(PACK // LANES)]
        if on_rim:
            copies[0].wait()
        for at, field in enumerate((V, W, PR, U)):
            if on_rim:
                bounds = [expand_all(parent_win[field, :, coarse, :]) for coarse in range(ROWS // RATIO)]
            copies[1 + at].wait()
            for row in range(ROWS):
                value = nest_win[field, row]
                if on_rim:
                    i = gx * ROWS + row - RATIO * off_x
                    held = is_edge(i, nx).astype(jnp.int32)
                    value = jnp.where(edge_col | (held > 0), bounds[row // RATIO], value)
                cur_ref[field, row] = value
                pack(packs, value, field * ROWS + row)
            rim = jnp.where(gx == 0, bounds[0], bounds[-1]) if on_rim else jnp.zeros((levels, COLS), F32)
            edge_ref[field] = rim
            if on_rim:
                pack(packs, rim, EDGE_GROUP + field)
        copies[5].wait()
        for row in range(ROWS):
            pack(packs, stiff_ref[row], S_GROUP + row)
        for tile, (left, right) in enumerate(packs):
            at = slice(LANES * tile, LANES * (tile + 1))
            if left is None:
                left = right = jnp.zeros((levels, LANES), F32)
            left_ref[:, at], right_ref[:, at] = by_pair(is_odd(gy), right, left)
        if not on_rim:
            copies[0].wait()
        for field in range(4):
            for coarse in range(ROWS // RATIO):
                parent_ref[field, coarse] = parent_win[field, :, coarse, :]

    rim_x = (gx == 0) | (gx == nx // ROWS - 1)
    rim_y = (gy == 0) | (gy == ny // COLS - 1)
    pl.when(rim_x | rim_y)(lambda: fill(True))
    pl.when(jnp.logical_not(rim_x | rim_y))(lambda: fill(False))
    fill_message(CHUNK_1, cur_ref, stiff_ref, up_ref, down_ref)


def fill_message(chunk, cur_ref, stiff_ref, first_ref, second_ref):
    odd = is_odd(lax.axis_index("gx"))
    for at, (what, near) in enumerate(rows_of(chunk)):
        rows = by_pair(odd, own_row(near, 0), own_row(near, 1))
        for row, out in zip(rows, (first_ref, second_ref)):
            out[at] = stiff_ref[row] if what == "s" else cur_ref[what, row]


def group_of(what, row):
    return S_GROUP + row if what == "s" else what * ROWS + row


def near_kernel(last_y, cur_ref, stiff_ref, parent_ref, left_ref, right_ref, mine_ref, up_ref, down_ref):
    gx, gy = lax.axis_index("gx"), lax.axis_index("gy")
    levels = left_ref.shape[0]
    lane = lanes_of((levels, LANES))
    place = lane // SIDE
    from_left, from_right = low_high(is_odd(gy), left_ref, right_ref)
    mine_ref[0] = from_left[...]
    mine_ref[1] = from_right[...]

    def fill(side, cell):
        for tile in range(PACK // LANES):
            at = slice(LANES * tile, LANES * (tile + 1))
            out = mine_ref[side, :, at]
            for slot in range(SLOTS):
                group = tile * SLOTS + slot
                if group < S_GROUP:
                    value = parent_ref[group // ROWS, (group % ROWS) // RATIO, :, cell : cell + 1]
                elif EDGE_GROUP <= group < GROUPS:
                    field = group - EDGE_GROUP
                    value = jnp.where(
                        gx == 0,
                        parent_ref[field, 0, :, cell : cell + 1],
                        parent_ref[field, ROWS // RATIO - 1, :, cell : cell + 1],
                    )
                else:
                    continue
                out = jnp.where(place == slot, value, out)
            mine_ref[side, :, at] = out

    @pl.when(gy == 0)
    def _():
        fill(0, 0)

    @pl.when(gy == last_y)
    def _():
        fill(1, COLS // RATIO - 1)

    rows = rows_of(CHUNK_2)
    fill_message(CHUNK_2, cur_ref, stiff_ref, up_ref, down_ref)
    tight = []
    for side in range(2):
        tiles = [None] * (COLS // LANES)
        for hand in range(2):
            for at, (what, near) in enumerate(SENT):
                group = group_of(what, own_row(near, side))
                tile, slot = group // SLOTS, group % SLOTS
                target = hand * len(SENT) + at
                to_tile, to_slot = target // SLOTS, target % SLOTS
                value = turn(mine_ref[hand, :, LANES * tile : LANES * (tile + 1)], SIDE * (to_slot - slot))
                held = tiles[to_tile]
                tiles[to_tile] = value if held is None else jnp.where(place == to_slot, value, held)
        tight.append(jnp.concatenate(tiles, axis=1))
    up_ref[len(rows)], down_ref[len(rows)] = by_pair(is_odd(gx), *tight)


def beside(left, left_slot, right, right_slot):
    lane = lanes_of(left.shape)
    return jnp.where(
        lane < LANES // 2, turn(right, -SIDE * right_slot), turn(left, LANES - SIDE * (left_slot + 1))
    )


def mine_beside(mine_ref, group):
    tile, slot = group // SLOTS, group % SLOTS
    at = slice(LANES * tile, LANES * (tile + 1))
    return beside(mine_ref[0, :, at], slot, mine_ref[1, :, at], slot)


def sent_beside(near_ref, what, near):
    row = len(rows_of(CHUNK_2))
    index = SENT.index((what, near))
    tiles = []
    for target in (index, len(SENT) + index):
        tile = target // SLOTS
        tiles += [near_ref[row, :, LANES * tile : LANES * (tile + 1)], target % SLOTS]
    return beside(*tiles)


def far_kernel(
    counts, off_ref, cur_ref, stiff_ref, edge_ref, mine_ref, low1, high1, up_ref, down_ref, own_ref, own_s_ref, rim_ref
):
    del low1, high1
    at = Place(counts, off_ref, stiff_ref.shape[1])
    fill_message(CHUNK_3, cur_ref, stiff_ref, up_ref, down_ref)
    for n, (what, near) in enumerate(rows_of(CHUNK_3)):
        if what == U:
            rows = by_pair(is_odd(at.gx), own_row(near, 0), own_row(near, 1))
            for row, out in zip(rows, (up_ref, down_ref)):
                keep = at.keep(row)[:, :COLS]
                out[n] = wind_x(keep, cur_ref[U, row], cur_ref[PR, row - 1], cur_ref[PR, row + 1])
    for field in range(4):
        for row in range(ROWS):
            own_ref[field, row, :, :COLS] = cur_ref[field, row]
            own_ref[field, row, :, COLS:] = mine_beside(mine_ref, field * ROWS + row)
        rim_ref[field, :, :COLS] = edge_ref[field]
        rim_ref[field, :, COLS:] = mine_beside(mine_ref, EDGE_GROUP + field)
    for row in range(ROWS):
        own_s_ref[row, :, :COLS] = stiff_ref[row]
        own_s_ref[row, :, COLS:] = mine_beside(mine_ref, S_GROUP + row)


def received(refs, near_ref, what, near):
    for chunk, ref in zip((CHUNK_1, CHUNK_2, CHUNK_3), refs):
        rows = rows_of(chunk)
        if (what, near) in rows:
            main = ref[rows.index((what, near))]
    return jnp.concatenate([main, sent_beside(near_ref, what, near)], axis=1)


class Place:
    def __init__(self, counts, off_ref, levels):
        self.nx, self.ny = counts
        self.gx, self.gy = lax.axis_index("gx"), lax.axis_index("gy")
        self.last_x = self.nx // ROWS - 1
        self.off_x, self.off_y = off_ref[0], off_ref[1]
        j = column_of_lane(lanes_of((SUB, WIDE))) + (self.gy * COLS - RATIO * self.off_y)
        self.copies = levels // SUB
        self.held_once = is_edge(j, self.ny).astype(jnp.int32)
        self.held = self.over_levels(self.held_once)

    def neighbours(self, *swaps):
        return zip(*[low_high(is_odd(self.gx), first, second) for first, second in swaps])

    def keep(self, row):
        i = self.gx * ROWS + row - RATIO * self.off_x
        return self.over_levels(self.held_once + is_edge(i, self.nx).astype(jnp.int32)) > 0

    def over_levels(self, tile):
        return jnp.concatenate([tile] * self.copies, axis=0)

    def field_row(self, own, low, high, rim_ref, field, row):
        if 0 <= row < ROWS:
            return own[field, row]
        if row < 0:
            value = received(low, low[1], field, -1 - row)
            outer = self.gx == 0
        else:
            value = received(high, high[1], field, row - ROWS)
            outer = self.gx == self.last_x
        return jnp.where(outer, rim_ref[field], value)


def wind_x(keep, wind, p_low, p_high):
    return jnp.where(keep, wind, wind - GRAD * (p_high - p_low))


def in_groups(rows):
    rows = list(rows)
    return [rows[first : first + GROUP] for first in range(0, len(rows), GROUP)]


def side_by_side(rows):
    return rows[0] if len(rows) == 1 else jnp.concatenate(rows, axis=1)


def apart(x, count):
    return [x[:, WIDE * n : WIDE * (n + 1)] for n in range(count)]


def column_steps(table, rows):
    levels = table.shape[0] // 2
    winds, right_sides = [], []
    for keep, pressure, u_low, u_high, wind, lift, stiffness in rows:
        wind = jnp.where(keep, wind, wind - GRAD * (next_col(pressure) - prev_col(pressure)))
        change = (u_high - u_low) + (next_col(wind) - prev_col(wind)) + (level_up(lift) - level_down(lift))
        winds.append(wind)
        right_sides.append(pressure - DIV * change)
    both = split_dot(table, side_by_side(right_sides))
    firsts, arounds = apart(both[:levels], len(rows)), apart(both[levels:], len(rows))
    leftovers = [
        (right_side - first) - row[6] * first + around
        for row, right_side, first, around in zip(rows, right_sides, firsts, arounds)
    ]
    seconds = apart(split_dot(table[:levels], side_by_side(leftovers)), len(rows))
    results = []
    for (keep, pressure, _, _, _, lift, _), wind, first, second in zip(rows, winds, firsts, seconds):
        p_next = jnp.where(keep, pressure, first + second)
        w_next = jnp.where(keep, lift, lift - LIFT * (level_up(p_next) - p_next))
        results.append((wind, w_next, p_next))
    return results


def own_kernel(
    counts, off_ref, own_ref, own_s_ref, rim_ref, low1, low2, high1, high2, table_ref,
    u_out, v_out, w_out, p_out, up_ref, down_ref,
    p_win, s_win,
):
    levels = own_ref.shape[2]
    at = Place(counts, off_ref, levels)
    low, high = at.neighbours((low1, high1), (low2, high2), (None, None))
    deep = NEAR[PR]
    for row in range(-deep, ROWS + deep):
        p_win[row + deep] = at.field_row(own_ref, low, high, rim_ref, PR, row)
    for near in range(KEEP):
        s_win[KEEP - 1 - near] = received(low, low[1], "s", near)
        s_win[KEEP + ROWS + near] = received(high, high[1], "s", near)
    for row in range(ROWS):
        s_win[KEEP + row] = own_s_ref[row]
    for row in range(-1, ROWS + 1):
        wind = at.field_row(own_ref, low, high, rim_ref, U, row)
        u_out[row + 1] = wind_x(at.keep(row), wind, p_win[row + deep - 1], p_win[row + deep + 1])
    move_y = lax.rem(RATIO * at.off_y + WIDE, WIDE)
    table = table_ref[...]

    for rows in in_groups(range(ROWS)):
        results = column_steps(
            table,
            [
                (
                    at.keep(row), p_win[row + deep], u_out[row], u_out[row + 2],
                    own_ref[V, row], own_ref[W, row],
                    pltpu.roll(s_win[row + KEEP - RATIO * at.off_x], move_y, 1),
                )
                for row in rows
            ],
        )
        for row, result in zip(rows, results):
            v_out[row], w_out[row], p_out[row] = result
    starts = by_pair(is_odd(at.gx), 1, 3)
    for out, first in zip((up_ref, down_ref), starts):
        beyond = None
        for n in range(2):
            value = p_out[first + n]
            for tile in range(COLS // LANES):
                out[n * (COLS // LANES) + tile] = value[:, LANES * tile : LANES * (tile + 1)]
            ext = value[:, COLS:]
            beyond = ext if n == 0 else merge_ext(beyond, ext)
        out[2 * (COLS // LANES)] = beyond


def merge_ext(first, second):
    lane = lanes_of(first.shape)
    near = jnp.where(lane < LANES // 2, turn(second, SIDE), turn(second, -SIDE))
    return jnp.where((lane < SIDE) | (lane >= LANES - SIDE), first, near)


def split_ext(merged, n):
    if n == 0:
        return merged
    lane = lanes_of(merged.shape)
    return jnp.where(lane < LANES // 2, turn(merged, -SIDE), turn(merged, SIDE))


def halo_kernel(
    counts, off_ref, own_ref, own_s_ref, rim_ref, low1, low2, low3, high1, high2, high3, table_ref,
    u_own, v_own, w_own, p_own,
    u_rim, v_rim, w_rim, p_rim, s_rim, u_out, v_out, w_out, p_out,
    p_win, s_win, s_mid,
):
    levels = own_ref.shape[2]
    at = Place(counts, off_ref, levels)
    low, high = at.neighbours((low1, high1), (low2, high2), (low3, high3))
    table = table_ref[...]
    deep = KEEP
    for n in range(deep + 1):
        p_win[n] = at.field_row(own_ref, low, high, rim_ref, PR, n - deep)
        p_win[deep + 1 + n] = at.field_row(own_ref, low, high, rim_ref, PR, ROWS - 1 + n)
    for near in range(ROWS):
        s_win[ROWS - 1 - near] = received(low, low[1], "s", near)
        s_win[2 * ROWS + near] = received(high, high[1], "s", near)
        s_win[ROWS + near] = own_s_ref[near]
    move_y = lax.rem(RATIO * at.off_y + WIDE, WIDE)

    def stiffness(row):
        return pltpu.roll(s_win[row + ROWS - RATIO * at.off_x], move_y, 1)

    def p_before(row):
        return p_win[row + deep] if row <= 0 else p_win[row - ROWS + 1 + deep + 1]

    def rim_of(depth, row):
        return row + depth if row < 0 else row - ROWS + depth

    for row in (-4, -3, -2, 7, 8, 9):
        near = -1 - row if row < 0 else row - ROWS
        near_ref, outer = (low[1], at.gx == 0) if row < 0 else (high[1], at.gx == at.last_x)
        outward, inward = (sent_beside(near_ref, PR, near + by) for by in (1, -1))
        p_low, p_high = (outward, inward) if row < 0 else (inward, outward)
        main = received(low if row < 0 else high, near_ref, U, near)
        ext = wind_x(at.keep(row)[:, COLS:], main[:, COLS:], p_low, p_high)
        value = jnp.concatenate([main[:, :COLS], ext], axis=1)
        u_rim[rim_of(4, row)] = jnp.where(outer, rim_ref[U], value)

    def u_after(row):
        return u_own[row + 1] if -1 <= row <= ROWS else u_rim[rim_of(4, row)]

    for n, row in enumerate((-3, -2, 7, 8)):
        s_rim[n] = stiffness(row)
    for row in range(-1, ROWS + 1):
        s_mid[row + 1] = stiffness(row)
    for rows in in_groups((-3, -2, -1, 6, 7, 8)):
        results = column_steps(
            table,
            [
                (
                    at.keep(row), p_before(row), u_after(row - 1), u_after(row + 1),
                    at.field_row(own_ref, low, high, rim_ref, V, row),
                    at.field_row(own_ref, low, high, rim_ref, W, row),
                    s_rim[(-3, -2, 7, 8).index(row)] if row in (-3, -2, 7, 8) else s_mid[row + 1],
                )
                for row in rows
            ],
        )
        for row, result in zip(rows, results):
            n = rim_of(KEEP, row)
            v_rim[n], w_rim[n], p_rim[n] = result

    def pick(own, rim, row):
        return own[row] if 0 <= row < ROWS else rim[rim_of(KEEP, row)]

    for row in range(-2, ROWS + 2):
        u_out[row + 2] = wind_x(
            at.keep(row), u_after(row), pick(p_own, p_rim, row - 1), pick(p_own, p_rim, row + 1)
        )
    for rows in in_groups(range(-1, ROWS + 1)):
        results = column_steps(
            table,
            [
                (
                    at.keep(row), pick(p_own, p_rim, row), u_out[row + 1], u_out[row + 3],
                    pick(v_own, v_rim, row), pick(w_own, w_rim, row), s_mid[row + 1],
                )
                for row in rows
            ],
        )
        for row, result in zip(rows, results):
            v_out[row + 1], w_out[row + 1], p_out[row + 1] = result


def last_kernel(
    counts, off_ref, u_rim, v_rim, w_rim, p_rim, s_rim, u_mid, v_mid, w_mid, p_mid,
    low_ref, high_ref, table_ref, parent_ref,
    new_hbm, back_hbm,
    u_win, v_win, w_win, q_win, new_win, back_win, sems,
):
    levels = u_rim.shape[1]
    at = Place(counts, off_ref, levels)
    table = table_ref[...]
    tiles = COLS // LANES

    def sent(ref, n):
        parts = [ref[n * tiles + tile] for tile in range(tiles)] + [split_ext(ref[2 * tiles], n)]
        return jnp.concatenate(parts, axis=1)

    low_ref, high_ref = low_high(is_odd(at.gx), low_ref, high_ref)
    for row in range(ROWS + 4):
        u_win[row + 2] = u_mid[row]
    for row in range(ROWS + 2):
        v_win[row + 2] = v_mid[row]
        w_win[row + 2] = w_mid[row]
        q_win[row + 2] = p_mid[row]
    windows = ((U, u_win, 4), (V, v_win, KEEP), (W, w_win, KEEP), (PR, q_win, KEEP))
    send_out(True, at, windows, new_win, new_hbm, sems)
    low_p = [sent(low_ref, 0), sent(low_ref, 1), p_rim[0], p_rim[1]]
    high_p = [p_rim[4], p_rim[5], sent(high_ref, 0), sent(high_ref, 1)]
    for n, row in enumerate((-4, -3)):
        u_win[n] = wind_x(at.keep(row), u_rim[n], low_p[n], low_p[n + 2])
    for n, row in enumerate((8, 9)):
        u_win[12 + n] = wind_x(at.keep(row), u_rim[6 + n], high_p[n], high_p[n + 2])
    for rows in in_groups(enumerate((-3, -2, 7, 8))):
        rims = [(0, 1, 4, 5)[n] for n, _ in rows]
        results = column_steps(
            table,
            [
                (
                    at.keep(row), p_rim[rim], u_win[row + 3], u_win[row + 5],
                    v_rim[rim], w_rim[rim], s_rim[n],
                )
                for (n, row), rim in zip(rows, rims)
            ],
        )
        for (_, row), result in zip(rows, results):
            v_win[row + KEEP], w_win[row + KEEP], q_win[row + KEEP] = result
    send_out(False, at, windows, new_win, new_hbm, sems)
    feed_back(at, windows, parent_ref, back_win, back_hbm, sems)
    for ready in (True, False):
        send_out(ready, at, windows, new_win, new_hbm, sems, wait=True)


def send_out(ready, at, windows, new_win, new_hbm, sems, wait=False):
    move_y = lax.rem(WIDE - RATIO * at.off_y, WIDE)
    for step in (-1, 0, 1):
        kept = [row for row in range(ROWS) if (-1 <= row + RATIO * step <= ROWS) == ready]
        if not kept:
            continue

        @pl.when(at.off_x == step)
        def _(step=step, kept=kept):
            for field, window, deep in windows:
                if not wait:
                    @pl.when(at.off_y == 0)
                    def _(field=field, window=window, deep=deep):
                        for row in kept:
                            new_win[field, row] = window[row + deep + RATIO * step, :, :COLS]

                    @pl.when(at.off_y != 0)
                    def _(field=field, window=window, deep=deep):
                        for row in kept:
                            moved = pltpu.roll(window[row + deep + RATIO * step], move_y, 1)
                            new_win[field, row] = moved[:, :COLS]

                part = pl.ds(kept[0], len(kept))
                copy = pltpu.make_async_copy(
                    new_win.at[field, part], new_hbm.at[field, part], sems.at[field + (0 if ready else 4)]
                )
                if wait:
                    copy.wait()
                else:
                    copy.start()


def feed_back(at, windows, parent_ref, back_win, back_hbm, sems):
    levels = parent_ref.shape[2]
    cells_x, cells_y = at.nx // RATIO, at.ny // RATIO
    coarse_rows, coarse_cols = ROWS // RATIO, COLS // RATIO

    def inside(index, count):
        return (index >= 1) & (index <= count - 2)

    source = column_of_lane(lax.broadcasted_iota(jnp.int32, (WIDE, coarse_cols), 0))
    apart = source - RATIO * lax.broadcasted_iota(jnp.int32, (WIDE, coarse_cols), 1)
    spread = jnp.where(
        (apart >= 0) & (apart < RATIO),
        0.5,
        jnp.where((apart >= -RATIO) & (apart < 2 * RATIO), 0.25, 0.0),
    ).astype(BF16)
    cell = lanes_of((levels, coarse_cols)) + (at.gy * coarse_cols - at.off_y)
    weight_y = (
        0.25 * inside(cell - 1, cells_y).astype(F32)
        + 0.5 * inside(cell, cells_y).astype(F32)
        + 0.25 * inside(cell + 1, cells_y).astype(F32)
    )
    centre_y = inside(cell, cells_y).astype(jnp.int32)
    smooth = []
    for coarse in range(coarse_rows):
        a = at.gx * coarse_rows + coarse - at.off_x
        inner = [inside(a + d, cells_x).astype(F32) for d in (-1, 0, 1)]
        weights = [s * m for s, m in zip((0.25, 0.5, 0.25), inner)]
        weight_x = weights[0] + weights[1] + weights[2]
        centre = (centre_y * inside(a, cells_x).astype(jnp.int32)) > 0
        scale = jnp.where(centre, 1.0 / jnp.where(centre, 9.0 * weight_x * weight_y, 1.0), 0.0)
        smooth.append((inner, weights, centre, scale))
    copies = []
    for field, window, deep in windows:
        for coarse, (inner, weights, centre, scale) in enumerate(smooth):
            start = deep - KEEP + RATIO * coarse
            total = None
            for d in range(3):
                part = window[start + 3 * d] + window[start + 3 * d + 1] + window[start + 3 * d + 2]
                part = jnp.where(inner[d] > 0, part * weights[d], 0.0)
                total = part if total is None else total + part
            total = jnp.where(at.held > 0, 0.0, total)
            high = total.astype(BF16)
            low = (total - high.astype(F32)).astype(BF16)
            summed = jnp.dot(high, spread, preferred_element_type=F32) + jnp.dot(
                low, spread, preferred_element_type=F32
            )
            back_win[field, :, coarse, :] = jnp.where(centre, summed * scale, parent_ref[field, coarse])
        copies.append(pltpu.make_async_copy(back_win.at[field], back_hbm.at[field], sems.at[8 + field]))
        copies[-1].start()
    for copy in copies:
        copy.wait()


def call(body, ins, outs, scratch=(), spaces=None, out_spaces=None):
    def space(x):
        if x.dtype == jnp.int32:
            return pltpu.SMEM
        return pltpu.VMEM

    spaces = spaces or [space(x) for x in ins]
    return pl.pallas_call(
        body,
        out_shape=[jax.ShapeDtypeStruct(shape, F32) for shape in outs],
        in_specs=[pl.BlockSpec(memory_space=s) for s in spaces],
        out_specs=[pl.BlockSpec(memory_space=s) for s in out_spaces or [pltpu.VMEM] * len(outs)],
        scratch_shapes=[s if not isinstance(s, tuple) else pltpu.VMEM(s, F32) for s in scratch],
        compiler_params=pltpu.CompilerParams(vmem_limit_bytes=VMEM_BYTES),
    )(*ins)


def exchange(first, second, axis):
    def swap(x, start):
        pairs = [(i, i + 1) for i in range(start, lax.axis_size(axis) - 1, 2)]
        return lax.ppermute(x, axis, pairs + [(high, low) for low, high in pairs])

    return swap(first, 1), swap(second, 0)


def per_device(nest_state, stiffness, parent, inverse_table, offsets):
    levels = nest_state.shape[1]
    nx = nest_state.shape[2] * lax.axis_size("gx")
    ny = nest_state.shape[3] * lax.axis_size("gy")
    counts = (nx, ny)
    nest = jnp.transpose(nest_state, (0, 2, 1, 3))
    stiff_in = jnp.transpose(stiffness, (1, 0, 2))

    nothing = jnp.zeros_like(inverse_table[:1])
    shifted = jnp.concatenate([inverse_table[1:], nothing], 0)
    shifted += jnp.concatenate([nothing, inverse_table[:-1]], 0)
    stack = jnp.concatenate([inverse_table, 0.25 * shifted], 0)
    top = lax.reduce_precision(stack, 8, 7)
    table = jnp.concatenate([top, top, stack - top], 1).astype(BF16)

    def rows(count, width=WIDE):
        return (count, levels, width)

    first, near, far = (len(rows_of(chunk)) for chunk in (CHUNK_1, CHUNK_2, CHUNK_3))
    cur, stiff, coarse, to_left, to_right, edge, up, down = call(
        functools.partial(prepare_kernel, counts),
        [pltpu.with_memory_space_constraint(x, pltpu.HBM) for x in (offsets, nest, stiff_in, parent)],
        [nest.shape, stiff_in.shape, (4, ROWS // RATIO, levels, LANES), (levels, PACK), (levels, PACK)]
        + [(4, levels, COLS), rows(first, COLS), rows(first, COLS)],
        [nest.shape, parent.shape, pltpu.SemaphoreType.DMA((6,))],
        [pltpu.SMEM, pltpu.HBM, pltpu.HBM, pltpu.HBM],
    )
    low1, high1 = exchange(up, down, "gx")
    from_left, from_right = exchange(to_left, to_right, "gy")
    mine, up, down = call(
        functools.partial(near_kernel, lax.axis_size("gy") - 1),
        (cur, stiff, coarse, from_left, from_right),
        [(2, levels, PACK), rows(near + 1, COLS), rows(near + 1, COLS)],
    )
    low2, high2 = exchange(up, down, "gx")
    up, down, own, own_s, rim = call(
        functools.partial(far_kernel, counts),
        (offsets, cur, stiff, edge, mine, low1, high1),
        [rows(far, COLS), rows(far, COLS), (4, ROWS, levels, WIDE), rows(ROWS), rows(4)],
    )
    low3, high3 = exchange(up, down, "gx")
    message = (2 * (COLS // LANES) + 1, levels, LANES)
    u1, v1, w1, p1, up, down = call(
        functools.partial(own_kernel, counts),
        (offsets, own, own_s, rim, low1, low2, high1, high2, table),
        [rows(ROWS + 2), rows(ROWS), rows(ROWS), rows(ROWS), message, message],
        [rows(ROWS + 4), rows(2 * ROWS)],
    )
    low4, high4 = exchange(up, down, "gx")
    outer = call(
        functools.partial(halo_kernel, counts),
        (offsets, own, own_s, rim, low1, low2, low3, high1, high2, high3, table, u1, v1, w1, p1),
        [rows(8), rows(6), rows(6), rows(6), rows(4), rows(ROWS + 4), rows(ROWS + 2), rows(ROWS + 2), rows(ROWS + 2)],
        [rows(8), rows(3 * ROWS), rows(ROWS + 2)],
    )
    new, back = call(
        functools.partial(last_kernel, counts),
        (offsets, *outer, low4, high4, table, coarse),
        [nest.shape, parent.shape],
        [rows(ROWS + 8), rows(ROWS + 6), rows(ROWS + 6), rows(ROWS + 6)]
        + [nest.shape, parent.shape, pltpu.SemaphoreType.DMA((12,))],
        out_spaces=[pl.ANY, pl.ANY],
    )
    return jnp.transpose(new, (0, 2, 1, 3)), back


def solution(mesh):
    return jax.shard_map(
        per_device,
        mesh=mesh,
        in_specs=(
            P(None, None, "gx", "gy"),
            P(None, "gx", "gy"),
            P(None, None, "gx", "gy"),
            P(),
            P(),
        ),
        out_specs=(P(None, None, "gx", "gy"), P(None, None, "gx", "gy")),
        check_vma=False,
    )
```
